128 devices in a mesh: gx: 8 (over x, core), gy: 16 (over y, z).
Axes of the slice: x: 4, y: 4, z: 4, core: 2. Of those that a mesh axis runs over, the one named last changes fastest.
Arguments:
- state: float32 [16, 512, 2048], P(None, 'gx', 'gy'), may hold values from -5.5 to 5.5
- kappa_x: float32 [16, 512, 2048], P(None, 'gx', 'gy'), may hold values from 300 to 30000
- kappa_y: float32 [16, 512, 2048], P(None, 'gx', 'gy'), may hold values from 300 to 30000
Outputs:
- updated: float32 [16, 512, 2048], P(None, 'gx', 'gy')
The draws below stay inside these ranges and needn't reach their ends.
All inputs are finite; a program needn't handle non-finite values.
Results may differ from the reference program's by a relative error of at most 0.025.
Values sent between devices are 32-bit elements; how exact they have to be, the bound alone decides.
No kernel may reach another device: no remote copies, remote signals or barrier semaphores. Data moves between devices by JAX's collectives and lax.ppermute only.
A program may use at most 128 MiB of HBM per device.

```python
import math
import jax
import jax.numpy as jnp
from jax import lax

NZ = 16
NX = 512
NY = 2048


def wave_field(key, base, single, paired):
    keys = jax.random.split(key, 2)
    phase_x = jax.random.uniform(keys[0], (NZ, 1, 1), jnp.float32, 0.0, 2.0 * math.pi)
    phase_y = jax.random.uniform(keys[1], (NZ, 1, 1), jnp.float32, 0.0, 2.0 * math.pi)
    place_x = jnp.arange(NX, dtype=jnp.float32)[None, :, None] / NX
    place_y = jnp.arange(NY, dtype=jnp.float32)[None, None, :] / NY
    wave_x = jnp.cos(2.0 * math.pi * place_x + phase_x)
    wave_y = jnp.cos(2.0 * math.pi * place_y + phase_y)
    return base + single * (wave_x + wave_y) + paired * wave_x * wave_y


def kappa_field(key, base, single, paired):
    keys = jax.random.split(key, 2)
    smooth = wave_field(keys[0], base, single, paired)
    rough = jax.random.uniform(keys[1], (NZ, NX, NY), jnp.float32, -0.15, 0.15)
    return 300.0 * jnp.power(10.0, 0.15 + 1.7 * smooth + rough)


def draw_kappa_x(key, part):
    key = jax.random.fold_in(key, 11)
    return kappa_field(key, 0.5, 0.25, 0.0)


def draw_kappa_y(key, part):
    key = jax.random.fold_in(key, 17)
    return kappa_field(key, 0.5, 0.25, 0.0)


def draw_state(key, part):
    key = jax.random.fold_in(key, 23)
    keys = jax.random.split(key, 2)
    rough = jnp.clip(jax.random.normal(keys[0], (NZ, NX, NY), jnp.float32), -5.0, 5.0)
    return rough + wave_field(keys[1], 0.0, 0.0, 0.5)


def setup_inputs(seed: int = 0) -> dict:
    arg_keys = jax.random.split(jax.random.key(seed), 4)
    return {
        "state": draw_state(jax.random.fold_in(arg_keys[3], 71), 0),
        "kappa_x": draw_kappa_x(jax.random.fold_in(arg_keys[3], 71), 0),
        "kappa_y": draw_kappa_y(jax.random.fold_in(arg_keys[3], 71), 0),
    }


def faces(kappa, axis):
    length = kappa.shape[axis]
    widths = [(0, 0)] * kappa.ndim
    widths[axis] = (1, 1)
    padded = jnp.pad(kappa, widths)
    before = lax.slice_in_dim(padded, 0, length, axis=axis)
    centre = lax.slice_in_dim(padded, 1, length + 1, axis=axis)
    after = lax.slice_in_dim(padded, 2, length + 2, axis=axis)
    return (0.5 * (before + centre), 0.5 * (centre + after))

def apply_lap(field, left, right, axis):
    length = field.shape[axis]
    widths = [(0, 0)] * field.ndim
    widths[axis] = (1, 1)
    padded = jnp.pad(field, widths)
    before = lax.slice_in_dim(padded, 0, length, axis=axis)
    after = lax.slice_in_dim(padded, 2, length + 2, axis=axis)
    return right * (after - field) - left * (field - before)

def solve_lines(left, right, source, axis):
    left_last = jnp.moveaxis(left, axis, -1)
    right_last = jnp.moveaxis(right, axis, -1)
    source_last = jnp.moveaxis(source, axis, -1)
    lower = (-left_last).at[..., 0].set(0.0)
    upper = (-right_last).at[..., -1].set(0.0)
    diag = 1.0 + left_last + right_last
    solved = lax.linalg.tridiagonal_solve(lower, diag, upper, source_last[..., None])[..., 0]
    return jnp.moveaxis(solved, -1, axis)

def reference(state, kappa_x, kappa_y):
    left_x, right_x = faces(kappa_x, 1)
    left_y, right_y = faces(kappa_y, 2)
    lap_x = apply_lap(state, left_x, right_x, 1)
    lap_y = apply_lap(state, left_y, right_y, 2)
    source = state + lap_x + 2.0 * lap_y
    middle = solve_lines(left_x, right_x, source, 1)
    return solve_lines(left_y, right_y, middle - lap_y, 2)
```

```python
import jax
import jax.numpy as jnp
from jax import lax
from jax.experimental import pallas as pl
from jax.experimental.pallas import tpu as pltpu
from jax.sharding import PartitionSpec as P

F32 = jnp.float32
NZ, BX, BY = 16, 64, 128
ROWS = NZ * BX
GROUPS = ROWS // 128
LIMIT = 40 * 1024 * 1024


def inverse(x):
    guess = pl.reciprocal(x, approx=True)
    return guess * (2.0 - x * guess)


def load_kernel(st_hbm, kx_hbm, ky_hbm, st, kx, ky, ky_t, up, down, sems):
    moves = [
        pltpu.make_async_copy(src, dst, sems.at[n])
        for n, (src, dst) in enumerate(((ky_hbm, ky), (st_hbm, st), (kx_hbm, kx)))
    ]
    for move in moves:
        move.start()
    moves[0].wait()
    for g in range(GROUPS):
        ky_t[pl.ds(g, BY, stride=GROUPS), :] = ky[pl.ds(g * 128, 128), :].T
    moves[1].wait()
    for g in range(GROUPS):
        turned = st[pl.ds(g * 128, 128), :].T
        down[0, pl.ds(g, 1), :] = turned[0:1, :]
        up[0, pl.ds(g, 1), :] = turned[127:128, :]
    down[1] = ky_t[pl.ds(0, GROUPS), :]
    up[1] = ky_t[pl.ds((BY - 1) * GROUPS, GROUPS), :]
    moves[2].wait()


def matrix_kernel(st, kx, ky, ky_t, fx, ux, wf, wl, fy, uy, yf, yl, mx, my, source):
    def x_row(ref, i):
        return jnp.concatenate(
            [ref[pl.ds(i, 8, stride=BX), :], ref[pl.ds(8 * BX + i, 8, stride=BX), :]], axis=0
        )

    def y_row(ref, i):
        return ref[pl.ds(i * GROUPS, GROUPS), :]

    def chains(count, row, f, u, first, last, m):
        ahead = jnp.ones_like(row(0))
        back = jnp.ones_like(ahead)
        low, high = row(0), row(count - 1)
        m[3] = low
        m[4] = high
        for i in range(count - 1):
            nxt = row(i + 1)
            r = 0.5 * (low + nxt)
            low = nxt
            inv = inverse(r + ahead)
            ratio = r * inv
            ahead = 1.0 + ratio * ahead
            u[i] = inv
            f[i] = ratio
            j = count - 1 - i
            prev = row(j - 1)
            r = 0.5 * (high + prev)
            high = prev
            ratio = r * inverse(r + back)
            back = 1.0 + ratio * back
            first[j] = ratio
            yield
        start = inverse(back)
        end = inverse(ahead)
        m[0] = start
        m[2] = end
        first[0] = start
        last[count - 1] = end
        u[count - 1] = end
        f[count - 1] = jnp.zeros_like(end)
        for i in range(1, count):
            start = start * first[i]
            first[i] = start
            j = count - 1 - i
            end = end * f[j]
            last[j] = end
            yield
        m[1] = end

    running = [
        chains(BX, lambda i: x_row(kx, i), fx, ux, wf, wl, mx),
        chains(BY, lambda i: y_row(ky_t, i), fy, uy, yf, yl, my),
    ]
    while running:
        for chain in list(running):
            if next(chain, 0) == 0:
                running.remove(chain)
    lane = lax.broadcasted_iota(jnp.int32, (128, 128), 1)
    for g in range(GROUPS):
        rows = pl.ds(g * 128, 128)
        s = st[rows, :]
        k = ky[rows, :]
        flux = 0.5 * (k + pltpu.roll(k, 127, 1)) * (pltpu.roll(s, 127, 1) - s)
        flux = jnp.where(lane == 127, 0.0, flux)
        source[rows, :] = s + flux - pltpu.roll(flux, 1, 1)


def x_send_kernel(above, below, up, down, source, wf, wl, mx, s_out, send):
    flux_l = 0.5 * (below[1] + down[1]) * (down[0] - below[0])
    flux_r = 0.5 * (above[1] + up[1]) * (above[0] - up[0])
    both = jnp.concatenate([flux_l, flux_r], axis=0)
    turned = jnp.concatenate([both] * 8, axis=0).T
    lane = lax.broadcasted_iota(jnp.int32, (128, 128), 1)
    for g in range(GROUPS):
        rows = pl.ds(g * 128, 128)
        left = jnp.broadcast_to(turned[:, g : g + 1], (128, 128))
        right = jnp.broadcast_to(turned[:, 8 + g : 9 + g], (128, 128))
        extra = jnp.where(lane == 0, -left, jnp.where(lane == 127, right, 0.0))
        s_out[rows, :] = source[rows, :] + extra
    firsts = [jnp.zeros((NZ, BY), F32) for _ in range(2)]
    lasts = [jnp.zeros((NZ, BY), F32) for _ in range(2)]
    for i in range(BX):
        s = jnp.concatenate(
            [s_out[pl.ds(i, 8, stride=BX), :], s_out[pl.ds(8 * BX + i, 8, stride=BX), :]], axis=0
        )
        firsts[i % 2] = firsts[i % 2] + wf[i] * s
        lasts[i % 2] = lasts[i % 2] + wl[i] * s
    sums = (firsts[0] + firsts[1], lasts[0] + lasts[1])
    for p in range(send.shape[0]):
        send[p, 0:5] = mx[...]
        send[p, 5] = sums[0]
        send[p, 6] = sums[1]


def interface(got, slots, me):
    count = got.shape[0]
    zero = jnp.zeros_like(got[0, 0])
    gammas, rhos = [], []
    gamma, rho = zero, zero
    for i in range(count + 1):
        below = [got[i - 1, n] for n in range(7)] if i else [zero] * 7
        above = [got[i, n] for n in range(7)] if i < count else [zero] * 7
        pivot = 2.0 * inverse(below[4] + above[3]) + below[2] + above[0] - below[1] * gamma
        inv = inverse(pivot)
        rho = (below[6] - above[5] + below[1] * rho) * inv
        gamma = above[1] * inv
        gammas.append(gamma)
        rhos.append(rho)
    flow = rhos[count]
    slots[count] = flow
    for i in range(count - 1, -1, -1):
        flow = rhos[i] + gammas[i] * flow
        slots[i] = flow
    return slots[me], slots[me + 1]


def x_solve_kernel(got, s_in, st, fx, ux, wf, wl, yf, yl, my, v_t, send, slots, work, v):
    me = lax.axis_index("gx")
    q_l, q_r = interface(got, slots, me)

    def x_row(ref, i):
        return jnp.concatenate(
            [ref[pl.ds(i, 8, stride=BX), :], ref[pl.ds(8 * BX + i, 8, stride=BX), :]], axis=0
        )

    total = x_row(s_in, 0) + q_l
    work[0] = total
    for i in range(1, BX):
        total = x_row(s_in, i) + fx[i - 1] * total
        work[i] = total
    total = total - q_r
    x = jnp.zeros_like(total)
    for i in range(BX - 1, -1, -1):
        x = ux[i] * (total if i == BX - 1 else work[i]) + fx[i] * x
        d = x - x_row(st, i)
        v[pl.ds(i, 8, stride=BX), :] = d[:8]
        v[pl.ds(8 * BX + i, 8, stride=BX), :] = d[8:]
    for g in range(GROUPS):
        v_t[pl.ds(g, BY, stride=GROUPS), :] = v[pl.ds(g * 128, 128), :].T
    firsts = [jnp.zeros((GROUPS, 128), F32) for _ in range(4)]
    lasts = [jnp.zeros((GROUPS, 128), F32) for _ in range(4)]
    for j in range(BY):
        row = v_t[pl.ds(j * GROUPS, GROUPS), :]
        firsts[j % 4] = firsts[j % 4] + yf[j] * row
        lasts[j % 4] = lasts[j % 4] + yl[j] * row
    sums = (
        (firsts[0] + firsts[1]) + (firsts[2] + firsts[3]),
        (lasts[0] + lasts[1]) + (lasts[2] + lasts[3]),
    )
    for p in range(send.shape[0]):
        send[p, 0:5] = my[...]
        send[p, 5] = sums[0]
        send[p, 6] = sums[1]


def y_solve_kernel(got, v_t, st, fy, uy, out_hbm, slots, work, out, sems):
    me = lax.axis_index("gy")
    p_l, p_r = interface(got, slots, me)

    def y_row(ref, j):
        return ref[pl.ds(j * GROUPS, GROUPS), :]

    total = y_row(v_t, 0) + p_l
    work[pl.ds(0, GROUPS), :] = total
    for j in range(1, BY):
        total = y_row(v_t, j) + fy[j - 1] * total
        work[pl.ds(j * GROUPS, GROUPS), :] = total
    total = total - p_r
    x = jnp.zeros_like(total)
    for j in range(BY - 1, -1, -1):
        x = uy[j] * (total if j == BY - 1 else y_row(work, j)) + fy[j] * x
        work[pl.ds(j * GROUPS, GROUPS), :] = x
    moves = []
    for g in range(GROUPS):
        rows = pl.ds(g * 128, 128)
        out[rows, :] = st[rows, :] + 2.0 * work[pl.ds(g, BY, stride=GROUPS), :].T
        move = pltpu.make_async_copy(out.at[rows], out_hbm.at[rows], sems.at[g])
        move.start()
        moves.append(move)
    for move in moves:
        move.wait()


def call(kernel, outs, args, scratch=(), flops=0):
    vm = pl.BlockSpec(memory_space=pltpu.VMEM)
    anywhere = pl.BlockSpec(memory_space=pl.ANY)
    return pl.pallas_call(
        kernel,
        out_shape=[
            jax.ShapeDtypeStruct(shape, F32) if hbm else pltpu.VMEM(shape, F32)
            for shape, hbm in outs
        ],
        in_specs=[anywhere if hbm else vm for _, hbm in args],
        out_specs=[anywhere if hbm else vm for _, hbm in outs],
        scratch_shapes=list(scratch),
        compiler_params=pltpu.CompilerParams(vmem_limit_bytes=LIMIT),
        cost_estimate=pl.CostEstimate(flops=flops, bytes_accessed=flops, transcendentals=0),
    )(*[value for value, _ in args])


def inside(*shape):
    return (shape, False)


def on_device(state, kappa_x, kappa_y):
    flat = [a.reshape(ROWS, BY) for a in (state, kappa_x, kappa_y)]
    plane = inside(ROWS, BY)
    edge = inside(2, GROUPS, 128)
    st, kx, ky, ky_t, up, down = call(
        load_kernel,
        [plane, plane, plane, plane, edge, edge],
        [(a, True) for a in flat],
        [pltpu.SemaphoreType.DMA((3,))],
    )
    count = lax.axis_size("gy")
    below = lax.ppermute(up, "gy", [(i, i + 1) for i in range(count - 1)])
    above = lax.ppermute(down, "gy", [(i + 1, i) for i in range(count - 1)])
    xs = inside(BX, NZ, BY)
    ys = inside(BY, GROUPS, 128)
    fx, ux, wf, wl, fy, uy, yf, yl, mx, my, source = call(
        matrix_kernel,
        [xs] * 4 + [ys] * 4 + [inside(5, NZ, BY), inside(5, GROUPS, 128), plane],
        [(a, False) for a in (st, kx, ky, ky_t)],
        flops=10_000_000,
    )
    s, send = call(
        x_send_kernel,
        [plane, inside(lax.axis_size("gx"), 7, NZ, BY)],
        [(a, False) for a in (above, below, up, down, source, wf, wl, mx)],
    )
    got = lax.all_to_all(send, "gx", 0, 0)
    v_t, send = call(
        x_solve_kernel,
        [plane, inside(count, 7, GROUPS, 128)],
        [(a, False) for a in (got, s, st, fx, ux, wf, wl, yf, yl, my)],
        [
            pltpu.VMEM((lax.axis_size("gx") + 1, NZ, BY), F32),
            pltpu.VMEM((BX, NZ, BY), F32),
            pltpu.VMEM((ROWS, BY), F32),
        ],
    )
    got = lax.all_to_all(send, "gy", 0, 0)
    (out,) = call(
        y_solve_kernel,
        [((ROWS, BY), True)],
        [(a, False) for a in (got, v_t, st, fy, uy)],
        [
            pltpu.VMEM((count + 1, GROUPS, 128), F32),
            pltpu.VMEM((ROWS, BY), F32),
            pltpu.VMEM((ROWS, BY), F32),
            pltpu.SemaphoreType.DMA((GROUPS,)),
        ],
    )
    return out.reshape(state.shape)


def solution(mesh):
    spec = P(None, "gx", "gy")
    return jax.shard_map(
        on_device, mesh=mesh, in_specs=(spec, spec, spec), out_specs=spec, check_vma=False
    )
```

```python
import jax
import jax.numpy as jnp
from jax import lax
from jax.experimental import pallas as pl
from jax.experimental.pallas import tpu as pltpu
from jax.sharding import PartitionSpec as P

F32 = jnp.float32
NZ, BX, BY = 16, 64, 128
ROWS = NZ * BX
GROUPS = ROWS // 128
LIMIT = 40 * 1024 * 1024
SIDE = 4


def inverse(x):
    guess = pl.reciprocal(x, approx=True)
    return guess * (2.0 - x * guess)


def x_row(ref, i):
    return jnp.concatenate(
        [ref[pl.ds(i, 8, stride=BX), :], ref[pl.ds(8 * BX + i, 8, stride=BX), :]], axis=0
    )


def y_row(ref, j):
    return ref[pl.ds(j * GROUPS, GROUPS), :]


def read(ref):
    return [ref[n] for n in range(7)]


def merge(low, high):
    inv = inverse(2.0 * inverse(low[4] + high[3]) + low[2] + high[0])
    e = (low[6] - high[5]) * inv
    a = low[1] * inv
    b = high[1] * inv
    joined = [
        low[0] - low[1] * a,
        low[1] * b,
        high[2] - high[1] * b,
        low[3],
        high[4],
        low[5] - low[1] * e,
        high[6] + high[1] * e,
    ]
    return joined, (e, a, b)


def chain_ends(blocks):
    zero = jnp.zeros_like(blocks[0][0])
    gammas, rhos = [], []
    gamma, rho = zero, zero
    count = len(blocks)
    for i in range(count + 1):
        below = blocks[i - 1] if i else [zero] * 7
        above = blocks[i] if i < count else [zero] * 7
        inv = inverse(2.0 * inverse(below[4] + above[3]) + below[2] + above[0] - below[1] * gamma)
        rho = (below[6] - above[5] + below[1] * rho) * inv
        gamma = above[1] * inv
        gammas.append(gamma)
        rhos.append(rho)
    flows = [rhos[count]]
    for i in range(count - 1, -1, -1):
        flows.append(rhos[i] + gammas[i] * flows[-1])
    return flows[::-1]


def arrange(own, others, place, slots):
    slots[place] = own[...]
    for k, other in enumerate(others):
        slots[lax.rem(place + SIDE - 1 - k, SIDE)] = other[...]
    return [[slots[c, n] for n in range(7)] for c in range(SIDE)]


def load_kernel(st_hbm, kx_hbm, ky_hbm, st, kx, ky, ky_t, up, down, sems):
    moves = [
        pltpu.make_async_copy(src, dst, sems.at[n])
        for n, (src, dst) in enumerate(((ky_hbm, ky), (st_hbm, st), (kx_hbm, kx)))
    ]
    for move in moves:
        move.start()
    moves[0].wait()
    for g in range(GROUPS):
        ky_t[pl.ds(g, BY, stride=GROUPS), :] = ky[pl.ds(g * 128, 128), :].T
    moves[1].wait()
    for g in range(GROUPS):
        turned = st[pl.ds(g * 128, 128), :].T
        down[0, pl.ds(g, 1), :] = turned[0:1, :]
        up[0, pl.ds(g, 1), :] = turned[127:128, :]
    down[1] = ky_t[pl.ds(0, GROUPS), :]
    up[1] = ky_t[pl.ds((BY - 1) * GROUPS, GROUPS), :]
    moves[2].wait()


def sweep(count, row, f, u, first, last, m):
    ahead = jnp.ones_like(row(0))
    back = jnp.ones_like(ahead)
    low, high = row(0), row(count - 1)
    m[3] = low
    m[4] = high
    for i in range(count - 1):
        nxt = row(i + 1)
        r = 0.5 * (low + nxt)
        low = nxt
        inv = inverse(r + ahead)
        ratio = r * inv
        ahead = 1.0 + ratio * ahead
        u[i] = inv
        f[i] = ratio
        j = count - 1 - i
        prev = row(j - 1)
        r = 0.5 * (high + prev)
        high = prev
        ratio = r * inverse(r + back)
        back = 1.0 + ratio * back
        first[j] = ratio
    start = inverse(back)
    end = inverse(ahead)
    m[0] = start
    m[2] = end
    first[0] = start
    last[count - 1] = end
    u[count - 1] = end
    f[count - 1] = jnp.zeros_like(end)
    for i in range(1, count):
        start = start * first[i]
        first[i] = start
        j = count - 1 - i
        end = end * f[j]
        last[j] = end
    m[1] = end


def x_matrix_kernel(st, kx, ky, fx, ux, wf, wl, mx, source):
    sweep(BX, lambda i: x_row(kx, i), fx, ux, wf, wl, mx)
    lane = lax.broadcasted_iota(jnp.int32, (128, 128), 1)
    for g in range(GROUPS):
        rows = pl.ds(g * 128, 128)
        s = st[rows, :]
        k = ky[rows, :]
        flux = 0.5 * (k + pltpu.roll(k, 127, 1)) * (pltpu.roll(s, 127, 1) - s)
        flux = jnp.where(lane == 127, 0.0, flux)
        source[rows, :] = s + flux - pltpu.roll(flux, 1, 1)


def y_matrix_kernel(ky_t, after, fy, uy, yf, yl, my):
    sweep(BY, lambda j: y_row(ky_t, j), fy, uy, yf, yl, my)


def x_ends_kernel(above, below, up, down, source, wf, wl, mx, s_out, send):
    flux_l = 0.5 * (below[1] + down[1]) * (down[0] - below[0])
    flux_r = 0.5 * (above[1] + up[1]) * (above[0] - up[0])
    both = jnp.concatenate([flux_l, flux_r], axis=0)
    turned = jnp.concatenate([both] * 8, axis=0).T
    lane = lax.broadcasted_iota(jnp.int32, (128, 128), 1)
    for g in range(GROUPS):
        rows = pl.ds(g * 128, 128)
        left = jnp.broadcast_to(turned[:, g : g + 1], (128, 128))
        right = jnp.broadcast_to(turned[:, 8 + g : 9 + g], (128, 128))
        extra = jnp.where(lane == 0, -left, jnp.where(lane == 127, right, 0.0))
        s_out[rows, :] = source[rows, :] + extra
    firsts = [jnp.zeros((NZ, BY), F32) for _ in range(2)]
    lasts = [jnp.zeros((NZ, BY), F32) for _ in range(2)]
    for i in range(BX):
        s = x_row(s_out, i)
        firsts[i % 2] = firsts[i % 2] + wf[i] * s
        lasts[i % 2] = lasts[i % 2] + wl[i] * s
    send[0:5] = mx[...]
    send[5] = firsts[0] + firsts[1]
    send[6] = lasts[0] + lasts[1]


def x_local_kernel(s_in, st, fx, ux, d):
    total = x_row(s_in, 0)
    d[0] = total
    for i in range(1, BX):
        total = x_row(s_in, i) + fx[i - 1] * total
        d[i] = total
    x = jnp.zeros_like(total)
    for i in range(BX - 1, -1, -1):
        x = ux[i] * d[i] + fx[i] * x
        d[i] = x - x_row(st, i)


def x_merge_kernel(own, other, send, coefs):
    core = lax.rem(lax.axis_index("gx"), 2)
    mine, theirs = read(own), read(other)
    low = [jnp.where(core == 0, a, b) for a, b in zip(mine, theirs)]
    high = [jnp.where(core == 0, b, a) for a, b in zip(mine, theirs)]
    joined, flow = merge(low, high)
    for n in range(7):
        send[n] = joined[n]
    for n in range(3):
        coefs[n] = flow[n]


def x_flow_kernel(own, other1, other2, other3, coefs, after, for_low, for_high, slots, ends):
    place = lax.div(lax.axis_index("gx"), 2)
    blocks = arrange(own, (other1, other2, other3), place, slots)
    for n, flow in enumerate(chain_ends(blocks)):
        ends[n] = flow
    enter, leave = ends[place], ends[place + 1]
    middle = coefs[0] + coefs[1] * enter + coefs[2] * leave
    for_low[0] = enter
    for_low[1] = middle
    for_high[0] = middle
    for_high[1] = leave


def y_ends_kernel(came, held, d, wf, wl, yf, yl, my, v_t, send, v):
    core = lax.rem(lax.axis_index("gx"), 2)
    enter = jnp.where(core == 0, came[0], held[0])
    leave = jnp.where(core == 0, came[1], held[1])
    for i in range(BX):
        part = d[i] + wf[i] * enter - wl[i] * leave
        v[pl.ds(i, 8, stride=BX), :] = part[:8]
        v[pl.ds(8 * BX + i, 8, stride=BX), :] = part[8:]
    for g in range(GROUPS):
        v_t[pl.ds(g, BY, stride=GROUPS), :] = v[pl.ds(g * 128, 128), :].T
    firsts = [jnp.zeros((GROUPS, 128), F32) for _ in range(4)]
    lasts = [jnp.zeros((GROUPS, 128), F32) for _ in range(4)]
    for j in range(BY):
        row = y_row(v_t, j)
        firsts[j % 4] = firsts[j % 4] + yf[j] * row
        lasts[j % 4] = lasts[j % 4] + yl[j] * row
    send[0:5] = my[...]
    send[5] = (firsts[0] + firsts[1]) + (firsts[2] + firsts[3])
    send[6] = (lasts[0] + lasts[1]) + (lasts[2] + lasts[3])


def y_pack_kernel(own, other, send):
    send[:, 0:GROUPS] = own[...]
    send[:, GROUPS : 2 * GROUPS] = other[...]


def y_local_kernel(v_t, fy, uy, after, g_t):
    total = y_row(v_t, 0)
    g_t[0] = total
    for j in range(1, BY):
        total = y_row(v_t, j) + fy[j - 1] * total
        g_t[j] = total
    x = jnp.zeros_like(total)
    for j in range(BY - 1, -1, -1):
        x = uy[j] * g_t[j] + fy[j] * x
        g_t[j] = x


def y_merge_kernel(own, other1, other2, other3, after, send, coefs, slots):
    place = lax.rem(lax.axis_index("gy"), SIDE)
    blocks = arrange(own, (other1, other2, other3), place, slots)
    joined = blocks[0]
    for c in range(1, SIDE):
        joined, flow = merge(joined, blocks[c])
        for n in range(3):
            coefs[c - 1, n] = flow[n]
    for n in range(7):
        send[n] = joined[n]


def y_flow_kernel(own, other1, other2, other3, coefs, for_low, for_high, slots, ends, inner):
    place = lax.div(lax.axis_index("gy"), SIDE)
    blocks = arrange(own, (other1, other2, other3), place, slots)
    for n, flow in enumerate(chain_ends(blocks)):
        ends[n] = flow
    enter, leave = ends[place], ends[place + 1]
    inner[0] = enter
    inner[SIDE] = leave
    flow = leave
    for c in range(SIDE - 1, 0, -1):
        flow = coefs[c - 1, 0] + coefs[c - 1, 1] * enter + coefs[c - 1, 2] * flow
        inner[c] = flow
    depth = lax.rem(lax.axis_index("gy"), SIDE)
    enter, leave = inner[depth], inner[depth + 1]
    for_high[0] = enter[:GROUPS]
    for_high[1] = leave[:GROUPS]
    for_low[0] = enter[GROUPS:]
    for_low[1] = leave[GROUPS:]


def y_solve_kernel(came, held, g_t, yf, yl, st, out_hbm, work, out, sems):
    core = lax.rem(lax.axis_index("gx"), 2)
    enter = jnp.where(core == 0, came[0], held[0])
    leave = jnp.where(core == 0, came[1], held[1])
    for j in range(BY):
        work[pl.ds(j * GROUPS, GROUPS), :] = 2.0 * (g_t[j] + yf[j] * enter - yl[j] * leave)
    moves = []
    for g in range(GROUPS):
        rows = pl.ds(g * 128, 128)
        out[rows, :] = st[rows, :] + work[pl.ds(g, BY, stride=GROUPS), :].T
        move = pltpu.make_async_copy(out.at[rows], out_hbm.at[rows], sems.at[g])
        move.start()
        moves.append(move)
    for move in moves:
        move.wait()


def call(kernel, outs, args, scratch=(), cost=100_000):
    vm = pl.BlockSpec(memory_space=pltpu.VMEM)
    hbm = pl.BlockSpec(memory_space=pltpu.HBM)
    return pl.pallas_call(
        kernel,
        out_shape=[
            jax.ShapeDtypeStruct(shape, F32) if far else pltpu.VMEM(shape, F32)
            for shape, far in outs
        ],
        in_specs=[hbm if far else vm for _, far in args],
        out_specs=[hbm if far else vm for _, far in outs],
        scratch_shapes=list(scratch),
        compiler_params=pltpu.CompilerParams(vmem_limit_bytes=LIMIT),
        cost_estimate=pl.CostEstimate(flops=cost, bytes_accessed=cost, transcendentals=0),
    )(*[value for value, _ in args])


def near(*values):
    return [(value, False) for value in values]


def on_device(state, kappa_x, kappa_y):
    flat = [a.reshape(ROWS, BY) for a in (state, kappa_x, kappa_y)]
    plane = (ROWS, BY)
    xs = (BX, NZ, BY)
    ys = (BY, GROUPS, 128)
    x_block = (7, NZ, BY)
    y_block = (7, GROUPS, 128)
    wide = (7, 2 * GROUPS, 128)
    edge = (2, GROUPS, 128)
    nx, ny = lax.axis_size("gx"), lax.axis_size("gy")

    def to_core(value, sources):
        return lax.ppermute(value, "gx", [(i, i ^ 1) for i in range(nx) if i % 2 in sources])

    def to_chips(value, target):
        return [
            lax.ppermute(
                value,
                ("gx", "gy"),
                [(i * ny + j, target(i, j, k)) for i in range(1, nx, 2) for j in range(ny)],
            )
            for k in range(1, SIDE)
        ]

    st, kx, ky, ky_t, up, down = call(
        load_kernel,
        near(plane, plane, plane, plane, edge, edge),
        [(a, True) for a in flat],
        [pltpu.SemaphoreType.DMA((3,))],
    )
    below = lax.ppermute(up, "gy", [(i, i + 1) for i in range(ny - 1)])
    above = lax.ppermute(down, "gy", [(i + 1, i) for i in range(ny - 1)])
    fx, ux, wf, wl, mx, source = call(
        x_matrix_kernel, near(xs, xs, xs, xs, (5, NZ, BY), plane), near(st, kx, ky), cost=5_000_000
    )
    s, ends = call(
        x_ends_kernel,
        near(plane, x_block),
        near(above, below, up, down, source, wf, wl, mx),
    )
    other = to_core(ends, (0, 1))
    (d,) = call(x_local_kernel, near(xs), near(s, st, fx, ux), cost=3_000_000)
    chip, coefs = call(x_merge_kernel, near(x_block, (3, NZ, BY)), near(ends, other))
    others = to_chips(chip, lambda i, j, k: (i + 2 * k) % nx * ny + j)
    fy, uy, yf, yl, my = call(
        y_matrix_kernel, near(ys, ys, ys, ys, (5, GROUPS, 128)), near(ky_t, coefs), cost=5_000_000
    )
    for_low, for_high = call(
        x_flow_kernel,
        near((2, NZ, BY), (2, NZ, BY)),
        near(chip, *others, coefs, my),
        [pltpu.VMEM((SIDE,) + x_block, F32), pltpu.VMEM((SIDE + 1, NZ, BY), F32)],
    )
    came = to_core(for_low, (1,))
    v_t, ends = call(
        y_ends_kernel,
        near(plane, y_block),
        near(came, for_high, d, wf, wl, yf, yl, my),
        [pltpu.VMEM(plane, F32)],
    )
    other = to_core(ends, (0,))
    (pair,) = call(y_pack_kernel, near(wide), near(ends, other))
    others = to_chips(pair, lambda i, j, k: i * ny + j // SIDE * SIDE + (j + k) % SIDE)
    (g_t,) = call(y_local_kernel, near(ys), near(v_t, fy, uy, pair), cost=5_000_000)
    quad, coefs = call(
        y_merge_kernel,
        near(wide, (SIDE - 1, 3, 2 * GROUPS, 128)),
        near(pair, *others, g_t),
        [pltpu.VMEM((SIDE,) + wide, F32)],
    )
    others = to_chips(quad, lambda i, j, k: i * ny + (j + SIDE * k) % ny)
    for_low, for_high = call(
        y_flow_kernel,
        near(edge, edge),
        near(quad, *others, coefs),
        [
            pltpu.VMEM((SIDE,) + wide, F32),
            pltpu.VMEM((SIDE + 1, 2 * GROUPS, 128), F32),
            pltpu.VMEM((SIDE + 1, 2 * GROUPS, 128), F32),
        ],
    )
    came = to_core(for_low, (1,))
    (out,) = call(
        y_solve_kernel,
        [(plane, True)],
        near(came, for_high, g_t, yf, yl, st),
        [
            pltpu.VMEM(plane, F32),
            pltpu.VMEM(plane, F32),
            pltpu.SemaphoreType.DMA((GROUPS,)),
        ],
    )
    return out.reshape(state.shape)


def solution(mesh):
    spec = P(None, "gx", "gy")
    return jax.shard_map(
        on_device, mesh=mesh, in_specs=(spec, spec, spec), out_specs=spec, check_vma=False
    )
```

```python
import jax
import jax.numpy as jnp
from jax import lax
from jax.experimental import pallas as pl
from jax.experimental.pallas import tpu as pltpu
from jax.sharding import PartitionSpec as P

F32 = jnp.float32
NZ, BX, BY = 16, 64, 128
ROWS = NZ * BX
GROUPS = ROWS // 128
LIMIT = 40 * 1024 * 1024


def inverse(x):
    guess = pl.reciprocal(x, approx=True)
    return guess * (2.0 - x * guess)


def x_row(ref, i):
    return jnp.concatenate(
        [ref[pl.ds(i, 8, stride=BX), :], ref[pl.ds(8 * BX + i, 8, stride=BX), :]], axis=0
    )


def y_row(ref, j):
    return ref[pl.ds(j * GROUPS, GROUPS), :]


def place_rows(ref, i, value):
    ref[pl.ds(i, 8, stride=BX), :] = value[:8]
    ref[pl.ds(8 * BX + i, 8, stride=BX), :] = value[8:]


def interface(blocks, ends, slots, me):
    count = blocks.shape[0]
    zero = jnp.zeros_like(ends[0, 0])
    gammas, rhos = [], []
    gamma, rho = zero, zero
    for i in range(count + 1):
        below = [blocks[i - 1, n] for n in range(5)] if i else [zero] * 5
        above = [blocks[i, n] for n in range(5)] if i < count else [zero] * 5
        gain = (ends[i - 1, 1] if i else zero) - (ends[i, 0] if i < count else zero)
        inv = inverse(2.0 * inverse(below[4] + above[3]) + below[2] + above[0] - below[1] * gamma)
        rho = (gain + below[1] * rho) * inv
        gamma = above[1] * inv
        gammas.append(gamma)
        rhos.append(rho)
    flow = rhos[count]
    slots[count] = flow
    for i in range(count - 1, -1, -1):
        flow = rhos[i] + gammas[i] * flow
        slots[i] = flow
    return slots[me], slots[me + 1]


def sweep(count, row, f, u, first, last, m):
    ahead = jnp.ones_like(row(0))
    back = jnp.ones_like(ahead)
    low, high = row(0), row(count - 1)
    m[3] = low
    m[4] = high
    for i in range(count - 1):
        nxt = row(i + 1)
        r = 0.5 * (low + nxt)
        low = nxt
        inv = inverse(r + ahead)
        ratio = r * inv
        ahead = 1.0 + ratio * ahead
        u[i] = inv
        f[i] = ratio
        j = count - 1 - i
        prev = row(j - 1)
        r = 0.5 * (high + prev)
        high = prev
        ratio = r * inverse(r + back)
        back = 1.0 + ratio * back
        first[j] = ratio
    start = inverse(back)
    end = inverse(ahead)
    m[0] = start
    m[2] = end
    first[0] = start
    last[count - 1] = end
    u[count - 1] = end
    f[count - 1] = jnp.zeros_like(end)
    for i in range(1, count):
        start = start * first[i]
        first[i] = start
        j = count - 1 - i
        end = end * f[j]
        last[j] = end
    m[1] = end


def x_matrix_kernel(
    st_hbm, kx_hbm, ky_hbm, st, ky_t, up, down, fx, ux, wf, wl, mx, source, kx, ky, sems
):
    moves = [
        pltpu.make_async_copy(src, dst, sems.at[n])
        for n, (src, dst) in enumerate(((kx_hbm, kx), (ky_hbm, ky), (st_hbm, st)))
    ]
    for move in moves:
        move.start()
    moves[0].wait()
    sweep(BX, lambda i: x_row(kx, i), fx, ux, wf, wl, mx)
    moves[1].wait()
    for g in range(GROUPS):
        ky_t[pl.ds(g, BY, stride=GROUPS), :] = ky[pl.ds(g * 128, 128), :].T
    moves[2].wait()
    for g in range(GROUPS):
        turned = st[pl.ds(g * 128, 128), :].T
        down[0, pl.ds(g, 1), :] = turned[0:1, :]
        up[0, pl.ds(g, 1), :] = turned[127:128, :]
    down[1] = ky_t[pl.ds(0, GROUPS), :]
    up[1] = ky_t[pl.ds((BY - 1) * GROUPS, GROUPS), :]
    lane = lax.broadcasted_iota(jnp.int32, (128, 128), 1)
    for g in range(GROUPS):
        rows = pl.ds(g * 128, 128)
        s = st[rows, :]
        k = ky[rows, :]
        flux = 0.5 * (k + pltpu.roll(k, 127, 1)) * (pltpu.roll(s, 127, 1) - s)
        flux = jnp.where(lane == 127, 0.0, flux)
        source[rows, :] = s + flux - pltpu.roll(flux, 1, 1)


def y_matrix_kernel(ky_t, fy, uy, yf, yl, my):
    sweep(BY, lambda j: y_row(ky_t, j), fy, uy, yf, yl, my)


def x_ends_kernel(above, below, up, down, source, wf, wl, s_out, send):
    flux_l = 0.5 * (below[1] + down[1]) * (down[0] - below[0])
    flux_r = 0.5 * (above[1] + up[1]) * (above[0] - up[0])
    both = jnp.concatenate([flux_l, flux_r], axis=0)
    turned = jnp.concatenate([both] * 8, axis=0).T
    lane = lax.broadcasted_iota(jnp.int32, (128, 128), 1)
    for g in range(GROUPS):
        rows = pl.ds(g * 128, 128)
        left = jnp.broadcast_to(turned[:, g : g + 1], (128, 128))
        right = jnp.broadcast_to(turned[:, 8 + g : 9 + g], (128, 128))
        extra = jnp.where(lane == 0, -left, jnp.where(lane == 127, right, 0.0))
        s_out[rows, :] = source[rows, :] + extra
    firsts = [jnp.zeros((NZ, BY), F32) for _ in range(2)]
    lasts = [jnp.zeros((NZ, BY), F32) for _ in range(2)]
    for i in range(BX):
        s = x_row(s_out, i)
        firsts[i % 2] = firsts[i % 2] + wf[i] * s
        lasts[i % 2] = lasts[i % 2] + wl[i] * s
    first, last = firsts[0] + firsts[1], lasts[0] + lasts[1]
    for p in range(send.shape[0]):
        send[p, 0] = first
        send[p, 1] = last


def x_local_kernel(s_in, st, fx, ux, d):
    total = x_row(s_in, 0)
    d[0] = total
    for i in range(1, BX):
        total = x_row(s_in, i) + fx[i - 1] * total
        d[i] = total
    x = jnp.zeros_like(total)
    for i in range(BX - 1, -1, -1):
        x = ux[i] * d[i] + fx[i] * x
        d[i] = x - x_row(st, i)


def y_ends_kernel(blocks, ends, d, wf, wl, yf, yl, v_t, send, slots, v):
    enter, leave = interface(blocks, ends, slots, lax.axis_index("gx"))
    for i in range(BX):
        place_rows(v, i, d[i] + wf[i] * enter - wl[i] * leave)
    for g in range(GROUPS):
        v_t[pl.ds(g, BY, stride=GROUPS), :] = v[pl.ds(g * 128, 128), :].T
    firsts = [jnp.zeros((GROUPS, 128), F32) for _ in range(4)]
    lasts = [jnp.zeros((GROUPS, 128), F32) for _ in range(4)]
    for j in range(BY):
        row = y_row(v_t, j)
        firsts[j % 4] = firsts[j % 4] + yf[j] * row
        lasts[j % 4] = lasts[j % 4] + yl[j] * row
    first = (firsts[0] + firsts[1]) + (firsts[2] + firsts[3])
    last = (lasts[0] + lasts[1]) + (lasts[2] + lasts[3])
    for p in range(send.shape[0]):
        send[p, 0] = first
        send[p, 1] = last


def y_local_kernel(v_t, fy, uy, g_t):
    total = y_row(v_t, 0)
    g_t[0] = total
    for j in range(1, BY):
        total = y_row(v_t, j) + fy[j - 1] * total
        g_t[j] = total
    x = jnp.zeros_like(total)
    for j in range(BY - 1, -1, -1):
        x = uy[j] * g_t[j] + fy[j] * x
        g_t[j] = x


def y_solve_kernel(blocks, ends, g_t, yf, yl, st, out_hbm, slots, work, out, sems):
    enter, leave = interface(blocks, ends, slots, lax.axis_index("gy"))
    for j in range(BY):
        work[pl.ds(j * GROUPS, GROUPS), :] = 2.0 * (g_t[j] + yf[j] * enter - yl[j] * leave)
    moves = []
    for g in range(GROUPS):
        rows = pl.ds(g * 128, 128)
        out[rows, :] = st[rows, :] + work[pl.ds(g, BY, stride=GROUPS), :].T
        move = pltpu.make_async_copy(out.at[rows], out_hbm.at[rows], sems.at[g])
        move.start()
        moves.append(move)
    for move in moves:
        move.wait()


def call(kernel, outs, args, scratch=(), cost=100_000, limit=LIMIT):
    vm = pl.BlockSpec(memory_space=pltpu.VMEM)
    hbm = pl.BlockSpec(memory_space=pltpu.HBM)
    return pl.pallas_call(
        kernel,
        out_shape=[
            jax.ShapeDtypeStruct(shape, F32) if far else pltpu.VMEM(shape, F32)
            for shape, far in outs
        ],
        in_specs=[hbm if far else vm for _, far in args],
        out_specs=[hbm if far else vm for _, far in outs],
        scratch_shapes=list(scratch),
        compiler_params=pltpu.CompilerParams(vmem_limit_bytes=limit),
        cost_estimate=pl.CostEstimate(flops=cost, bytes_accessed=cost, transcendentals=0),
    )(*[value for value, _ in args])


def near(*values):
    return [(value, False) for value in values]


def on_device(state, kappa_x, kappa_y):
    flat = [a.reshape(ROWS, BY) for a in (state, kappa_x, kappa_y)]
    plane = (ROWS, BY)
    xs = (BX, NZ, BY)
    ys = (BY, GROUPS, 128)
    edge = (2, GROUPS, 128)
    nx, ny = lax.axis_size("gx"), lax.axis_size("gy")
    st, ky_t, up, down, fx, ux, wf, wl, mx, source = call(
        x_matrix_kernel,
        near(plane, plane, edge, edge, xs, xs, xs, xs, (5, NZ, BY), plane),
        [(a, True) for a in flat],
        [pltpu.VMEM(plane, F32), pltpu.VMEM(plane, F32), pltpu.SemaphoreType.DMA((3,))],
        limit=54 * 1024 * 1024,
    )
    x_blocks = lax.all_gather(mx, "gx")
    below = lax.ppermute(up, "gy", [(i, i + 1) for i in range(ny - 1)])
    above = lax.ppermute(down, "gy", [(i + 1, i) for i in range(ny - 1)])
    fy, uy, yf, yl, my = call(
        y_matrix_kernel, near(ys, ys, ys, ys, (5, GROUPS, 128)), near(ky_t), cost=5_000_000
    )
    y_blocks = lax.all_gather(my, "gy")
    s, send = call(
        x_ends_kernel,
        near(plane, (nx, 2, NZ, BY)),
        near(above, below, up, down, source, wf, wl),
    )
    x_ends = lax.all_to_all(send, "gx", 0, 0)
    (d,) = call(x_local_kernel, near(xs), near(s, st, fx, ux), cost=3_000_000)
    v_t, send = call(
        y_ends_kernel,
        near(plane, (ny, 2, GROUPS, 128)),
        near(x_blocks, x_ends, d, wf, wl, yf, yl),
        [pltpu.VMEM((nx + 1, NZ, BY), F32), pltpu.VMEM(plane, F32)],
    )
    y_ends = lax.all_to_all(send, "gy", 0, 0)
    (g_t,) = call(y_local_kernel, near(ys), near(v_t, fy, uy), cost=5_000_000)
    (out,) = call(
        y_solve_kernel,
        [(plane, True)],
        near(y_blocks, y_ends, g_t, yf, yl, st),
        [
            pltpu.VMEM((ny + 1, GROUPS, 128), F32),
            pltpu.VMEM(plane, F32),
            pltpu.VMEM(plane, F32),
            pltpu.SemaphoreType.DMA((GROUPS,)),
        ],
    )
    return out.reshape(state.shape)


def solution(mesh):
    spec = P(None, "gx", "gy")
    return jax.shard_map(
        on_device, mesh=mesh, in_specs=(spec, spec, spec), out_specs=spec, check_vma=False
    )
```

```python
import jax
import jax.numpy as jnp
from jax import lax
from jax.experimental import pallas as pl
from jax.experimental.pallas import tpu as pltpu
from jax.sharding import PartitionSpec as P

F32 = jnp.float32
NZ, BX, BY = 16, 64, 128
ROWS = NZ * BX
GROUPS = ROWS // 128
LIMIT = 40 * 1024 * 1024


def inverse(x):
    guess = pl.reciprocal(x, approx=True)
    return guess * (2.0 - x * guess)


def x_row(ref, i):
    return jnp.concatenate(
        [ref[pl.ds(i, 8, stride=BX), :], ref[pl.ds(8 * BX + i, 8, stride=BX), :]], axis=0
    )


def y_row(ref, j):
    return ref[pl.ds(j * GROUPS, GROUPS), :]


def place_rows(ref, i, value):
    ref[pl.ds(i, 8, stride=BX), :] = value[:8]
    ref[pl.ds(8 * BX + i, 8, stride=BX), :] = value[8:]


def merge(low, high):
    inv = inverse(2.0 * inverse(low[4] + high[3]) + low[2] + high[0])
    e = (low[6] - high[5]) * inv
    a = low[1] * inv
    b = high[1] * inv
    joined = [
        low[0] - low[1] * a,
        low[1] * b,
        high[2] - high[1] * b,
        low[3],
        high[4],
        low[5] - low[1] * e,
        high[6] + high[1] * e,
    ]
    return joined, (e, a, b)


def flows_of(count, pivot, lower, upper, gain, slots):
    gamma = rho = None
    gammas, rhos = [], []
    for i in range(count + 1):
        if i == 0:
            inv = inverse(pivot(i))
            rho = gain(i) * inv
        else:
            inv = inverse(pivot(i) - lower(i) * gamma)
            rho = (gain(i) + lower(i) * rho) * inv
        if i < count:
            gamma = upper(i) * inv
            gammas.append(gamma)
        rhos.append(rho)
    flow = rhos[count]
    slots[count] = flow
    for i in range(count - 1, -1, -1):
        flow = rhos[i] + gammas[i] * flow
        slots[i] = flow


def x_flows(blocks, slots):
    count = blocks.shape[0]

    def pivot(i):
        if i == 0:
            return 2.0 * inverse(blocks[0, 3]) + blocks[0, 0]
        if i == count:
            return 2.0 * inverse(blocks[count - 1, 4]) + blocks[count - 1, 2]
        return 2.0 * inverse(blocks[i - 1, 4] + blocks[i, 3]) + blocks[i - 1, 2] + blocks[i, 0]

    def gain(i):
        if i == 0:
            return -blocks[0, 5]
        return blocks[i - 1, 6] - blocks[i, 5] if i < count else blocks[i - 1, 6]

    flows_of(count, pivot, lambda i: blocks[i - 1, 1], lambda i: blocks[i, 1], gain, slots)


def y_flows(blocks, slots):
    count = blocks.shape[0]

    def pivot(i):
        if i == 0:
            return blocks[0, 0]
        return blocks[i - 1, 2] + blocks[i, 0] if i < count else blocks[i - 1, 2]

    def gain(i):
        if i == 0:
            return -blocks[0, 3]
        return blocks[i - 1, 4] - blocks[i, 3] if i < count else blocks[i - 1, 4]

    flows_of(count, pivot, lambda i: blocks[i - 1, 1], lambda i: blocks[i, 1], gain, slots)


def load_kernel(st_hbm, kx_hbm, ky_hbm, st, kx, ky, ky_t, up, down, sems):
    moves = [
        pltpu.make_async_copy(src, dst, sems.at[n])
        for n, (src, dst) in enumerate(((ky_hbm, ky), (st_hbm, st), (kx_hbm, kx)))
    ]
    for move in moves:
        move.start()
    moves[0].wait()
    for g in range(GROUPS):
        ky_t[pl.ds(g, BY, stride=GROUPS), :] = ky[pl.ds(g * 128, 128), :].T
    moves[1].wait()
    for g in range(GROUPS):
        turned = st[pl.ds(g * 128, 128), :].T
        down[0, pl.ds(g, 1), :] = turned[0:1, :]
        up[0, pl.ds(g, 1), :] = turned[127:128, :]
    down[1] = ky_t[pl.ds(0, GROUPS), :]
    up[1] = ky_t[pl.ds((BY - 1) * GROUPS, GROUPS), :]
    moves[2].wait()


def sweep(count, row, f, u, first, last):
    ahead = jnp.ones_like(row(0))
    back = jnp.ones_like(ahead)
    low, high = row(0), row(count - 1)
    for i in range(count - 1):
        nxt = row(i + 1)
        r = 0.5 * (low + nxt)
        low = nxt
        inv = inverse(r + ahead)
        ratio = r * inv
        ahead = 1.0 + ratio * ahead
        u[i] = inv
        f[i] = ratio
        j = count - 1 - i
        prev = row(j - 1)
        r = 0.5 * (high + prev)
        high = prev
        ratio = r * inverse(r + back)
        back = 1.0 + ratio * back
        first[j] = ratio
    start = inverse(back)
    end = inverse(ahead)
    lead, trail = start, end
    first[0] = start
    last[count - 1] = end
    u[count - 1] = end
    f[count - 1] = jnp.zeros_like(end)
    for i in range(1, count):
        start = start * first[i]
        first[i] = start
        j = count - 1 - i
        end = end * f[j]
        last[j] = end
    return lead, end, trail


def x_matrix_kernel(st, kx, ky, fx, ux, wf, wl, mx, source):
    values = sweep(BX, lambda i: x_row(kx, i), fx, ux, wf, wl)
    for n, value in enumerate(values + (x_row(kx, 0), x_row(kx, BX - 1))):
        mx[n] = value
    lane = lax.broadcasted_iota(jnp.int32, (128, 128), 1)
    for g in range(GROUPS):
        rows = pl.ds(g * 128, 128)
        s = st[rows, :]
        k = ky[rows, :]
        flux = 0.5 * (k + pltpu.roll(k, 127, 1)) * (pltpu.roll(s, 127, 1) - s)
        flux = jnp.where(lane == 127, 0.0, flux)
        source[rows, :] = s + flux - pltpu.roll(flux, 1, 1)


def y_matrix_kernel(ky_t, came, after, fy, uy, yf, yl, my):
    me = lax.axis_index("gy")
    last = lax.axis_size("gy") - 1
    lead, across, trail = sweep(BY, lambda j: y_row(ky_t, j), fy, uy, yf, yl)
    below = jnp.where(me == 0, 0.0, came[1])
    my[0] = lead + 2.0 * inverse(below + y_row(ky_t, 0))
    my[1] = across
    my[2] = trail + jnp.where(me == last, 2.0 * inverse(y_row(ky_t, BY - 1)), 0.0)


def x_ends_kernel(from_above, from_below, up, down, source, wf, wl, mx, s_out, send):
    me = lax.axis_index("gy")
    below = jnp.where(me == 0, 0.0, from_below[...])
    above = jnp.where(me == lax.axis_size("gy") - 1, 0.0, from_above[...])
    flux_l = 0.5 * (below[1] + down[1]) * (down[0] - below[0])
    flux_r = 0.5 * (above[1] + up[1]) * (above[0] - up[0])
    both = jnp.concatenate([flux_l, flux_r], axis=0)
    turned = jnp.concatenate([both] * 8, axis=0).T
    lane = lax.broadcasted_iota(jnp.int32, (128, 128), 1)
    for g in range(GROUPS):
        rows = pl.ds(g * 128, 128)
        left = jnp.broadcast_to(turned[:, g : g + 1], (128, 128))
        right = jnp.broadcast_to(turned[:, 8 + g : 9 + g], (128, 128))
        extra = jnp.where(lane == 0, -left, jnp.where(lane == 127, right, 0.0))
        s_out[rows, :] = source[rows, :] + extra
    firsts = [jnp.zeros((NZ, BY), F32) for _ in range(2)]
    lasts = [jnp.zeros((NZ, BY), F32) for _ in range(2)]
    for i in range(BX):
        s = x_row(s_out, i)
        firsts[i % 2] = firsts[i % 2] + wf[i] * s
        lasts[i % 2] = lasts[i % 2] + wl[i] * s
    send[0:5] = mx[...]
    send[5] = firsts[0] + firsts[1]
    send[6] = lasts[0] + lasts[1]


def x_local_kernel(s_in, st, fx, ux, d):
    total = x_row(s_in, 0)
    d[0] = total
    for i in range(1, BX):
        total = x_row(s_in, i) + fx[i - 1] * total
        d[i] = total
    x = jnp.zeros_like(total)
    for i in range(BX - 1, -1, -1):
        x = ux[i] * d[i] + fx[i] * x
        d[i] = x - x_row(st, i)


def x_merge_kernel(own, other, send, coefs):
    core = lax.rem(lax.axis_index("gx"), 2)
    mine, theirs = [own[n] for n in range(7)], [other[n] for n in range(7)]
    low = [jnp.where(core == 0, a, b) for a, b in zip(mine, theirs)]
    high = [jnp.where(core == 0, b, a) for a, b in zip(mine, theirs)]
    joined, flow = merge(low, high)
    for p in range(send.shape[0]):
        for n in range(7):
            send[p, n] = joined[n]
    for n in range(3):
        coefs[n] = flow[n]


def y_ends_kernel(blocks, coefs, d, wf, wl, yf, yl, my, v_t, send, slots, v):
    me = lax.axis_index("gx")
    x_flows(blocks, slots)
    place = lax.div(me, 2)
    enter, leave = slots[place], slots[place + 1]
    middle = coefs[0] + coefs[1] * enter + coefs[2] * leave
    low = lax.rem(me, 2) == 0
    enter, leave = jnp.where(low, enter, middle), jnp.where(low, middle, leave)
    for i in range(BX):
        place_rows(v, i, d[i] + wf[i] * enter - wl[i] * leave)
    for g in range(GROUPS):
        v_t[pl.ds(g, BY, stride=GROUPS), :] = v[pl.ds(g * 128, 128), :].T
    firsts = [jnp.zeros((GROUPS, 128), F32) for _ in range(4)]
    lasts = [jnp.zeros((GROUPS, 128), F32) for _ in range(4)]
    for j in range(BY):
        row = y_row(v_t, j)
        firsts[j % 4] = firsts[j % 4] + yf[j] * row
        lasts[j % 4] = lasts[j % 4] + yl[j] * row
    first = (firsts[0] + firsts[1]) + (firsts[2] + firsts[3])
    last = (lasts[0] + lasts[1]) + (lasts[2] + lasts[3])
    for p in range(send.shape[0]):
        send[p, 0:3] = my[...]
        send[p, 3] = first
        send[p, 4] = last


def y_local_kernel(v_t, fy, uy, g_t):
    total = y_row(v_t, 0)
    g_t[0] = total
    for j in range(1, BY):
        total = y_row(v_t, j) + fy[j - 1] * total
        g_t[j] = total
    x = jnp.zeros_like(total)
    for j in range(BY - 1, -1, -1):
        x = uy[j] * g_t[j] + fy[j] * x
        g_t[j] = x


def y_solve_kernel(blocks, g_t, yf, yl, st, out_hbm, slots, work, out, sems):
    me = lax.axis_index("gy")
    y_flows(blocks, slots)
    enter, leave = slots[me], slots[me + 1]
    for j in range(BY):
        work[pl.ds(j * GROUPS, GROUPS), :] = 2.0 * (g_t[j] + yf[j] * enter - yl[j] * leave)
    moves = []
    for g in range(GROUPS):
        rows = pl.ds(g * 128, 128)
        out[rows, :] = st[rows, :] + work[pl.ds(g, BY, stride=GROUPS), :].T
        move = pltpu.make_async_copy(out.at[rows], out_hbm.at[rows], sems.at[g])
        move.start()
        moves.append(move)
    for move in moves:
        move.wait()


def call(kernel, outs, args, scratch=(), cost=100_000):
    vm = pl.BlockSpec(memory_space=pltpu.VMEM)
    hbm = pl.BlockSpec(memory_space=pltpu.HBM)
    return pl.pallas_call(
        kernel,
        out_shape=[
            jax.ShapeDtypeStruct(shape, F32) if far else pltpu.VMEM(shape, F32)
            for shape, far in outs
        ],
        in_specs=[hbm if far else vm for _, far in args],
        out_specs=[hbm if far else vm for _, far in outs],
        scratch_shapes=list(scratch),
        compiler_params=pltpu.CompilerParams(vmem_limit_bytes=LIMIT),
        cost_estimate=pl.CostEstimate(flops=cost, bytes_accessed=cost, transcendentals=0),
    )(*[value for value, _ in args])


def near(*values):
    return [(value, False) for value in values]


def on_device(state, kappa_x, kappa_y):
    flat = [
        pltpu.with_memory_space_constraint(a.reshape(ROWS, BY), pltpu.HBM)
        for a in (state, kappa_x, kappa_y)
    ]
    plane = (ROWS, BY)
    xs = (BX, NZ, BY)
    ys = (BY, GROUPS, 128)
    x_block = (7, NZ, BY)
    edge = (2, GROUPS, 128)
    nx, ny = lax.axis_size("gx"), lax.axis_size("gy")
    chips = nx // 2
    st, kx, ky, ky_t, up, down = call(
        load_kernel,
        near(plane, plane, plane, plane, edge, edge),
        [(a, True) for a in flat],
        [pltpu.SemaphoreType.DMA((3,))],
    )
    below = lax.ppermute(up, "gy", [(i, (i + 1) % ny) for i in range(ny)])
    above = lax.ppermute(down, "gy", [((i + 1) % ny, i) for i in range(ny)])
    fx, ux, wf, wl, mx, source = call(
        x_matrix_kernel, near(xs, xs, xs, xs, (5, NZ, BY), plane), near(st, kx, ky), cost=5_000_000
    )
    s, ends = call(
        x_ends_kernel, near(plane, x_block), near(above, below, up, down, source, wf, wl, mx)
    )
    other = lax.ppermute(ends, "gx", [(i, i ^ 1) for i in range(nx)])
    (d,) = call(x_local_kernel, near(xs), near(s, st, fx, ux), cost=3_000_000)
    send, coefs = call(x_merge_kernel, near((chips,) + x_block, (3, NZ, BY)), near(ends, other))
    groups = [list(range(c, nx, 2)) for c in range(2)]
    x_blocks = lax.all_to_all(send, "gx", 0, 0, axis_index_groups=groups)
    fy, uy, yf, yl, my = call(
        y_matrix_kernel,
        near(ys, ys, ys, ys, (3, GROUPS, 128)),
        near(ky_t, below, coefs),
        cost=5_000_000,
    )
    v_t, send = call(
        y_ends_kernel,
        near(plane, (ny, 5, GROUPS, 128)),
        near(x_blocks, coefs, d, wf, wl, yf, yl, my),
        [pltpu.VMEM((chips + 1, NZ, BY), F32), pltpu.VMEM(plane, F32)],
    )
    y_blocks = lax.all_to_all(send, "gy", 0, 0)
    (g_t,) = call(y_local_kernel, near(ys), near(v_t, fy, uy), cost=5_000_000)
    (out,) = call(
        y_solve_kernel,
        [(plane, True)],
        near(y_blocks, g_t, yf, yl, st),
        [
            pltpu.VMEM((ny + 1, GROUPS, 128), F32),
            pltpu.VMEM(plane, F32),
            pltpu.VMEM(plane, F32),
            pltpu.SemaphoreType.DMA((GROUPS,)),
        ],
    )
    return out.reshape(state.shape)


def solution(mesh):
    spec = P(None, "gx", "gy")
    return jax.shard_map(
        on_device, mesh=mesh, in_specs=(spec, spec, spec), out_specs=spec, check_vma=False
    )
```

```python
import jax
import jax.numpy as jnp
from jax import lax
from jax.experimental import pallas as pl
from jax.experimental.pallas import tpu as pltpu
from jax.sharding import PartitionSpec as P

F32 = jnp.float32
NZ, BX, BY = 16, 64, 128
ROWS = NZ * BX
GROUPS = ROWS // 128
LIMIT = 8 * 1024 * 1024


def inverse(x):
    guess = pl.reciprocal(x, approx=True)
    return guess * (2.0 - x * guess)


def x_row(ref, i):
    return jnp.concatenate(
        [ref[pl.ds(i, 8, stride=BX), :], ref[pl.ds(8 * BX + i, 8, stride=BX), :]], axis=0
    )


def y_row(ref, j):
    return ref[pl.ds(j * GROUPS, GROUPS), :]


def place_rows(ref, i, value):
    ref[pl.ds(i, 8, stride=BX), :] = value[:8]
    ref[pl.ds(8 * BX + i, 8, stride=BX), :] = value[8:]


def merge(low, high):
    inv = inverse(2.0 * inverse(low[4] + high[3]) + low[2] + high[0])
    e = (low[6] - high[5]) * inv
    a = low[1] * inv
    b = high[1] * inv
    joined = [
        low[0] - low[1] * a,
        low[1] * b,
        high[2] - high[1] * b,
        low[3],
        high[4],
        low[5] - low[1] * e,
        high[6] + high[1] * e,
    ]
    return joined, (e, a, b)


def flows_of(count, pivot, lower, upper, gain, slots):
    gamma = rho = None
    gammas, rhos = [], []
    for i in range(count + 1):
        if i == 0:
            inv = inverse(pivot(i))
            rho = gain(i) * inv
        else:
            inv = inverse(pivot(i) - lower(i) * gamma)
            rho = (gain(i) + lower(i) * rho) * inv
        if i < count:
            gamma = upper(i) * inv
            gammas.append(gamma)
        rhos.append(rho)
    flow = rhos[count]
    slots[count] = flow
    for i in range(count - 1, -1, -1):
        flow = rhos[i] + gammas[i] * flow
        slots[i] = flow


def x_flows(own, others, place, blocks, slots):
    count = blocks.shape[0]
    blocks[place] = own[...]
    for k, other in enumerate(others):
        blocks[place ^ (k + 1)] = other[...]

    def pivot(i):
        if i == 0:
            return 2.0 * inverse(blocks[0, 3]) + blocks[0, 0]
        if i == count:
            return 2.0 * inverse(blocks[count - 1, 4]) + blocks[count - 1, 2]
        return 2.0 * inverse(blocks[i - 1, 4] + blocks[i, 3]) + blocks[i - 1, 2] + blocks[i, 0]

    def gain(i):
        if i == 0:
            return -blocks[0, 5]
        return blocks[i - 1, 6] - blocks[i, 5] if i < count else blocks[i - 1, 6]

    flows_of(count, pivot, lambda i: blocks[i - 1, 1], lambda i: blocks[i, 1], gain, slots)


def y_flows(blocks, slots):
    count = blocks.shape[0]

    def pivot(i):
        if i == 0:
            return blocks[0, 0]
        return blocks[i - 1, 2] + blocks[i, 0] if i < count else blocks[i - 1, 2]

    def gain(i):
        if i == 0:
            return -blocks[0, 3]
        return blocks[i - 1, 4] - blocks[i, 3] if i < count else blocks[i - 1, 4]

    flows_of(count, pivot, lambda i: blocks[i - 1, 1], lambda i: blocks[i, 1], gain, slots)


def load_kernel(st_hbm, kx_hbm, ky_hbm, st, kx, ky, ky_t, mine, first, second, sems):
    moves = [
        pltpu.make_async_copy(src, dst, sems.at[n])
        for n, (src, dst) in enumerate(((ky_hbm, ky), (st_hbm, st), (kx_hbm, kx)))
    ]
    for move in moves:
        move.start()
    moves[0].wait()
    for g in range(GROUPS):
        ky_t[pl.ds(g, BY, stride=GROUPS), :] = ky[pl.ds(g * 128, 128), :].T
    moves[1].wait()
    for g in range(GROUPS):
        turned = st[pl.ds(g * 128, 128), :].T
        mine[0, pl.ds(g, 1), :] = turned[0:1, :]
        mine[2, pl.ds(g, 1), :] = turned[127:128, :]
    mine[1] = ky_t[pl.ds(0, GROUPS), :]
    mine[3] = ky_t[pl.ds((BY - 1) * GROUPS, GROUPS), :]
    even = lax.rem(lax.axis_index("gy"), 2) == 0
    low, high = mine[0:2], mine[2:4]
    first[...] = jnp.where(even, high, low)
    second[...] = jnp.where(even, low, high)
    moves[2].wait()


def sweep(count, row, f, u, first, last):
    ahead = jnp.ones_like(row(0))
    back = jnp.ones_like(ahead)
    low, high = row(0), row(count - 1)
    for i in range(count - 1):
        nxt = row(i + 1)
        r = 0.5 * (low + nxt)
        low = nxt
        inv = inverse(r + ahead)
        ratio = r * inv
        ahead = 1.0 + ratio * ahead
        u[i] = inv
        f[i] = ratio
        j = count - 1 - i
        prev = row(j - 1)
        r = 0.5 * (high + prev)
        high = prev
        ratio = r * inverse(r + back)
        back = 1.0 + ratio * back
        first[j] = ratio
    start = inverse(back)
    end = inverse(ahead)
    lead, trail = start, end
    first[0] = start
    last[count - 1] = end
    u[count - 1] = end
    f[count - 1] = jnp.zeros_like(end)
    for i in range(1, count):
        start = start * first[i]
        first[i] = start
        j = count - 1 - i
        end = end * f[j]
        last[j] = end
    return lead, end, trail


def x_matrix_kernel(st, kx, ky, fx, ux, wf, wl, mx, source):
    values = sweep(BX, lambda i: x_row(kx, i), fx, ux, wf, wl)
    for n, value in enumerate(values + (x_row(kx, 0), x_row(kx, BX - 1))):
        mx[n] = value
    lane = lax.broadcasted_iota(jnp.int32, (128, 128), 1)
    for g in range(GROUPS):
        rows = pl.ds(g * 128, 128)
        s = st[rows, :]
        k = ky[rows, :]
        flux = 0.5 * (k + pltpu.roll(k, 127, 1)) * (pltpu.roll(s, 127, 1) - s)
        flux = jnp.where(lane == 127, 0.0, flux)
        source[rows, :] = s + flux - pltpu.roll(flux, 1, 1)


def y_matrix_kernel(ky_t, came1, came2, after, yf, yl, my, f, u):
    me = lax.axis_index("gy")
    last = lax.axis_size("gy") - 1
    lead, across, trail = sweep(BY, lambda j: y_row(ky_t, j), f, u, yf, yl)
    below = jnp.where(lax.rem(me, 2) == 0, came2[1], came1[1])
    below = jnp.where(me == 0, 0.0, below)
    my[0] = lead + 2.0 * inverse(below + y_row(ky_t, 0))
    my[1] = across
    my[2] = trail + jnp.where(me == last, 2.0 * inverse(y_row(ky_t, BY - 1)), 0.0)


def x_ends_kernel(came1, came2, mine, source, wf, wl, mx, s_out, send):
    me = lax.axis_index("gy")
    even = lax.rem(me, 2) == 0
    below = jnp.where(me == 0, 0.0, jnp.where(even, came2[...], came1[...]))
    above = jnp.where(me == lax.axis_size("gy") - 1, 0.0, jnp.where(even, came1[...], came2[...]))
    flux_l = 0.5 * (below[1] + mine[1]) * (mine[0] - below[0])
    flux_r = 0.5 * (above[1] + mine[3]) * (above[0] - mine[2])
    both = jnp.concatenate([flux_l, flux_r], axis=0)
    turned = jnp.concatenate([both] * 8, axis=0).T
    lane = lax.broadcasted_iota(jnp.int32, (128, 128), 1)
    for g in range(GROUPS):
        rows = pl.ds(g * 128, 128)
        left = jnp.broadcast_to(turned[:, g : g + 1], (128, 128))
        right = jnp.broadcast_to(turned[:, 8 + g : 9 + g], (128, 128))
        extra = jnp.where(lane == 0, -left, jnp.where(lane == 127, right, 0.0))
        s_out[rows, :] = source[rows, :] + extra
    firsts = [jnp.zeros((NZ, BY), F32) for _ in range(2)]
    lasts = [jnp.zeros((NZ, BY), F32) for _ in range(2)]
    for i in range(BX):
        s = x_row(s_out, i)
        firsts[i % 2] = firsts[i % 2] + wf[i] * s
        lasts[i % 2] = lasts[i % 2] + wl[i] * s
    send[0:5] = mx[...]
    send[5] = firsts[0] + firsts[1]
    send[6] = lasts[0] + lasts[1]


def x_local_kernel(s_in, st, fx, ux, d):
    total = x_row(s_in, 0)
    d[0] = total
    for i in range(1, BX):
        total = x_row(s_in, i) + fx[i - 1] * total
        d[i] = total
    x = jnp.zeros_like(total)
    for i in range(BX - 1, -1, -1):
        x = ux[i] * d[i] + fx[i] * x
        d[i] = x - x_row(st, i)


def x_merge_kernel(own, other, after, send, coefs):
    core = lax.rem(lax.axis_index("gx"), 2)
    mine, theirs = [own[n] for n in range(7)], [other[n] for n in range(7)]
    low = [jnp.where(core == 0, a, b) for a, b in zip(mine, theirs)]
    high = [jnp.where(core == 0, b, a) for a, b in zip(mine, theirs)]
    joined, flow = merge(low, high)
    for n in range(7):
        send[n] = joined[n]
    for n in range(3):
        coefs[n] = flow[n]


def y_ends_kernel(
    own, other1, other2, other3, coefs, d, wf, wl, yf, yl, my, v_t, send, blocks, slots, v
):
    me = lax.axis_index("gx")
    place = lax.div(me, 2)
    x_flows(own, (other1, other2, other3), place, blocks, slots)
    enter, leave = slots[place], slots[place + 1]
    middle = coefs[0] + coefs[1] * enter + coefs[2] * leave
    low = lax.rem(me, 2) == 0
    enter, leave = jnp.where(low, enter, middle), jnp.where(low, middle, leave)
    for i in range(BX):
        place_rows(v, i, d[i] + wf[i] * enter - wl[i] * leave)
    for g in range(GROUPS):
        v_t[pl.ds(g, BY, stride=GROUPS), :] = v[pl.ds(g * 128, 128), :].T
    firsts = [jnp.zeros((GROUPS, 128), F32) for _ in range(4)]
    lasts = [jnp.zeros((GROUPS, 128), F32) for _ in range(4)]
    for j in range(BY):
        row = y_row(v_t, j)
        firsts[j % 4] = firsts[j % 4] + yf[j] * row
        lasts[j % 4] = lasts[j % 4] + yl[j] * row
    first = (firsts[0] + firsts[1]) + (firsts[2] + firsts[3])
    last = (lasts[0] + lasts[1]) + (lasts[2] + lasts[3])
    for p in range(send.shape[0]):
        send[p, 0:3] = my[...]
        send[p, 3] = first
        send[p, 4] = last


def y_local_kernel(v_t, ky_t, st_hbm, g_t, st, f, u, sem):
    move = pltpu.make_async_copy(st_hbm, st, sem)
    move.start()
    total = y_row(v_t, 0)
    g_t[0] = total
    ahead = jnp.ones_like(total)
    low = y_row(ky_t, 0)
    for j in range(1, BY):
        high = y_row(ky_t, j)
        r = 0.5 * (low + high)
        low = high
        inv = inverse(r + ahead)
        ratio = r * inv
        ahead = 1.0 + ratio * ahead
        u[j - 1] = inv
        f[j - 1] = ratio
        total = y_row(v_t, j) + ratio * total
        g_t[j] = total
    x = total * inverse(ahead)
    g_t[BY - 1] = x
    for j in range(BY - 2, -1, -1):
        x = u[j] * g_t[j] + f[j] * x
        g_t[j] = x
    move.wait()


def y_solve_kernel(blocks, g_t, yf, yl, st, out_hbm, slots, work, out, sems):
    me = lax.axis_index("gy")
    y_flows(blocks, slots)
    enter, leave = slots[me], slots[me + 1]
    for j in range(BY):
        work[pl.ds(j * GROUPS, GROUPS), :] = 2.0 * (g_t[j] + yf[j] * enter - yl[j] * leave)
    moves = []
    for g in range(GROUPS):
        rows = pl.ds(g * 128, 128)
        out[rows, :] = st[rows, :] + work[pl.ds(g, BY, stride=GROUPS), :].T
        move = pltpu.make_async_copy(out.at[rows], out_hbm.at[rows], sems.at[g])
        move.start()
        moves.append(move)
    for move in moves:
        move.wait()


def call(kernel, outs, args, scratch=(), cost=100_000):
    vm = pl.BlockSpec(memory_space=pltpu.VMEM)
    hbm = pl.BlockSpec(memory_space=pltpu.HBM)
    return pl.pallas_call(
        kernel,
        out_shape=[
            jax.ShapeDtypeStruct(shape, F32) if far else pltpu.VMEM(shape, F32)
            for shape, far in outs
        ],
        in_specs=[hbm if far else vm for _, far in args],
        out_specs=[hbm if far else vm for _, far in outs],
        scratch_shapes=list(scratch),
        compiler_params=pltpu.CompilerParams(vmem_limit_bytes=LIMIT),
        cost_estimate=pl.CostEstimate(flops=cost, bytes_accessed=cost, transcendentals=0),
    )(*[value for value, _ in args])


def near(*values):
    return [(value, False) for value in values]


def on_device(state, kappa_x, kappa_y):
    flat = [
        pltpu.with_memory_space_constraint(a.reshape(ROWS, BY), pltpu.HBM)
        for a in (state, kappa_x, kappa_y)
    ]
    plane = (ROWS, BY)
    xs = (BX, NZ, BY)
    ys = (BY, GROUPS, 128)
    x_block = (7, NZ, BY)
    edge = (2, GROUPS, 128)
    nx, ny = lax.axis_size("gx"), lax.axis_size("gy")
    chips = nx // 2
    st, kx, ky, ky_t, mine, first, second = call(
        load_kernel,
        near(plane, plane, plane, plane, (4, GROUPS, 128), edge, edge),
        [(a, True) for a in flat],
        [pltpu.SemaphoreType.DMA((3,))],
    )
    came1 = lax.ppermute(first, "gy", [(i, i ^ 1) for i in range(ny)])
    came2 = lax.ppermute(second, "gy", [(i, (i + 2 * (i % 2) - 1) % ny) for i in range(ny)])
    fx, ux, wf, wl, mx, source = call(
        x_matrix_kernel, near(xs, xs, xs, xs, (5, NZ, BY), plane), near(st, kx, ky), cost=5_000_000
    )
    s, ends = call(
        x_ends_kernel, near(plane, x_block), near(came1, came2, mine, source, wf, wl, mx)
    )
    other = lax.ppermute(ends, "gx", [(i, i ^ 1) for i in range(nx)])
    (d,) = call(x_local_kernel, near(xs), near(s, st, fx, ux), cost=3_000_000)
    chip, coefs = call(x_merge_kernel, near(x_block, (3, NZ, BY)), near(ends, other, d))
    others = [lax.ppermute(chip, "gx", [(i, i ^ (2 * k)) for i in range(nx)]) for k in range(1, chips)]
    yf, yl, my = call(
        y_matrix_kernel,
        near(ys, ys, (3, GROUPS, 128)),
        near(ky_t, came1, came2, coefs),
        [pltpu.VMEM(ys, F32), pltpu.VMEM(ys, F32)],
        cost=5_000_000,
    )
    v_t, send = call(
        y_ends_kernel,
        near(plane, (ny, 5, GROUPS, 128)),
        near(chip, *others, coefs, d, wf, wl, yf, yl, my),
        [
            pltpu.VMEM((chips,) + x_block, F32),
            pltpu.VMEM((chips + 1, NZ, BY), F32),
            pltpu.VMEM(plane, F32),
        ],
    )
    y_blocks = lax.all_to_all(send, "gy", 0, 0)
    g_t, st = call(
        y_local_kernel,
        near(ys, plane),
        near(v_t, ky_t) + [(flat[0], True)],
        [pltpu.VMEM(ys, F32), pltpu.VMEM(ys, F32), pltpu.SemaphoreType.DMA],
        cost=5_000_000,
    )
    (out,) = call(
        y_solve_kernel,
        [(plane, True)],
        near(y_blocks, g_t, yf, yl, st),
        [
            pltpu.VMEM((ny + 1, GROUPS, 128), F32),
            pltpu.VMEM(plane, F32),
            pltpu.VMEM(plane, F32),
            pltpu.SemaphoreType.DMA((GROUPS,)),
        ],
    )
    return out.reshape(state.shape)


def solution(mesh):
    spec = P(None, "gx", "gy")
    return jax.shard_map(
        on_device, mesh=mesh, in_specs=(spec, spec, spec), out_specs=spec, check_vma=False
    )
```

```python
import jax
import jax.numpy as jnp
from jax import lax
from jax.experimental import pallas as pl
from jax.experimental.pallas import tpu as pltpu
from jax.sharding import PartitionSpec as P

F32 = jnp.float32
NZ, BX, BY = 16, 64, 128
ROWS = NZ * BX
GROUPS = ROWS // 128
LIMIT = 8 * 1024 * 1024
CHUNKS = 4


def inverse(x):
    guess = pl.reciprocal(x, approx=True)
    return guess * (2.0 - x * guess)


def x_row(ref, i):
    return jnp.concatenate(
        [ref[pl.ds(i, 8, stride=BX), :], ref[pl.ds(8 * BX + i, 8, stride=BX), :]], axis=0
    )


def y_row(ref, j):
    return ref[pl.ds(j * GROUPS, GROUPS), :]


def place_rows(ref, i, value):
    ref[pl.ds(i, 8, stride=BX), :] = value[:8]
    ref[pl.ds(8 * BX + i, 8, stride=BX), :] = value[8:]


def merge(low, high):
    inv = inverse(2.0 * inverse(low[4] + high[3]) + low[2] + high[0])
    e = (low[6] - high[5]) * inv
    a = low[1] * inv
    b = high[1] * inv
    joined = [
        low[0] - low[1] * a,
        low[1] * b,
        high[2] - high[1] * b,
        low[3],
        high[4],
        low[5] - low[1] * e,
        high[6] + high[1] * e,
    ]
    return joined, (e, a, b)


def flows_of(count, pivot, lower, upper, gain, slots):
    half = (count + 1) // 2
    up, down = {}, {}
    for n in range(half + 1):
        i = n
        if i < half:
            gain_i, pivot_i = gain(i), pivot(i)
            if i:
                gain_i = gain_i + lower(i) * up[i - 1][0]
                pivot_i = pivot_i - lower(i) * up[i - 1][1]
            inv = inverse(pivot_i)
            up[i] = gain_i * inv, upper(i) * inv
        i = count - n
        if i > half:
            gain_i, pivot_i = gain(i), pivot(i)
            if n:
                gain_i = gain_i + upper(i) * down[i + 1][0]
                pivot_i = pivot_i - upper(i) * down[i + 1][1]
            inv = inverse(pivot_i)
            down[i] = gain_i * inv, lower(i) * inv
    below, above = up[half - 1], down[half + 1]
    low, high = lower(half), upper(half)
    flow = (gain(half) + low * below[0] + high * above[0]) * inverse(
        pivot(half) - low * below[1] - high * above[1]
    )
    slots[half] = flow
    rising = flow
    for n in range(1, half + 1):
        if half - n >= 0:
            flow = up[half - n][0] + up[half - n][1] * flow
            slots[half - n] = flow
        if half + n <= count:
            rising = down[half + n][0] + down[half + n][1] * rising
            slots[half + n] = rising


def x_flows(own, others, place, blocks, slots):
    count = blocks.shape[0]
    blocks[place] = own[...]
    for k, other in enumerate(others):
        blocks[place ^ (k + 1)] = other[...]

    def pivot(i):
        if i == 0:
            return 2.0 * inverse(blocks[0, 3]) + blocks[0, 0]
        if i == count:
            return 2.0 * inverse(blocks[count - 1, 4]) + blocks[count - 1, 2]
        return 2.0 * inverse(blocks[i - 1, 4] + blocks[i, 3]) + blocks[i - 1, 2] + blocks[i, 0]

    def gain(i):
        if i == 0:
            return -blocks[0, 5]
        return blocks[i - 1, 6] - blocks[i, 5] if i < count else blocks[i - 1, 6]

    flows_of(count, pivot, lambda i: blocks[i - 1, 1], lambda i: blocks[i, 1], gain, slots)


def y_flows(blocks, slots):
    count = blocks.shape[0]

    def pivot(i):
        if i == 0:
            return blocks[0, 0]
        return blocks[i - 1, 2] + blocks[i, 0] if i < count else blocks[i - 1, 2]

    def gain(i):
        if i == 0:
            return -blocks[0, 3]
        return blocks[i - 1, 4] - blocks[i, 3] if i < count else blocks[i - 1, 4]

    flows_of(count, pivot, lambda i: blocks[i - 1, 1], lambda i: blocks[i, 1], gain, slots)


def load_kernel(st_hbm, kx_hbm, ky_hbm, st, kx, ky, ky_t, mine, first, second, sems):
    chunk = ROWS // CHUNKS
    waits = []
    for c in range(CHUNKS):
        rows = pl.ds(c * chunk, chunk)
        waits.append(
            [
                pltpu.make_async_copy(src.at[rows], dst.at[rows], sems.at[2 * c + n])
                for n, (src, dst) in enumerate(((ky_hbm, ky), (st_hbm, st)))
            ]
        )
        for move in waits[-1]:
            move.start()
    rest = pltpu.make_async_copy(kx_hbm, kx, sems.at[2 * CHUNKS])
    rest.start()
    for g in range(GROUPS):
        if g * CHUNKS % GROUPS == 0:
            for move in waits[g * CHUNKS // GROUPS]:
                move.wait()
        rows = pl.ds(g * 128, 128)
        ky_t[pl.ds(g, BY, stride=GROUPS), :] = ky[rows, :].T
        turned = st[rows, :].T
        mine[0, pl.ds(g, 1), :] = turned[0:1, :]
        mine[2, pl.ds(g, 1), :] = turned[127:128, :]
    mine[1] = ky_t[pl.ds(0, GROUPS), :]
    mine[3] = ky_t[pl.ds((BY - 1) * GROUPS, GROUPS), :]
    even = lax.rem(lax.axis_index("gy"), 2) == 0
    low, high = mine[0:2], mine[2:4]
    first[...] = jnp.where(even, high, low)
    second[...] = jnp.where(even, low, high)
    rest.wait()


def sweep(count, row, f, u, ratios, put_first, put_last):
    ahead = jnp.ones_like(row(0))
    back = jnp.ones_like(ahead)
    low, high = row(0), row(count - 1)
    for i in range(count - 1):
        nxt = row(i + 1)
        r = 0.5 * (low + nxt)
        low = nxt
        inv = inverse(r + ahead)
        ratio = r * inv
        ahead = 1.0 + ratio * ahead
        u[i] = inv
        f[i] = ratio
        j = count - 1 - i
        prev = row(j - 1)
        r = 0.5 * (high + prev)
        high = prev
        ratio = r * inverse(r + back)
        back = 1.0 + ratio * back
        ratios[j] = ratio
    start = inverse(back)
    end = inverse(ahead)
    lead, trail = start, end
    put_first(0, start)
    put_last(count - 1, end)
    u[count - 1] = end
    f[count - 1] = jnp.zeros_like(end)
    for i in range(1, count):
        start = start * ratios[i]
        put_first(i, start)
        j = count - 1 - i
        end = end * f[j]
        put_last(j, end)
    return lead, end, trail


def x_matrix_kernel(st, kx, ky, fx, ux, wf, wl, part, edges, source, ratios):
    lane = lax.broadcasted_iota(jnp.int32, (128, 128), 1)
    for g in range(GROUPS):
        rows = pl.ds(g * 128, 128)
        s = st[rows, :]
        k = ky[rows, :]
        flux = 0.5 * (k + pltpu.roll(k, 127, 1)) * (pltpu.roll(s, 127, 1) - s)
        flux = jnp.where(lane == 127, 0.0, flux)
        source[rows, :] = s + flux - pltpu.roll(flux, 1, 1)
    sums = [[jnp.zeros((NZ, BY), F32) for _ in range(2)] for _ in range(2)]

    def put(ref, total):
        def store(i, value):
            place_rows(ref, i, value)
            total[i % 2] = total[i % 2] + value * x_row(source, i)

        return store

    values = sweep(BX, lambda i: x_row(kx, i), fx, ux, ratios, put(wf, sums[0]), put(wl, sums[1]))
    values += (x_row(kx, 0), x_row(kx, BX - 1), sums[0][0] + sums[0][1], sums[1][0] + sums[1][1])
    for n, value in enumerate(values):
        part[n] = value
    for n, ref in enumerate((wf, wl)):
        for g in range(GROUPS):
            turned = ref[pl.ds(g * 128, 128), :].T
            edges[2 * n, pl.ds(g, 1), :] = turned[0:1, :]
            edges[2 * n + 1, pl.ds(g, 1), :] = turned[127:128, :]


def y_matrix_kernel(ky_t, came2, came1, after, yf, yl, my, f, u, ratios):
    def put(ref):
        def store(j, value):
            ref[j] = value

        return store

    me = lax.axis_index("gy")
    last = lax.axis_size("gy") - 1
    lead, across, trail = sweep(BY, lambda j: y_row(ky_t, j), f, u, ratios, put(yf), put(yl))
    below = jnp.where(lax.rem(me, 2) == 0, came2[1], came1[1])
    below = jnp.where(me == 0, 0.0, below)
    my[0] = lead + 2.0 * inverse(below + y_row(ky_t, 0))
    my[1] = across
    my[2] = trail + jnp.where(me == last, 2.0 * inverse(y_row(ky_t, BY - 1)), 0.0)


def x_ends_kernel(came2, came1, mine, part, edges, send, flux, rows):
    me = lax.axis_index("gy")
    even = lax.rem(me, 2) == 0
    below = jnp.where(me == 0, 0.0, jnp.where(even, came2[...], came1[...]))
    above = jnp.where(me == lax.axis_size("gy") - 1, 0.0, jnp.where(even, came1[...], came2[...]))
    enter = 0.5 * (below[1] + mine[1]) * (mine[0] - below[0])
    leave = 0.5 * (above[1] + mine[3]) * (above[0] - mine[2])
    flux[0] = enter
    flux[1] = leave
    lane = lax.broadcasted_iota(jnp.int32, (GROUPS, 128), 1)
    send[0:5] = part[0:5]
    for n in range(2):
        low = -edges[2 * n] * enter
        high = edges[2 * n + 1] * leave
        for h in range(2):
            inside = lane // BX == h
            at_low = jnp.sum(jnp.where(inside, low, 0.0), axis=1, keepdims=True)
            at_high = jnp.sum(jnp.where(inside, high, 0.0), axis=1, keepdims=True)
            value = jnp.where(lane == 0, at_low, jnp.where(lane == 127, at_high, 0.0))
            rows[n, pl.ds(h, GROUPS, stride=2), :] = value
        send[5 + n] = part[5 + n] + rows[n]


def x_local_kernel(source, flux, st, fx, ux, d, s, work):
    both = jnp.concatenate([flux[0], flux[1]], axis=0)
    turned = jnp.concatenate([both] * 8, axis=0).T
    lane = lax.broadcasted_iota(jnp.int32, (128, 128), 1)
    for g in range(GROUPS):
        rows = pl.ds(g * 128, 128)
        left = jnp.broadcast_to(turned[:, g : g + 1], (128, 128))
        right = jnp.broadcast_to(turned[:, 8 + g : 9 + g], (128, 128))
        extra = jnp.where(lane == 0, -left, jnp.where(lane == 127, right, 0.0))
        s[rows, :] = source[rows, :] + extra
    total = x_row(s, 0)
    work[0] = total
    for i in range(1, BX):
        total = x_row(s, i) + fx[i - 1] * total
        work[i] = total
    x = jnp.zeros_like(total)
    for i in range(BX - 1, -1, -1):
        x = ux[i] * work[i] + fx[i] * x
        place_rows(d, i, x - x_row(st, i))


def x_merge_kernel(own, other, after, send, coefs):
    core = lax.rem(lax.axis_index("gx"), 2)
    mine, theirs = [own[n] for n in range(7)], [other[n] for n in range(7)]
    low = [jnp.where(core == 0, a, b) for a, b in zip(mine, theirs)]
    high = [jnp.where(core == 0, b, a) for a, b in zip(mine, theirs)]
    joined, flow = merge(low, high)
    for n in range(7):
        send[n] = joined[n]
    for n in range(3):
        coefs[n] = flow[n]


def y_ends_kernel(
    own, other1, other2, other3, coefs, d, wf, wl, yf, yl, my, v_t, send, blocks, slots, flows
):
    me = lax.axis_index("gx")
    place = lax.div(me, 2)
    x_flows(own, (other1, other2, other3), place, blocks, slots)
    enter, leave = slots[place], slots[place + 1]
    middle = coefs[0] + coefs[1] * enter + coefs[2] * leave
    low = lax.rem(me, 2) == 0
    flows[0] = jnp.where(low, enter, middle)
    flows[1] = jnp.where(low, middle, leave)
    for g in range(GROUPS):
        parts = []
        for z in range(2 * g, 2 * g + 2):
            rows = pl.ds(z * BX, BX)
            parts.append(
                d[rows, :]
                + wf[rows, :] * flows[0, pl.ds(z, 1), :]
                - wl[rows, :] * flows[1, pl.ds(z, 1), :]
            )
        v_t[pl.ds(g, BY, stride=GROUPS), :] = jnp.concatenate(parts, axis=0).T
    firsts = [jnp.zeros((GROUPS, 128), F32) for _ in range(4)]
    lasts = [jnp.zeros((GROUPS, 128), F32) for _ in range(4)]
    for j in range(BY):
        row = y_row(v_t, j)
        firsts[j % 4] = firsts[j % 4] + yf[j] * row
        lasts[j % 4] = lasts[j % 4] + yl[j] * row
    first = (firsts[0] + firsts[1]) + (firsts[2] + firsts[3])
    last = (lasts[0] + lasts[1]) + (lasts[2] + lasts[3])
    for p in range(send.shape[0]):
        send[p, 0:3] = my[...]
        send[p, 3] = first
        send[p, 4] = last


def y_local_kernel(v_t, ky_t, st_hbm, g_t, st, f, u, sem):
    move = pltpu.make_async_copy(st_hbm, st, sem)
    move.start()
    total = y_row(v_t, 0)
    g_t[0] = total
    ahead = jnp.ones_like(total)
    low = y_row(ky_t, 0)
    for j in range(1, BY):
        high = y_row(ky_t, j)
        r = 0.5 * (low + high)
        low = high
        inv = inverse(r + ahead)
        ratio = r * inv
        ahead = 1.0 + ratio * ahead
        u[j - 1] = inv
        f[j - 1] = ratio
        total = y_row(v_t, j) + ratio * total
        g_t[j] = total
    x = total * inverse(ahead)
    g_t[BY - 1] = x
    for j in range(BY - 2, -1, -1):
        x = u[j] * g_t[j] + f[j] * x
        g_t[j] = x
    move.wait()


def y_solve_kernel(blocks, g_t, yf, yl, st, out_hbm, slots, work, out, sems):
    me = lax.axis_index("gy")
    y_flows(blocks, slots)
    enter, leave = slots[me], slots[me + 1]
    for j in range(BY):
        work[pl.ds(j * GROUPS, GROUPS), :] = 2.0 * (g_t[j] + yf[j] * enter - yl[j] * leave)
    moves = []
    for g in range(GROUPS):
        rows = pl.ds(g * 128, 128)
        out[rows, :] = st[rows, :] + work[pl.ds(g, BY, stride=GROUPS), :].T
        move = pltpu.make_async_copy(out.at[rows], out_hbm.at[rows], sems.at[g])
        move.start()
        moves.append(move)
    for move in moves:
        move.wait()


def call(kernel, outs, args, scratch=(), cost=100_000):
    vm = pl.BlockSpec(memory_space=pltpu.VMEM)
    hbm = pl.BlockSpec(memory_space=pltpu.HBM)
    return pl.pallas_call(
        kernel,
        out_shape=[
            jax.ShapeDtypeStruct(shape, F32) if far else pltpu.VMEM(shape, F32)
            for shape, far in outs
        ],
        in_specs=[hbm if far else vm for _, far in args],
        out_specs=[hbm if far else vm for _, far in outs],
        scratch_shapes=list(scratch),
        compiler_params=pltpu.CompilerParams(vmem_limit_bytes=LIMIT),
        cost_estimate=pl.CostEstimate(flops=cost, bytes_accessed=cost, transcendentals=0),
    )(*[value for value, _ in args])


def near(*values):
    return [(value, False) for value in values]


def on_device(state, kappa_x, kappa_y):
    flat = [
        pltpu.with_memory_space_constraint(a.reshape(ROWS, BY), pltpu.HBM)
        for a in (state, kappa_x, kappa_y)
    ]
    plane = (ROWS, BY)
    xs = (BX, NZ, BY)
    ys = (BY, GROUPS, 128)
    x_block = (7, NZ, BY)
    edge = (2, GROUPS, 128)
    nx, ny = lax.axis_size("gx"), lax.axis_size("gy")
    chips = nx // 2
    st, kx, ky, ky_t, mine, first, second = call(
        load_kernel,
        near(plane, plane, plane, plane, (4, GROUPS, 128), edge, edge),
        [(a, True) for a in flat],
        [pltpu.SemaphoreType.DMA((2 * CHUNKS + 1,))],
    )
    pairs = [
        (i * ny + j, i * ny + j + 2 * (j % 2) - 1 if 0 < j < ny - 1 else (i ^ 1) * ny + j)
        for i in range(nx)
        for j in range(ny)
    ]
    came2 = lax.ppermute(second, ("gx", "gy"), pairs)
    came1 = lax.ppermute(first, "gy", [(i, i ^ 1) for i in range(ny)])
    fx, ux, wf, wl, part, edges, source = call(
        x_matrix_kernel,
        near(xs, xs, plane, plane, x_block, (4, GROUPS, 128), plane),
        near(st, kx, ky),
        [pltpu.VMEM(xs, F32)],
        cost=5_000_000,
    )
    ends, flux = call(
        x_ends_kernel,
        near(x_block, edge),
        near(came2, came1, mine, part, edges),
        [pltpu.VMEM((2, NZ, BY), F32)],
    )
    other = lax.ppermute(ends, "gx", [(i, i ^ 1) for i in range(nx)])
    (d,) = call(
        x_local_kernel,
        near(plane),
        near(source, flux, st, fx, ux),
        [pltpu.VMEM(plane, F32), pltpu.VMEM(xs, F32)],
        cost=3_000_000,
    )
    chip, coefs = call(x_merge_kernel, near(x_block, (3, NZ, BY)), near(ends, other, d))
    others = [lax.ppermute(chip, "gx", [(i, i ^ (2 * k)) for i in range(nx)]) for k in range(1, chips)]
    yf, yl, my = call(
        y_matrix_kernel,
        near(ys, ys, (3, GROUPS, 128)),
        near(ky_t, came2, came1, coefs),
        [pltpu.VMEM(ys, F32)] * 3,
        cost=5_000_000,
    )
    v_t, send = call(
        y_ends_kernel,
        near(plane, (ny, 5, GROUPS, 128)),
        near(chip, *others, coefs, d, wf, wl, yf, yl, my),
        [
            pltpu.VMEM((chips,) + x_block, F32),
            pltpu.VMEM((chips + 1, NZ, BY), F32),
            pltpu.VMEM((2, NZ, BY), F32),
        ],
    )
    y_blocks = lax.all_to_all(send, "gy", 0, 0)
    g_t, st = call(
        y_local_kernel,
        near(ys, plane),
        near(v_t, ky_t) + [(flat[0], True)],
        [pltpu.VMEM(ys, F32), pltpu.VMEM(ys, F32), pltpu.SemaphoreType.DMA],
        cost=5_000_000,
    )
    (out,) = call(
        y_solve_kernel,
        [(plane, True)],
        near(y_blocks, g_t, yf, yl, st),
        [
            pltpu.VMEM((ny + 1, GROUPS, 128), F32),
            pltpu.VMEM(plane, F32),
            pltpu.VMEM(plane, F32),
            pltpu.SemaphoreType.DMA((GROUPS,)),
        ],
    )
    return out.reshape(state.shape)


def solution(mesh):
    spec = P(None, "gx", "gy")
    return jax.shard_map(
        on_device, mesh=mesh, in_specs=(spec, spec, spec), out_specs=spec, check_vma=False
    )
```

```python
import jax
import jax.numpy as jnp
from jax import lax
from jax.experimental import pallas as pl
from jax.experimental.pallas import tpu as pltpu
from jax.sharding import PartitionSpec as P

F32 = jnp.float32
NZ, BX, BY = 16, 64, 128
ROWS = NZ * BX
GROUPS = ROWS // 128
LIMIT = 8 * 1024 * 1024
CHUNKS = 1


def inverse(x):
    guess = pl.reciprocal(x, approx=True)
    return guess * (2.0 - x * guess)


def x_row(ref, i):
    return jnp.concatenate(
        [ref[pl.ds(i, 8, stride=BX), :], ref[pl.ds(8 * BX + i, 8, stride=BX), :]], axis=0
    )


def y_row(ref, j):
    return ref[pl.ds(j * GROUPS, GROUPS), :]


def place_rows(ref, i, value):
    ref[pl.ds(i, 8, stride=BX), :] = value[:8]
    ref[pl.ds(8 * BX + i, 8, stride=BX), :] = value[8:]


def merge(low, high):
    inv = inverse(2.0 * inverse(low[4] + high[3]) + low[2] + high[0])
    e = (low[6] - high[5]) * inv
    a = low[1] * inv
    b = high[1] * inv
    joined = [
        low[0] - low[1] * a,
        low[1] * b,
        high[2] - high[1] * b,
        low[3],
        high[4],
        low[5] - low[1] * e,
        high[6] + high[1] * e,
    ]
    return joined, (e, a, b)


def flows_of(count, pivot, lower, upper, gain, slots):
    half = (count + 1) // 2
    up, down = {}, {}
    for n in range(half + 1):
        i = n
        if i < half:
            gain_i, pivot_i = gain(i), pivot(i)
            if i:
                gain_i = gain_i + lower(i) * up[i - 1][0]
                pivot_i = pivot_i - lower(i) * up[i - 1][1]
            inv = inverse(pivot_i)
            up[i] = gain_i * inv, upper(i) * inv
        i = count - n
        if i > half:
            gain_i, pivot_i = gain(i), pivot(i)
            if n:
                gain_i = gain_i + upper(i) * down[i + 1][0]
                pivot_i = pivot_i - upper(i) * down[i + 1][1]
            inv = inverse(pivot_i)
            down[i] = gain_i * inv, lower(i) * inv
    below, above = up[half - 1], down[half + 1]
    low, high = lower(half), upper(half)
    flow = (gain(half) + low * below[0] + high * above[0]) * inverse(
        pivot(half) - low * below[1] - high * above[1]
    )
    slots[half] = flow
    rising = flow
    for n in range(1, half + 1):
        if half - n >= 0:
            flow = up[half - n][0] + up[half - n][1] * flow
            slots[half - n] = flow
        if half + n <= count:
            rising = down[half + n][0] + down[half + n][1] * rising
            slots[half + n] = rising


def x_flows(own, others, place, blocks, slots):
    count = blocks.shape[0]
    blocks[place] = own[...]
    for k, other in enumerate(others):
        blocks[place ^ (k + 1)] = other

    def pivot(i):
        if i == 0:
            return 2.0 * inverse(blocks[0, 3]) + blocks[0, 0]
        if i == count:
            return 2.0 * inverse(blocks[count - 1, 4]) + blocks[count - 1, 2]
        return 2.0 * inverse(blocks[i - 1, 4] + blocks[i, 3]) + blocks[i - 1, 2] + blocks[i, 0]

    def gain(i):
        if i == 0:
            return -blocks[0, 5]
        return blocks[i - 1, 6] - blocks[i, 5] if i < count else blocks[i - 1, 6]

    flows_of(count, pivot, lambda i: blocks[i - 1, 1], lambda i: blocks[i, 1], gain, slots)


def y_flows(blocks, slots):
    count = blocks.shape[0]

    def pivot(i):
        if i == 0:
            return blocks[0, 0]
        return blocks[i - 1, 2] + blocks[i, 0] if i < count else blocks[i - 1, 2]

    def gain(i):
        if i == 0:
            return -blocks[0, 3]
        return blocks[i - 1, 4] - blocks[i, 3] if i < count else blocks[i - 1, 4]

    flows_of(count, pivot, lambda i: blocks[i - 1, 1], lambda i: blocks[i, 1], gain, slots)


def edge_columns(a, b, turned):
    lane = lax.broadcasted_iota(jnp.int32, (1, 128), 1)
    packed = jnp.zeros((128, 128), F32)
    for g in range(GROUPS):
        rows = pl.ds(g * 128, 128)
        of_a = (lane == 4 * g) | (lane == 4 * g + 1)
        of_b = (lane == 4 * g + 2) | (lane == 4 * g + 3)
        packed = jnp.where(of_a, pltpu.roll(a[rows, :], 4 * g + 1, 1), packed)
        packed = jnp.where(of_b, pltpu.roll(b[rows, :], 4 * g + 3, 1), packed)
    turned[...] = packed.T
    return [turned[pl.ds(n, GROUPS, stride=4), :] for n in range(4)]


def load_kernel(st_hbm, kx_hbm, ky_hbm, st, kx, ky, mine, first, second, turned, sems):
    chunk = ROWS // CHUNKS
    waits = []
    for c in range(CHUNKS):
        rows = pl.ds(c * chunk, chunk)
        waits.append(
            [
                pltpu.make_async_copy(src.at[rows], dst.at[rows], sems.at[2 * c + n])
                for n, (src, dst) in enumerate(((ky_hbm, ky), (st_hbm, st)))
            ]
        )
        for move in waits[-1]:
            move.start()
    rest = pltpu.make_async_copy(kx_hbm, kx, sems.at[2 * CHUNKS])
    rest.start()
    for moves in waits:
        for move in moves:
            move.wait()
    mine[2], mine[0], mine[3], mine[1] = edge_columns(st, ky, turned)
    even = lax.rem(lax.axis_index("gy"), 2) == 0
    low, high = mine[0:2], mine[2:4]
    first[...] = jnp.where(even, high, low)
    second[...] = jnp.where(even, low, high)
    rest.wait()


def sweep(count, row, f, u, ratios, put_first, put_last):
    ahead = jnp.ones_like(row(0))
    back = jnp.ones_like(ahead)
    low, high = row(0), row(count - 1)
    for i in range(count - 1):
        nxt = row(i + 1)
        r = 0.5 * (low + nxt)
        low = nxt
        inv = inverse(r + ahead)
        ratio = r * inv
        ahead = 1.0 + ratio * ahead
        u[i] = inv
        f[i] = ratio
        j = count - 1 - i
        prev = row(j - 1)
        r = 0.5 * (high + prev)
        high = prev
        ratio = r * inverse(r + back)
        back = 1.0 + ratio * back
        ratios[j] = ratio
    start = inverse(back)
    end = inverse(ahead)
    lead, trail = start, end
    put_first(0, start)
    put_last(count - 1, end)
    u[count - 1] = end
    f[count - 1] = jnp.zeros_like(end)
    for i in range(1, count):
        start = start * ratios[i]
        put_first(i, start)
        j = count - 1 - i
        end = end * f[j]
        put_last(j, end)
    return lead, end, trail


def x_matrix_kernel(st, kx, ky, fx, ux, wf, wl, part, edges, source, ratios, turned):
    lane = lax.broadcasted_iota(jnp.int32, (128, 128), 1)
    for g in range(GROUPS):
        rows = pl.ds(g * 128, 128)
        s = st[rows, :]
        k = ky[rows, :]
        flux = 0.5 * (k + pltpu.roll(k, 127, 1)) * (pltpu.roll(s, 127, 1) - s)
        flux = jnp.where(lane == 127, 0.0, flux)
        source[rows, :] = s + flux - pltpu.roll(flux, 1, 1)
    sums = [[jnp.zeros((NZ, BY), F32) for _ in range(2)] for _ in range(2)]

    def put(ref, total):
        def store(i, value):
            place_rows(ref, i, value)
            total[i % 2] = total[i % 2] + value * x_row(source, i)

        return store

    values = sweep(BX, lambda i: x_row(kx, i), fx, ux, ratios, put(wf, sums[0]), put(wl, sums[1]))
    values += (x_row(kx, 0), x_row(kx, BX - 1), sums[0][0] + sums[0][1], sums[1][0] + sums[1][1])
    for n, value in enumerate(values):
        part[n] = value
    edges[1], edges[0], edges[3], edges[2] = edge_columns(wf, wl, turned)


def y_matrix_kernel(ky, after, ky_t, yf, yl, my, f, u, ratios):
    for g in range(GROUPS):
        ky_t[pl.ds(g, BY, stride=GROUPS), :] = ky[pl.ds(g * 128, 128), :].T

    def put(ref):
        def store(j, value):
            ref[j] = value

        return store

    me = lax.axis_index("gy")
    last = lax.axis_size("gy") - 1
    lead, across, trail = sweep(BY, lambda j: y_row(ky_t, j), f, u, ratios, put(yf), put(yl))
    my[0] = lead
    my[1] = across
    my[2] = trail + jnp.where(me == last, 2.0 * inverse(y_row(ky_t, BY - 1)), 0.0)


def x_ends_kernel(came2, came1, mine, part, edges, send, flux, rows):
    me = lax.axis_index("gy")
    even = lax.rem(me, 2) == 0
    below = jnp.where(me == 0, 0.0, jnp.where(even, came2[...], came1[...]))
    above = jnp.where(me == lax.axis_size("gy") - 1, 0.0, jnp.where(even, came1[...], came2[...]))
    enter = 0.5 * (below[1] + mine[1]) * (mine[0] - below[0])
    leave = 0.5 * (above[1] + mine[3]) * (above[0] - mine[2])
    flux[0] = enter
    flux[1] = leave
    flux[2] = 2.0 * inverse(below[1] + mine[1])
    lane = lax.broadcasted_iota(jnp.int32, (GROUPS, 128), 1)
    send[0:5] = part[0:5]
    for n in range(2):
        low = -edges[2 * n] * enter
        high = edges[2 * n + 1] * leave
        for h in range(2):
            inside = lane // BX == h
            at_low = jnp.sum(jnp.where(inside, low, 0.0), axis=1, keepdims=True)
            at_high = jnp.sum(jnp.where(inside, high, 0.0), axis=1, keepdims=True)
            value = jnp.where(lane == 0, at_low, jnp.where(lane == 127, at_high, 0.0))
            rows[n, pl.ds(h, GROUPS, stride=2), :] = value
        send[5 + n] = part[5 + n] + rows[n]


def x_local_kernel(source, flux, st, fx, ux, d, s, work):
    both = jnp.concatenate([flux[0], flux[1]], axis=0)
    turned = jnp.concatenate([both] * 8, axis=0).T
    lane = lax.broadcasted_iota(jnp.int32, (128, 128), 1)
    for g in range(GROUPS):
        rows = pl.ds(g * 128, 128)
        left = jnp.broadcast_to(turned[:, g : g + 1], (128, 128))
        right = jnp.broadcast_to(turned[:, 8 + g : 9 + g], (128, 128))
        extra = jnp.where(lane == 0, -left, jnp.where(lane == 127, right, 0.0))
        s[rows, :] = source[rows, :] + extra
    total = x_row(s, 0)
    work[0] = total
    for i in range(1, BX):
        total = x_row(s, i) + fx[i - 1] * total
        work[i] = total
    x = jnp.zeros_like(total)
    for i in range(BX - 1, -1, -1):
        x = ux[i] * work[i] + fx[i] * x
        place_rows(d, i, x - x_row(st, i))


def x_merge_kernel(own, other, after, send, coefs):
    core = lax.rem(lax.axis_index("gx"), 2)
    mine, theirs = [own[n] for n in range(7)], [other[n] for n in range(7)]
    low = [jnp.where(core == 0, a, b) for a, b in zip(mine, theirs)]
    high = [jnp.where(core == 0, b, a) for a, b in zip(mine, theirs)]
    joined, flow = merge(low, high)
    for n in range(7):
        send[n] = joined[n]
    for n in range(3):
        coefs[n] = flow[n]


def relay_kernel(value, after, out):
    out[...] = value[...]


def y_ends_kernel(
    own, far, near, shared, coefs, d, wf, wl, yf, yl, my, flux, v_t, send, blocks, slots, flows
):
    me = lax.axis_index("gx")
    place = lax.div(me, 2)
    on_low = lax.rem(me, 2) == 0
    second = jnp.where(on_low, shared[...], far[...])
    third = jnp.where(on_low, far[...], shared[...])
    x_flows(own, (near[...], second, third), place, blocks, slots)
    enter, leave = slots[place], slots[place + 1]
    middle = coefs[0] + coefs[1] * enter + coefs[2] * leave
    flows[0] = jnp.where(on_low, enter, middle)
    flows[1] = jnp.where(on_low, middle, leave)
    for g in range(GROUPS):
        parts = []
        for z in range(2 * g, 2 * g + 2):
            rows = pl.ds(z * BX, BX)
            parts.append(
                d[rows, :]
                + wf[rows, :] * flows[0, pl.ds(z, 1), :]
                - wl[rows, :] * flows[1, pl.ds(z, 1), :]
            )
        v_t[pl.ds(g, BY, stride=GROUPS), :] = jnp.concatenate(parts, axis=0).T
    firsts = [jnp.zeros((GROUPS, 128), F32) for _ in range(4)]
    lasts = [jnp.zeros((GROUPS, 128), F32) for _ in range(4)]
    for j in range(BY):
        row = y_row(v_t, j)
        firsts[j % 4] = firsts[j % 4] + yf[j] * row
        lasts[j % 4] = lasts[j % 4] + yl[j] * row
    first = (firsts[0] + firsts[1]) + (firsts[2] + firsts[3])
    last = (lasts[0] + lasts[1]) + (lasts[2] + lasts[3])
    lead = my[0] + flux[2]
    for p in range(send.shape[0]):
        send[p, 0] = lead
        send[p, 1:3] = my[1:3]
        send[p, 3] = first
        send[p, 4] = last


def y_local_kernel(v_t, ky_t, st_hbm, g_t, st, f, u, sem):
    move = pltpu.make_async_copy(st_hbm, st, sem)
    move.start()
    total = y_row(v_t, 0)
    g_t[0] = total
    ahead = jnp.ones_like(total)
    low = y_row(ky_t, 0)
    for j in range(1, BY):
        high = y_row(ky_t, j)
        r = 0.5 * (low + high)
        low = high
        inv = inverse(r + ahead)
        ratio = r * inv
        ahead = 1.0 + ratio * ahead
        u[j - 1] = inv
        f[j - 1] = ratio
        total = y_row(v_t, j) + ratio * total
        g_t[j] = total
    x = total * inverse(ahead)
    g_t[BY - 1] = x
    for j in range(BY - 2, -1, -1):
        x = u[j] * g_t[j] + f[j] * x
        g_t[j] = x
    move.wait()


def y_solve_kernel(blocks, g_t, yf, yl, st, out_hbm, slots, work, out, sems):
    me = lax.axis_index("gy")
    y_flows(blocks, slots)
    enter, leave = slots[me], slots[me + 1]
    for j in range(BY):
        work[pl.ds(j * GROUPS, GROUPS), :] = 2.0 * (g_t[j] + yf[j] * enter - yl[j] * leave)
    moves = []
    for g in range(GROUPS):
        rows = pl.ds(g * 128, 128)
        out[rows, :] = st[rows, :] + work[pl.ds(g, BY, stride=GROUPS), :].T
        move = pltpu.make_async_copy(out.at[rows], out_hbm.at[rows], sems.at[g])
        move.start()
        moves.append(move)
    for move in moves:
        move.wait()


def call(kernel, outs, args, scratch=(), cost=100_000):
    vm = pl.BlockSpec(memory_space=pltpu.VMEM)
    hbm = pl.BlockSpec(memory_space=pltpu.HBM)
    return pl.pallas_call(
        kernel,
        out_shape=[
            jax.ShapeDtypeStruct(shape, F32) if far else pltpu.VMEM(shape, F32)
            for shape, far in outs
        ],
        in_specs=[hbm if far else vm for _, far in args],
        out_specs=[hbm if far else vm for _, far in outs],
        scratch_shapes=list(scratch),
        compiler_params=pltpu.CompilerParams(vmem_limit_bytes=LIMIT),
        cost_estimate=pl.CostEstimate(flops=cost, bytes_accessed=cost, transcendentals=0),
    )(*[value for value, _ in args])


def near(*values):
    return [(value, False) for value in values]


def on_device(state, kappa_x, kappa_y):
    flat = [
        pltpu.with_memory_space_constraint(a.reshape(ROWS, BY), pltpu.HBM)
        for a in (state, kappa_x, kappa_y)
    ]
    plane = (ROWS, BY)
    xs = (BX, NZ, BY)
    ys = (BY, GROUPS, 128)
    x_block = (7, NZ, BY)
    edge = (2, GROUPS, 128)
    nx, ny = lax.axis_size("gx"), lax.axis_size("gy")
    chips = nx // 2
    st, kx, ky, mine, first, second = call(
        load_kernel,
        near(plane, plane, plane, (4, GROUPS, 128), edge, edge),
        [(a, True) for a in flat],
        [pltpu.VMEM((128, 128), F32), pltpu.SemaphoreType.DMA((2 * CHUNKS + 1,))],
    )
    pairs = [
        (i * ny + j, i * ny + j + 2 * (j % 2) - 1 if 0 < j < ny - 1 else (i ^ 1) * ny + j)
        for i in range(nx)
        for j in range(ny)
    ]
    came2 = lax.ppermute(second, ("gx", "gy"), pairs)
    came1 = lax.ppermute(first, "gy", [(i, i ^ 1) for i in range(ny)])
    fx, ux, wf, wl, part, edges, source = call(
        x_matrix_kernel,
        near(xs, xs, plane, plane, x_block, (4, GROUPS, 128), plane),
        near(st, kx, ky),
        [pltpu.VMEM(xs, F32), pltpu.VMEM((128, 128), F32)],
        cost=5_000_000,
    )
    ends, flux = call(
        x_ends_kernel,
        near(x_block, (3, GROUPS, 128)),
        near(came2, came1, mine, part, edges),
        [pltpu.VMEM((2, NZ, BY), F32)],
    )
    other = lax.ppermute(ends, "gx", [(i, i ^ 1) for i in range(nx)])
    (d,) = call(
        x_local_kernel,
        near(plane),
        near(source, flux, st, fx, ux),
        [pltpu.VMEM(plane, F32), pltpu.VMEM(xs, F32)],
        cost=3_000_000,
    )
    chip, coefs = call(x_merge_kernel, near(x_block, (3, NZ, BY)), near(ends, other, d))
    away = [lax.ppermute(chip, "gx", [(i, i ^ (6 - 2 * (i % 2))) for i in range(nx)])]
    away.append(lax.ppermute(chip, "gx", [(i, i ^ 2) for i in range(nx)]))
    ky_t, yf, yl, my = call(
        y_matrix_kernel,
        near(plane, ys, ys, (3, GROUPS, 128)),
        near(ky, coefs),
        [pltpu.VMEM(ys, F32)] * 3,
        cost=5_000_000,
    )
    (relayed,) = call(relay_kernel, near(x_block), near(away[0], my))
    away.append(lax.ppermute(relayed, "gx", [(i, i ^ 1) for i in range(nx)]))
    v_t, send = call(
        y_ends_kernel,
        near(plane, (ny, 5, GROUPS, 128)),
        near(chip, *away, coefs, d, wf, wl, yf, yl, my, flux),
        [
            pltpu.VMEM((chips,) + x_block, F32),
            pltpu.VMEM((chips + 1, NZ, BY), F32),
            pltpu.VMEM((2, NZ, BY), F32),
        ],
    )
    y_blocks = lax.all_to_all(send, "gy", 0, 0)
    g_t, st = call(
        y_local_kernel,
        near(ys, plane),
        near(v_t, ky_t) + [(flat[0], True)],
        [pltpu.VMEM(ys, F32), pltpu.VMEM(ys, F32), pltpu.SemaphoreType.DMA],
        cost=5_000_000,
    )
    (out,) = call(
        y_solve_kernel,
        [(plane, True)],
        near(y_blocks, g_t, yf, yl, st),
        [
            pltpu.VMEM((ny + 1, GROUPS, 128), F32),
            pltpu.VMEM(plane, F32),
            pltpu.VMEM(plane, F32),
            pltpu.SemaphoreType.DMA((GROUPS,)),
        ],
    )
    return out.reshape(state.shape)


def solution(mesh):
    spec = P(None, "gx", "gy")
    return jax.shard_map(
        on_device, mesh=mesh, in_specs=(spec, spec, spec), out_specs=spec, check_vma=False
    )
```

```python
import jax
import jax.numpy as jnp
from jax import lax
from jax.experimental import pallas as pl
from jax.experimental.pallas import tpu as pltpu
from jax.sharding import PartitionSpec as P

F32 = jnp.float32
NZ, BX, BY = 16, 64, 128
ROWS = NZ * BX
GROUPS = ROWS // 128
LIMIT = 8 * 1024 * 1024
PITCH = 72


def x_row(ref, i):
    return jnp.concatenate(
        [ref[pl.ds(i, 8, stride=PITCH), :], ref[pl.ds(8 * PITCH + i, 8, stride=PITCH), :]], axis=0
    )


def y_row(ref, j):
    return ref[pl.ds(j * GROUPS, GROUPS), :]


def place_rows(ref, i, value):
    ref[pl.ds(i, 8, stride=PITCH), :] = value[:8]
    ref[pl.ds(8 * PITCH + i, 8, stride=PITCH), :] = value[8:]


def group(ref, g):
    return jnp.concatenate([ref[pl.ds(z * PITCH, BX), :] for z in (2 * g, 2 * g + 1)], axis=0)


def place_group(ref, g, value):
    ref[pl.ds(2 * g * PITCH, BX), :] = value[:BX]
    ref[pl.ds((2 * g + 1) * PITCH, BX), :] = value[BX:]


def merge(low, high):
    inv = (1.0 / ((2.0 / (low[4] + high[3])) + low[2] + high[0]))
    e = (low[6] - high[5]) * inv
    a = low[1] * inv
    b = high[1] * inv
    joined = [
        low[0] - low[1] * a,
        low[1] * b,
        high[2] - high[1] * b,
        low[3],
        high[4],
        low[5] - low[1] * e,
        high[6] + high[1] * e,
    ]
    return joined, (e, a, b)


def flows_of(count, pivot, lower, upper, gain, slots):
    half = (count + 1) // 2
    up, down = {}, {}
    for n in range(half + 1):
        i = n
        if i < half:
            gain_i, pivot_i = gain(i), pivot(i)
            if i:
                gain_i = gain_i + lower(i) * up[i - 1][0]
                pivot_i = pivot_i - lower(i) * up[i - 1][1]
            inv = (1.0 / (pivot_i))
            up[i] = gain_i * inv, upper(i) * inv
        i = count - n
        if i > half:
            gain_i, pivot_i = gain(i), pivot(i)
            if n:
                gain_i = gain_i + upper(i) * down[i + 1][0]
                pivot_i = pivot_i - upper(i) * down[i + 1][1]
            inv = (1.0 / (pivot_i))
            down[i] = gain_i * inv, lower(i) * inv
    below, above = up[half - 1], down[half + 1]
    low, high = lower(half), upper(half)
    flow = (gain(half) + low * below[0] + high * above[0]) * (1.0 / (
        pivot(half) - low * below[1] - high * above[1]
    ))
    slots[half] = flow
    rising = flow
    for n in range(1, half + 1):
        if half - n >= 0:
            flow = up[half - n][0] + up[half - n][1] * flow
            slots[half - n] = flow
        if half + n <= count:
            rising = down[half + n][0] + down[half + n][1] * rising
            slots[half + n] = rising


def x_flows(own, others, place, blocks, slots):
    count = blocks.shape[0]
    blocks[place] = own[...]
    for k, other in enumerate(others):
        blocks[place ^ (k + 1)] = other

    def pivot(i):
        if i == 0:
            return (2.0 / (blocks[0, 3])) + blocks[0, 0]
        if i == count:
            return (2.0 / (blocks[count - 1, 4])) + blocks[count - 1, 2]
        return (2.0 / (blocks[i - 1, 4] + blocks[i, 3])) + blocks[i - 1, 2] + blocks[i, 0]

    def gain(i):
        if i == 0:
            return -blocks[0, 5]
        return blocks[i - 1, 6] - blocks[i, 5] if i < count else blocks[i - 1, 6]

    flows_of(count, pivot, lambda i: blocks[i - 1, 1], lambda i: blocks[i, 1], gain, slots)


def y_flows(blocks, slots):
    count = blocks.shape[0]

    def pivot(i):
        if i == 0:
            return blocks[0, 0]
        return blocks[i - 1, 2] + blocks[i, 0] if i < count else blocks[i - 1, 2]

    def gain(i):
        if i == 0:
            return -blocks[0, 3]
        return blocks[i - 1, 4] - blocks[i, 3] if i < count else blocks[i - 1, 4]

    flows_of(count, pivot, lambda i: blocks[i - 1, 1], lambda i: blocks[i, 1], gain, slots)


def load_kernel(st_hbm, kx_hbm, ky_hbm, st, kx, st_t, ky_t, mine, first, second, ky, sems):
    inside = pl.ds(0, BX)
    moves = [
        pltpu.make_async_copy(src, dst, sems.at[n])
        for n, (src, dst) in enumerate(
            ((ky_hbm, ky), (st_hbm, st.at[:, inside, :]), (kx_hbm, kx.at[:, inside, :]))
        )
    ]
    for move in moves:
        move.start()
    moves[0].wait()
    for g in range(GROUPS):
        pair = jnp.concatenate([ky[2 * g], ky[2 * g + 1]], axis=0)
        ky_t[pl.ds(g, BY, stride=GROUPS), :] = pair.T
    moves[1].wait()
    for g in range(GROUPS):
        pair = jnp.concatenate([st[2 * g, inside, :], st[2 * g + 1, inside, :]], axis=0)
        st_t[pl.ds(g, BY, stride=GROUPS), :] = pair.T
    for n, ref in enumerate((st_t, ky_t)):
        mine[n] = y_row(ref, 0)
        mine[2 + n] = y_row(ref, BY - 1)
    even = lax.rem(lax.axis_index("gy"), 2) == 0
    low, high = mine[0:2], mine[2:4]
    first[...] = jnp.where(even, high, low)
    second[...] = jnp.where(even, low, high)
    moves[2].wait()


def sweep(count, row, f, u, ratios, put_first, put_last):
    ahead = jnp.ones_like(row(0))
    back = jnp.ones_like(ahead)
    low, high = row(0), row(count - 1)
    for i in range(count - 1):
        nxt = row(i + 1)
        r = 0.5 * (low + nxt)
        low = nxt
        inv = (1.0 / (r + ahead))
        ratio = r * inv
        ahead = 1.0 + ratio * ahead
        u[i] = inv
        f[i] = ratio
        j = count - 1 - i
        prev = row(j - 1)
        r = 0.5 * (high + prev)
        high = prev
        ratio = r * (1.0 / (r + back))
        back = 1.0 + ratio * back
        ratios[j] = ratio
    start = (1.0 / (back))
    end = (1.0 / (ahead))
    lead, trail = start, end
    put_first(0, start)
    put_last(count - 1, end)
    u[count - 1] = end
    f[count - 1] = jnp.zeros_like(end)
    for i in range(1, count):
        start = start * ratios[i]
        put_first(i, start)
        j = count - 1 - i
        end = end * f[j]
        put_last(j, end)
    return lead, end, trail


def x_matrix_kernel(st_t, kx, ky_t, fx, ux, wf, wl, part, edges, base_t, source, ratios):
    here, k_here = y_row(st_t, 0), y_row(ky_t, 0)
    value = here
    for j in range(BY):
        if j < BY - 1:
            after, k_after = y_row(st_t, j + 1), y_row(ky_t, j + 1)
            flux = 0.5 * (k_here + k_after) * (after - here)
            value = value + flux
        base_t[pl.ds(j * GROUPS, GROUPS), :] = value
        here, k_here, value = after, k_after, after - flux
    for g in range(GROUPS):
        place_group(source, g, base_t[pl.ds(g, BY, stride=GROUPS), :].T)
    sums = [[jnp.zeros((NZ, BY), F32) for _ in range(2)] for _ in range(2)]

    def put(ref, total):
        def store(i, value):
            place_rows(ref, i, value)
            total[i % 2] = total[i % 2] + value * x_row(source, i)

        return store

    values = sweep(BX, lambda i: x_row(kx, i), fx, ux, ratios, put(wf, sums[0]), put(wl, sums[1]))
    values += (x_row(kx, 0), x_row(kx, BX - 1), sums[0][0] + sums[0][1], sums[1][0] + sums[1][1])
    for n, value in enumerate(values):
        part[n] = value
    for n, ref in enumerate((wf, wl)):
        for g in range(GROUPS):
            turned = group(ref, g).T
            edges[2 * n, pl.ds(g, 1), :] = turned[0:1, :]
            edges[2 * n + 1, pl.ds(g, 1), :] = turned[127:128, :]


def y_matrix_kernel(ky_t, after, yf, yl, my, f, u, ratios):
    def put(ref):
        def store(j, value):
            ref[j] = value

        return store

    me = lax.axis_index("gy")
    last = lax.axis_size("gy") - 1
    lead, across, trail = sweep(BY, lambda j: y_row(ky_t, j), f, u, ratios, put(yf), put(yl))
    my[0] = lead
    my[1] = across
    my[2] = trail + jnp.where(me == last, (2.0 / (y_row(ky_t, BY - 1))), 0.0)


def x_ends_kernel(came2, came1, mine, part, edges, send, flux, rows):
    me = lax.axis_index("gy")
    even = lax.rem(me, 2) == 0
    below = jnp.where(me == 0, 0.0, jnp.where(even, came2[...], came1[...]))
    above = jnp.where(me == lax.axis_size("gy") - 1, 0.0, jnp.where(even, came1[...], came2[...]))
    enter = 0.5 * (below[1] + mine[1]) * (mine[0] - below[0])
    leave = 0.5 * (above[1] + mine[3]) * (above[0] - mine[2])
    flux[0] = enter
    flux[1] = leave
    flux[2] = (2.0 / (below[1] + mine[1]))
    lane = lax.broadcasted_iota(jnp.int32, (GROUPS, 128), 1)
    send[0:5] = part[0:5]
    for n in range(2):
        low = -edges[2 * n] * enter
        high = edges[2 * n + 1] * leave
        for h in range(2):
            inside = lane // BX == h
            at_low = jnp.sum(jnp.where(inside, low, 0.0), axis=1, keepdims=True)
            at_high = jnp.sum(jnp.where(inside, high, 0.0), axis=1, keepdims=True)
            value = jnp.where(lane == 0, at_low, jnp.where(lane == 127, at_high, 0.0))
            rows[n, pl.ds(h, GROUPS, stride=2), :] = value
        send[5 + n] = part[5 + n] + rows[n]


def x_local_kernel(base_t, flux, st, fx, ux, d, s, work, work_t):
    work_t[...] = base_t[...]
    work_t[pl.ds(0, GROUPS), :] = y_row(base_t, 0) - flux[0]
    work_t[pl.ds((BY - 1) * GROUPS, GROUPS), :] = y_row(base_t, BY - 1) + flux[1]
    for g in range(GROUPS):
        place_group(s, g, work_t[pl.ds(g, BY, stride=GROUPS), :].T)
    total = x_row(s, 0)
    work[0] = total
    for i in range(1, BX):
        total = x_row(s, i) + fx[i - 1] * total
        work[i] = total
    x = jnp.zeros_like(total)
    for i in range(BX - 1, -1, -1):
        x = ux[i] * work[i] + fx[i] * x
        place_rows(d, i, x - x_row(st, i))


def x_merge_kernel(own, other, after, send, coefs):
    core = lax.rem(lax.axis_index("gx"), 2)
    mine, theirs = [own[n] for n in range(7)], [other[n] for n in range(7)]
    low = [jnp.where(core == 0, a, b) for a, b in zip(mine, theirs)]
    high = [jnp.where(core == 0, b, a) for a, b in zip(mine, theirs)]
    joined, flow = merge(low, high)
    for n in range(7):
        send[n] = joined[n]
    for n in range(3):
        coefs[n] = flow[n]


def relay_kernel(value, after, out):
    out[...] = value[...]


def y_ends_kernel(
    own, far, near, shared, coefs, d, wf, wl, yf, yl, my, flux, v_t, send, blocks, slots, flows
):
    me = lax.axis_index("gx")
    place = lax.div(me, 2)
    on_low = lax.rem(me, 2) == 0
    second = jnp.where(on_low, shared[...], far[...])
    third = jnp.where(on_low, far[...], shared[...])
    x_flows(own, (near[...], second, third), place, blocks, slots)
    enter, leave = slots[place], slots[place + 1]
    middle = coefs[0] + coefs[1] * enter + coefs[2] * leave
    flows[0] = jnp.where(on_low, enter, middle)
    flows[1] = jnp.where(on_low, middle, leave)
    for g in range(GROUPS):
        parts = []
        for z in range(2 * g, 2 * g + 2):
            rows = pl.ds(z * PITCH, BX)
            parts.append(
                d[rows, :]
                + wf[rows, :] * flows[0, pl.ds(z, 1), :]
                - wl[rows, :] * flows[1, pl.ds(z, 1), :]
            )
        v_t[pl.ds(g, BY, stride=GROUPS), :] = jnp.concatenate(parts, axis=0).T
    firsts = [jnp.zeros((GROUPS, 128), F32) for _ in range(4)]
    lasts = [jnp.zeros((GROUPS, 128), F32) for _ in range(4)]
    for j in range(BY):
        row = y_row(v_t, j)
        firsts[j % 4] = firsts[j % 4] + yf[j] * row
        lasts[j % 4] = lasts[j % 4] + yl[j] * row
    first = (firsts[0] + firsts[1]) + (firsts[2] + firsts[3])
    last = (lasts[0] + lasts[1]) + (lasts[2] + lasts[3])
    lead = my[0] + flux[2]
    for p in range(send.shape[0]):
        send[p, 0] = lead
        send[p, 1:3] = my[1:3]
        send[p, 3] = first
        send[p, 4] = last


def y_local_kernel(v_t, ky_t, st_hbm, g_t, st, f, u, sem):
    move = pltpu.make_async_copy(st_hbm, st, sem)
    move.start()
    total = y_row(v_t, 0)
    g_t[0] = total
    ahead = jnp.ones_like(total)
    low = y_row(ky_t, 0)
    for j in range(1, BY):
        high = y_row(ky_t, j)
        r = 0.5 * (low + high)
        low = high
        inv = (1.0 / (r + ahead))
        ratio = r * inv
        ahead = 1.0 + ratio * ahead
        u[j - 1] = inv
        f[j - 1] = ratio
        total = y_row(v_t, j) + ratio * total
        g_t[j] = total
    x = total / ahead
    g_t[BY - 1] = x
    for j in range(BY - 2, -1, -1):
        x = u[j] * g_t[j] + f[j] * x
        g_t[j] = x
    move.wait()


def y_solve_kernel(blocks, g_t, yf, yl, st, out_hbm, slots, work, out, sems):
    me = lax.axis_index("gy")
    y_flows(blocks, slots)
    enter, leave = slots[me], slots[me + 1]
    for j in range(BY):
        work[pl.ds(j * GROUPS, GROUPS), :] = 2.0 * (g_t[j] + yf[j] * enter - yl[j] * leave)
    moves = []
    for g in range(GROUPS):
        rows = pl.ds(g * 128, 128)
        out[rows, :] = st[rows, :] + work[pl.ds(g, BY, stride=GROUPS), :].T
        move = pltpu.make_async_copy(out.at[rows], out_hbm.at[rows], sems.at[g])
        move.start()
        moves.append(move)
    for move in moves:
        move.wait()


def call(kernel, outs, args, scratch=(), cost=100_000):
    vm = pl.BlockSpec(memory_space=pltpu.VMEM)
    hbm = pl.BlockSpec(memory_space=pltpu.HBM)
    return pl.pallas_call(
        kernel,
        out_shape=[
            jax.ShapeDtypeStruct(shape, F32) if far else pltpu.VMEM(shape, F32)
            for shape, far in outs
        ],
        in_specs=[hbm if far else vm for _, far in args],
        out_specs=[hbm if far else vm for _, far in outs],
        scratch_shapes=list(scratch),
        compiler_params=pltpu.CompilerParams(vmem_limit_bytes=LIMIT),
        cost_estimate=pl.CostEstimate(flops=cost, bytes_accessed=cost, transcendentals=0),
    )(*[value for value, _ in args])


def near(*values):
    return [(value, False) for value in values]


def on_device(state, kappa_x, kappa_y):
    flat = [
        pltpu.with_memory_space_constraint(a, pltpu.HBM) for a in (state, kappa_x, kappa_y)
    ]
    plane = (ROWS, BY)
    pitched = (NZ * PITCH, BY)
    planes = (NZ, PITCH, BY)
    xs = (BX, NZ, BY)
    ys = (BY, GROUPS, 128)
    x_block = (7, NZ, BY)
    edge = (2, GROUPS, 128)
    nx, ny = lax.axis_size("gx"), lax.axis_size("gy")
    chips = nx // 2
    st, kx, st_t, ky_t, mine, first, second = call(
        load_kernel,
        near(planes, planes, plane, plane, (4, GROUPS, 128), edge, edge),
        [(a, True) for a in flat],
        [pltpu.VMEM((NZ, BX, BY), F32), pltpu.SemaphoreType.DMA((3,))],
    )
    st, kx = st.reshape(pitched), kx.reshape(pitched)
    pairs = [
        (i * ny + j, i * ny + j + 2 * (j % 2) - 1 if 0 < j < ny - 1 else (i ^ 1) * ny + j)
        for i in range(nx)
        for j in range(ny)
    ]
    came2 = lax.ppermute(second, ("gx", "gy"), pairs)
    came1 = lax.ppermute(first, "gy", [(i, i ^ 1) for i in range(ny)])
    fx, ux, wf, wl, part, edges, base_t = call(
        x_matrix_kernel,
        near(xs, xs, pitched, pitched, x_block, (4, GROUPS, 128), plane),
        near(st_t, kx, ky_t),
        [pltpu.VMEM(pitched, F32), pltpu.VMEM(xs, F32)],
        cost=5_000_000,
    )
    ends, flux = call(
        x_ends_kernel,
        near(x_block, (3, GROUPS, 128)),
        near(came2, came1, mine, part, edges),
        [pltpu.VMEM((2, NZ, BY), F32)],
    )
    other = lax.ppermute(ends, "gx", [(i, i ^ 1) for i in range(nx)])
    (d,) = call(
        x_local_kernel,
        near(pitched),
        near(base_t, flux, st, fx, ux),
        [pltpu.VMEM(pitched, F32), pltpu.VMEM(xs, F32), pltpu.VMEM(plane, F32)],
        cost=3_000_000,
    )
    chip, coefs = call(x_merge_kernel, near(x_block, (3, NZ, BY)), near(ends, other, d))
    away = [lax.ppermute(chip, "gx", [(i, i ^ (6 - 2 * (i % 2))) for i in range(nx)])]
    away.append(lax.ppermute(chip, "gx", [(i, i ^ 2) for i in range(nx)]))
    yf, yl, my = call(
        y_matrix_kernel,
        near(ys, ys, (3, GROUPS, 128)),
        near(ky_t, coefs),
        [pltpu.VMEM(ys, F32)] * 3,
        cost=5_000_000,
    )
    (relayed,) = call(relay_kernel, near(x_block), near(away[0], my))
    away.append(lax.ppermute(relayed, "gx", [(i, i ^ 1) for i in range(nx)]))
    v_t, send = call(
        y_ends_kernel,
        near(plane, (ny, 5, GROUPS, 128)),
        near(chip, *away, coefs, d, wf, wl, yf, yl, my, flux),
        [
            pltpu.VMEM((chips,) + x_block, F32),
            pltpu.VMEM((chips + 1, NZ, BY), F32),
            pltpu.VMEM((2, NZ, BY), F32),
        ],
    )
    y_blocks = lax.all_to_all(send, "gy", 0, 0)
    g_t, st = call(
        y_local_kernel,
        near(ys, (NZ, BX, BY)),
        near(v_t, ky_t) + [(flat[0], True)],
        [pltpu.VMEM(ys, F32), pltpu.VMEM(ys, F32), pltpu.SemaphoreType.DMA],
        cost=5_000_000,
    )
    (out,) = call(
        y_solve_kernel,
        [(plane, True)],
        near(y_blocks, g_t, yf, yl, st.reshape(plane)),
        [
            pltpu.VMEM((ny + 1, GROUPS, 128), F32),
            pltpu.VMEM(plane, F32),
            pltpu.VMEM(plane, F32),
            pltpu.SemaphoreType.DMA((GROUPS,)),
        ],
    )
    return out.reshape(state.shape)


def solution(mesh):
    spec = P(None, "gx", "gy")
    return jax.shard_map(
        on_device, mesh=mesh, in_specs=(spec, spec, spec), out_specs=spec, check_vma=False
    )
```

```python
import jax
import jax.numpy as jnp
from jax import lax
from jax.experimental import pallas as pl
from jax.experimental.pallas import tpu as pltpu
from jax.sharding import PartitionSpec as P

F32 = jnp.float32
NZ, BX, BY = 16, 64, 128
ROWS = NZ * BX
GROUPS = ROWS // 128
LIMIT = 8 * 1024 * 1024
SIDE = 4
PITCH = 72


def x_row(ref, i):
    return jnp.concatenate(
        [ref[pl.ds(i, 8, stride=PITCH), :], ref[pl.ds(8 * PITCH + i, 8, stride=PITCH), :]], axis=0
    )


def y_row(ref, j):
    return ref[pl.ds(j * GROUPS, GROUPS), :]


def place_rows(ref, i, value):
    ref[pl.ds(i, 8, stride=PITCH), :] = value[:8]
    ref[pl.ds(8 * PITCH + i, 8, stride=PITCH), :] = value[8:]


def group(ref, g):
    return jnp.concatenate([ref[pl.ds(z * PITCH, BX), :] for z in (2 * g, 2 * g + 1)], axis=0)


def place_group(ref, g, value):
    ref[pl.ds(2 * g * PITCH, BX), :] = value[:BX]
    ref[pl.ds((2 * g + 1) * PITCH, BX), :] = value[BX:]


def merge(low, high):
    inv = (1.0 / ((2.0 / (low[4] + high[3])) + low[2] + high[0]))
    e = (low[6] - high[5]) * inv
    a = low[1] * inv
    b = high[1] * inv
    joined = [
        low[0] - low[1] * a,
        low[1] * b,
        high[2] - high[1] * b,
        low[3],
        high[4],
        low[5] - low[1] * e,
        high[6] + high[1] * e,
    ]
    return joined, (e, a, b)


def flows_of(count, pivot, lower, upper, gain, slots):
    half = (count + 1) // 2
    up, down = {}, {}
    for n in range(half + 1):
        i = n
        if i < half:
            gain_i, pivot_i = gain(i), pivot(i)
            if i:
                gain_i = gain_i + lower(i) * up[i - 1][0]
                pivot_i = pivot_i - lower(i) * up[i - 1][1]
            inv = (1.0 / (pivot_i))
            up[i] = gain_i * inv, upper(i) * inv
        i = count - n
        if i > half:
            gain_i, pivot_i = gain(i), pivot(i)
            if n:
                gain_i = gain_i + upper(i) * down[i + 1][0]
                pivot_i = pivot_i - upper(i) * down[i + 1][1]
            inv = (1.0 / (pivot_i))
            down[i] = gain_i * inv, lower(i) * inv
    below, above = up[half - 1], down[half + 1]
    low, high = lower(half), upper(half)
    flow = (gain(half) + low * below[0] + high * above[0]) * (1.0 / (
        pivot(half) - low * below[1] - high * above[1]
    ))
    slots[half] = flow
    rising = flow
    for n in range(1, half + 1):
        if half - n >= 0:
            flow = up[half - n][0] + up[half - n][1] * flow
            slots[half - n] = flow
        if half + n <= count:
            rising = down[half + n][0] + down[half + n][1] * rising
            slots[half + n] = rising


def x_flows(blocks, slots):
    count = blocks.shape[0]

    def pivot(i):
        if i == 0:
            return (2.0 / (blocks[0, 3])) + blocks[0, 0]
        if i == count:
            return (2.0 / (blocks[count - 1, 4])) + blocks[count - 1, 2]
        return (2.0 / (blocks[i - 1, 4] + blocks[i, 3])) + blocks[i - 1, 2] + blocks[i, 0]

    def gain(i):
        if i == 0:
            return -blocks[0, 5]
        return blocks[i - 1, 6] - blocks[i, 5] if i < count else blocks[i - 1, 6]

    flows_of(count, pivot, lambda i: blocks[i - 1, 1], lambda i: blocks[i, 1], gain, slots)


def y_merge(low, high):
    inv = 1.0 / (low[2] + high[0])
    e = (low[4] - high[3]) * inv
    a = low[1] * inv
    b = high[1] * inv
    joined = [
        low[0] - low[1] * a,
        low[1] * b,
        high[2] - high[1] * b,
        low[3] - low[1] * e,
        high[4] + high[1] * e,
    ]
    return joined, (e, a, b)


def arrange(own, far, near, shared, place, blocks):
    on_low = lax.rem(lax.axis_index("gx"), 2) == 0
    blocks[place] = own[...]
    blocks[place ^ 1] = near[...]
    blocks[place ^ 2] = jnp.where(on_low, shared[...], far[...])
    blocks[place ^ 3] = jnp.where(on_low, far[...], shared[...])


def y_flows(blocks, slots):
    count = blocks.shape[0]

    def pivot(i):
        if i == 0:
            return blocks[0, 0]
        return blocks[i - 1, 2] + blocks[i, 0] if i < count else blocks[i - 1, 2]

    def gain(i):
        if i == 0:
            return -blocks[0, 3]
        return blocks[i - 1, 4] - blocks[i, 3] if i < count else blocks[i - 1, 4]

    flows_of(count, pivot, lambda i: blocks[i - 1, 1], lambda i: blocks[i, 1], gain, slots)


def load_kernel(st_hbm, kx_hbm, ky_hbm, st, kx, st_t, ky_t, mine, first, second, ky, sems):
    inside = pl.ds(0, BX)
    moves = [
        pltpu.make_async_copy(src, dst, sems.at[n])
        for n, (src, dst) in enumerate(
            ((ky_hbm, ky), (st_hbm, st.at[:, inside, :]), (kx_hbm, kx.at[:, inside, :]))
        )
    ]
    for move in moves:
        move.start()
    moves[0].wait()
    for g in range(GROUPS):
        pair = jnp.concatenate([ky[2 * g], ky[2 * g + 1]], axis=0)
        ky_t[pl.ds(g, BY, stride=GROUPS), :] = pair.T
    moves[1].wait()
    for g in range(GROUPS):
        pair = jnp.concatenate([st[2 * g, inside, :], st[2 * g + 1, inside, :]], axis=0)
        st_t[pl.ds(g, BY, stride=GROUPS), :] = pair.T
    for n, ref in enumerate((st_t, ky_t)):
        mine[n] = y_row(ref, 0)
        mine[2 + n] = y_row(ref, BY - 1)
    even = lax.rem(lax.axis_index("gy"), 2) == 0
    low, high = mine[0:2], mine[2:4]
    first[...] = jnp.where(even, high, low)
    second[...] = jnp.where(even, low, high)
    moves[2].wait()


def sweep(count, row, f, u, ratios, put_first, put_last):
    ahead = jnp.ones_like(row(0))
    back = jnp.ones_like(ahead)
    low, high = row(0), row(count - 1)
    for i in range(count - 1):
        nxt = row(i + 1)
        r = 0.5 * (low + nxt)
        low = nxt
        inv = (1.0 / (r + ahead))
        ratio = r * inv
        ahead = 1.0 + ratio * ahead
        u[i] = inv
        f[i] = ratio
        j = count - 1 - i
        prev = row(j - 1)
        r = 0.5 * (high + prev)
        high = prev
        ratio = r * (1.0 / (r + back))
        back = 1.0 + ratio * back
        ratios[j] = ratio
    start = (1.0 / (back))
    end = (1.0 / (ahead))
    lead, trail = start, end
    put_first(0, start)
    put_last(count - 1, end)
    u[count - 1] = end
    f[count - 1] = jnp.zeros_like(end)
    for i in range(1, count):
        start = start * ratios[i]
        put_first(i, start)
        j = count - 1 - i
        end = end * f[j]
        put_last(j, end)
    return lead, end, trail


def x_matrix_kernel(st_t, kx, ky_t, fx, ux, wf, wl, part, edges, base_t, source, ratios):
    here, k_here = y_row(st_t, 0), y_row(ky_t, 0)
    value = here
    for j in range(BY):
        if j < BY - 1:
            after, k_after = y_row(st_t, j + 1), y_row(ky_t, j + 1)
            flux = 0.5 * (k_here + k_after) * (after - here)
            value = value + flux
        base_t[pl.ds(j * GROUPS, GROUPS), :] = value
        here, k_here, value = after, k_after, after - flux
    for g in range(GROUPS):
        place_group(source, g, base_t[pl.ds(g, BY, stride=GROUPS), :].T)
    sums = [[jnp.zeros((NZ, BY), F32) for _ in range(2)] for _ in range(2)]

    def put(ref, total):
        def store(i, value):
            place_rows(ref, i, value)
            total[i % 2] = total[i % 2] + value * x_row(source, i)

        return store

    values = sweep(BX, lambda i: x_row(kx, i), fx, ux, ratios, put(wf, sums[0]), put(wl, sums[1]))
    values += (x_row(kx, 0), x_row(kx, BX - 1), sums[0][0] + sums[0][1], sums[1][0] + sums[1][1])
    for n, value in enumerate(values):
        part[n] = value
    for n, ref in enumerate((wf, wl)):
        for g in range(GROUPS):
            turned = group(ref, g).T
            edges[2 * n, pl.ds(g, 1), :] = turned[0:1, :]
            edges[2 * n + 1, pl.ds(g, 1), :] = turned[127:128, :]


def y_matrix_kernel(ky_t, after, f, u, yf, yl, my, ratios):
    def put(ref):
        def store(j, value):
            ref[j] = value

        return store

    me = lax.axis_index("gy")
    last = lax.axis_size("gy") - 1
    lead, across, trail = sweep(BY, lambda j: y_row(ky_t, j), f, u, ratios, put(yf), put(yl))
    my[0] = lead
    my[1] = across
    my[2] = trail + jnp.where(me == last, (2.0 / (y_row(ky_t, BY - 1))), 0.0)


def x_ends_kernel(came2, came1, mine, part, edges, send, flux, rows):
    me = lax.axis_index("gy")
    even = lax.rem(me, 2) == 0
    below = jnp.where(me == 0, 0.0, jnp.where(even, came2[...], came1[...]))
    above = jnp.where(me == lax.axis_size("gy") - 1, 0.0, jnp.where(even, came1[...], came2[...]))
    enter = 0.5 * (below[1] + mine[1]) * (mine[0] - below[0])
    leave = 0.5 * (above[1] + mine[3]) * (above[0] - mine[2])
    flux[0] = enter
    flux[1] = leave
    flux[2] = (2.0 / (below[1] + mine[1]))
    lane = lax.broadcasted_iota(jnp.int32, (GROUPS, 128), 1)
    send[0:5] = part[0:5]
    for n in range(2):
        low = -edges[2 * n] * enter
        high = edges[2 * n + 1] * leave
        for h in range(2):
            inside = lane // BX == h
            at_low = jnp.sum(jnp.where(inside, low, 0.0), axis=1, keepdims=True)
            at_high = jnp.sum(jnp.where(inside, high, 0.0), axis=1, keepdims=True)
            value = jnp.where(lane == 0, at_low, jnp.where(lane == 127, at_high, 0.0))
            rows[n, pl.ds(h, GROUPS, stride=2), :] = value
        send[5 + n] = part[5 + n] + rows[n]


def x_local_kernel(base_t, flux, st, fx, ux, d, s, work, work_t):
    work_t[...] = base_t[...]
    work_t[pl.ds(0, GROUPS), :] = y_row(base_t, 0) - flux[0]
    work_t[pl.ds((BY - 1) * GROUPS, GROUPS), :] = y_row(base_t, BY - 1) + flux[1]
    for g in range(GROUPS):
        place_group(s, g, work_t[pl.ds(g, BY, stride=GROUPS), :].T)
    total = x_row(s, 0)
    work[0] = total
    for i in range(1, BX):
        total = x_row(s, i) + fx[i - 1] * total
        work[i] = total
    x = jnp.zeros_like(total)
    for i in range(BX - 1, -1, -1):
        x = ux[i] * work[i] + fx[i] * x
        place_rows(d, i, x - x_row(st, i))


def x_merge_kernel(own, other, after, send, coefs):
    core = lax.rem(lax.axis_index("gx"), 2)
    mine, theirs = [own[n] for n in range(7)], [other[n] for n in range(7)]
    low = [jnp.where(core == 0, a, b) for a, b in zip(mine, theirs)]
    high = [jnp.where(core == 0, b, a) for a, b in zip(mine, theirs)]
    joined, flow = merge(low, high)
    for n in range(7):
        send[n] = joined[n]
    for n in range(3):
        coefs[n] = flow[n]


def relay_kernel(value, after, out):
    out[...] = value[...]


def y_ends_kernel(
    own, far, near, shared, coefs, d, wf, wl, yf, yl, my, flux, v_t, send, blocks, slots, flows
):
    me = lax.axis_index("gx")
    place = lax.div(me, 2)
    on_low = lax.rem(me, 2) == 0
    arrange(own, far, near, shared, place, blocks)
    x_flows(blocks, slots)
    enter, leave = slots[place], slots[place + 1]
    middle = coefs[0] + coefs[1] * enter + coefs[2] * leave
    flows[0] = jnp.where(on_low, enter, middle)
    flows[1] = jnp.where(on_low, middle, leave)
    for g in range(GROUPS):
        parts = []
        for z in range(2 * g, 2 * g + 2):
            rows = pl.ds(z * PITCH, BX)
            parts.append(
                d[rows, :]
                + wf[rows, :] * flows[0, pl.ds(z, 1), :]
                - wl[rows, :] * flows[1, pl.ds(z, 1), :]
            )
        v_t[pl.ds(g, BY, stride=GROUPS), :] = jnp.concatenate(parts, axis=0).T
    firsts = [jnp.zeros((GROUPS, 128), F32) for _ in range(4)]
    lasts = [jnp.zeros((GROUPS, 128), F32) for _ in range(4)]
    for j in range(BY):
        row = y_row(v_t, j)
        firsts[j % 4] = firsts[j % 4] + yf[j] * row
        lasts[j % 4] = lasts[j % 4] + yl[j] * row
    first = (firsts[0] + firsts[1]) + (firsts[2] + firsts[3])
    last = (lasts[0] + lasts[1]) + (lasts[2] + lasts[3])
    send[0] = my[0] + flux[2]
    send[1:3] = my[1:3]
    send[3] = first
    send[4] = last


def y_pack_kernel(own, other, both):
    on_low = lax.rem(lax.axis_index("gx"), 2) == 0
    both[:, 0:GROUPS] = jnp.where(on_low, own[...], other[...])
    both[:, GROUPS : 2 * GROUPS] = jnp.where(on_low, other[...], own[...])


def y_local_kernel(v_t, f, u, after, g_t):
    total = y_row(v_t, 0)
    g_t[0] = total
    for j in range(1, BY):
        total = y_row(v_t, j) + f[j - 1] * total
        g_t[j] = total
    x = jnp.zeros_like(total)
    for j in range(BY - 1, -1, -1):
        x = u[j] * g_t[j] + f[j] * x
        g_t[j] = x


def y_merge_kernel(own, far, near, shared, quad, coefs, blocks):
    arrange(own, far, near, shared, lax.rem(lax.axis_index("gy"), SIDE), blocks)
    joined = [blocks[0, n] for n in range(5)]
    for c in range(1, SIDE):
        joined, flow = y_merge(joined, [blocks[c, n] for n in range(5)])
        for n in range(3):
            coefs[c - 1, n] = flow[n]
    for n in range(5):
        quad[n] = joined[n]


def y_solve_kernel(
    own, far, near, shared, coefs, g_t, yf, yl, st, out_hbm, blocks, slots, inner, work, out, sems
):
    me = lax.axis_index("gy")
    place, depth = lax.div(me, SIDE), lax.rem(me, SIDE)
    arrange(own, far, near, shared, place, blocks)
    y_flows(blocks, slots)
    enter, flow = slots[place], slots[place + 1]
    inner[0] = enter
    inner[SIDE] = flow
    for c in range(SIDE - 1, 0, -1):
        flow = coefs[c - 1, 0] + coefs[c - 1, 1] * enter + coefs[c - 1, 2] * flow
        inner[c] = flow
    rows = pl.ds(pl.multiple_of(lax.rem(lax.axis_index("gx"), 2) * GROUPS, GROUPS), GROUPS)
    enter, leave = inner[depth, rows, :], inner[depth + 1, rows, :]
    for j in range(BY):
        work[pl.ds(j * GROUPS, GROUPS), :] = 2.0 * (g_t[j] + yf[j] * enter - yl[j] * leave)
    moves = []
    for g in range(GROUPS):
        rows = pl.ds(g * 128, 128)
        out[rows, :] = group(st, g) + work[pl.ds(g, BY, stride=GROUPS), :].T
        move = pltpu.make_async_copy(out.at[rows], out_hbm.at[rows], sems.at[g])
        move.start()
        moves.append(move)
    for move in moves:
        move.wait()


def call(kernel, outs, args, scratch=(), cost=100_000):
    vm = pl.BlockSpec(memory_space=pltpu.VMEM)
    hbm = pl.BlockSpec(memory_space=pltpu.HBM)
    return pl.pallas_call(
        kernel,
        out_shape=[
            jax.ShapeDtypeStruct(shape, F32) if far else pltpu.VMEM(shape, F32)
            for shape, far in outs
        ],
        in_specs=[hbm if far else vm for _, far in args],
        out_specs=[hbm if far else vm for _, far in outs],
        scratch_shapes=list(scratch),
        compiler_params=pltpu.CompilerParams(vmem_limit_bytes=LIMIT),
        cost_estimate=pl.CostEstimate(flops=cost, bytes_accessed=cost, transcendentals=0),
    )(*[value for value, _ in args])


def near(*values):
    return [(value, False) for value in values]


def on_device(state, kappa_x, kappa_y):
    flat = [
        pltpu.with_memory_space_constraint(a, pltpu.HBM) for a in (state, kappa_x, kappa_y)
    ]
    plane = (ROWS, BY)
    pitched = (NZ * PITCH, BY)
    planes = (NZ, PITCH, BY)
    xs = (BX, NZ, BY)
    ys = (BY, GROUPS, 128)
    x_block = (7, NZ, BY)
    edge = (2, GROUPS, 128)
    nx, ny = lax.axis_size("gx"), lax.axis_size("gy")
    wide = (5, 2 * GROUPS, 128)
    st, kx, st_t, ky_t, mine, first, second = call(
        load_kernel,
        near(planes, planes, plane, plane, (4, GROUPS, 128), edge, edge),
        [(a, True) for a in flat],
        [pltpu.VMEM((NZ, BX, BY), F32), pltpu.SemaphoreType.DMA((3,))],
    )
    st, kx = st.reshape(pitched), kx.reshape(pitched)
    pairs = [
        (i * ny + j, i * ny + j + 2 * (j % 2) - 1 if 0 < j < ny - 1 else (i ^ 1) * ny + j)
        for i in range(nx)
        for j in range(ny)
    ]
    came2 = lax.ppermute(second, ("gx", "gy"), pairs)
    came1 = lax.ppermute(first, "gy", [(i, i ^ 1) for i in range(ny)])
    fx, ux, wf, wl, part, edges, base_t = call(
        x_matrix_kernel,
        near(xs, xs, pitched, pitched, x_block, (4, GROUPS, 128), plane),
        near(st_t, kx, ky_t),
        [pltpu.VMEM(pitched, F32), pltpu.VMEM(xs, F32)],
        cost=5_000_000,
    )
    ends, flux = call(
        x_ends_kernel,
        near(x_block, (3, GROUPS, 128)),
        near(came2, came1, mine, part, edges),
        [pltpu.VMEM((2, NZ, BY), F32)],
    )
    other = lax.ppermute(ends, "gx", [(i, i ^ 1) for i in range(nx)])
    (d,) = call(
        x_local_kernel,
        near(pitched),
        near(base_t, flux, st, fx, ux),
        [pltpu.VMEM(pitched, F32), pltpu.VMEM(xs, F32), pltpu.VMEM(plane, F32)],
        cost=3_000_000,
    )
    chip, coefs = call(x_merge_kernel, near(x_block, (3, NZ, BY)), near(ends, other, d))
    def swap(axes, bits, value):
        return lax.ppermute(
            value,
            ("gx", "gy"),
            [
                (i * ny + j, (i ^ (2 * bits[i % 2])) * ny + j if axes == "x" else i * ny + (j ^ bits[i % 2]))
                for i in range(nx)
                for j in range(ny)
            ],
        )

    def share(value):
        return lax.ppermute(value, "gx", [(i, i ^ 1) for i in range(nx)])

    far = swap("x", (3, 2), chip)
    near_x = swap("x", (1, 1), chip)
    f, u, yf, yl, my = call(
        y_matrix_kernel,
        near(ys, ys, ys, ys, (3, GROUPS, 128)),
        near(ky_t, coefs),
        [pltpu.VMEM(ys, F32)],
        cost=5_000_000,
    )
    (relayed,) = call(relay_kernel, near(x_block), near(far, my))
    v_t, own = call(
        y_ends_kernel,
        near(plane, (5, GROUPS, 128)),
        near(chip, far, near_x, share(relayed), coefs, d, wf, wl, yf, yl, my, flux),
        [
            pltpu.VMEM((SIDE,) + x_block, F32),
            pltpu.VMEM((SIDE + 1, NZ, BY), F32),
            pltpu.VMEM((2, NZ, BY), F32),
        ],
    )
    (both,) = call(y_pack_kernel, near(wide), near(own, share(own)))
    far = swap("y", (3, 2), both)
    near_y = swap("y", (1, 1), both)
    (g_t,) = call(y_local_kernel, near(ys), near(v_t, f, u, both), cost=3_000_000)
    (relayed,) = call(relay_kernel, near(wide), near(far, g_t))
    quad, coefs = call(
        y_merge_kernel,
        near(wide, (SIDE - 1, 3, 2 * GROUPS, 128)),
        near(both, far, near_y, share(relayed)),
        [pltpu.VMEM((SIDE,) + wide, F32)],
    )
    far = swap("y", (12, 8), quad)
    near_y = swap("y", (4, 4), quad)
    (out,) = call(
        y_solve_kernel,
        [(plane, True)],
        near(quad, far, near_y, share(far), coefs, g_t, yf, yl, st),
        [
            pltpu.VMEM((SIDE,) + wide, F32),
            pltpu.VMEM((SIDE + 1, 2 * GROUPS, 128), F32),
            pltpu.VMEM((SIDE + 1, 2 * GROUPS, 128), F32),
            pltpu.VMEM(plane, F32),
            pltpu.VMEM(plane, F32),
            pltpu.SemaphoreType.DMA((GROUPS,)),
        ],
    )
    return out.reshape(state.shape)


def solution(mesh):
    spec = P(None, "gx", "gy")
    return jax.shard_map(
        on_device, mesh=mesh, in_specs=(spec, spec, spec), out_specs=spec, check_vma=False
    )
```

```python
import jax
import jax.numpy as jnp
from jax import lax
from jax.experimental import pallas as pl
from jax.experimental.pallas import tpu as pltpu
from jax.sharding import PartitionSpec as P

F32 = jnp.float32
NZ, BX, BY = 16, 64, 128
ROWS = NZ * BX
GROUPS = ROWS // 128
LIMIT = 8 * 1024 * 1024
SIDE = 4
PITCH = 72


def x_row(ref, i):
    return jnp.concatenate(
        [ref[pl.ds(i, 8, stride=PITCH), :], ref[pl.ds(8 * PITCH + i, 8, stride=PITCH), :]], axis=0
    )


def y_row(ref, j):
    return ref[pl.ds(j * GROUPS, GROUPS), :]


def place_rows(ref, i, value):
    ref[pl.ds(i, 8, stride=PITCH), :] = value[:8]
    ref[pl.ds(8 * PITCH + i, 8, stride=PITCH), :] = value[8:]


def group(ref, g):
    return jnp.concatenate([ref[pl.ds(z * PITCH, BX), :] for z in (2 * g, 2 * g + 1)], axis=0)


def place_group(ref, g, value):
    ref[pl.ds(2 * g * PITCH, BX), :] = value[:BX]
    ref[pl.ds((2 * g + 1) * PITCH, BX), :] = value[BX:]


def merge(low, high):
    inv = (1.0 / ((2.0 / (low[4] + high[3])) + low[2] + high[0]))
    e = (low[6] - high[5]) * inv
    a = low[1] * inv
    b = high[1] * inv
    joined = [
        low[0] - low[1] * a,
        low[1] * b,
        high[2] - high[1] * b,
        low[3],
        high[4],
        low[5] - low[1] * e,
        high[6] + high[1] * e,
    ]
    return joined, (e, a, b)


def flows_of(count, pivot, lower, upper, gain, slots):
    half = (count + 1) // 2
    up, down = {}, {}
    for n in range(half + 1):
        i = n
        if i < half:
            gain_i, pivot_i = gain(i), pivot(i)
            if i:
                gain_i = gain_i + lower(i) * up[i - 1][0]
                pivot_i = pivot_i - lower(i) * up[i - 1][1]
            inv = (1.0 / (pivot_i))
            up[i] = gain_i * inv, upper(i) * inv
        i = count - n
        if i > half:
            gain_i, pivot_i = gain(i), pivot(i)
            if n:
                gain_i = gain_i + upper(i) * down[i + 1][0]
                pivot_i = pivot_i - upper(i) * down[i + 1][1]
            inv = (1.0 / (pivot_i))
            down[i] = gain_i * inv, lower(i) * inv
    below, above = up[half - 1], down[half + 1]
    low, high = lower(half), upper(half)
    flow = (gain(half) + low * below[0] + high * above[0]) * (1.0 / (
        pivot(half) - low * below[1] - high * above[1]
    ))
    slots[half] = flow
    rising = flow
    for n in range(1, half + 1):
        if half - n >= 0:
            flow = up[half - n][0] + up[half - n][1] * flow
            slots[half - n] = flow
        if half + n <= count:
            rising = down[half + n][0] + down[half + n][1] * rising
            slots[half + n] = rising


def x_flows(blocks, slots):
    count = blocks.shape[0]

    def pivot(i):
        if i == 0:
            return (2.0 / (blocks[0, 3])) + blocks[0, 0]
        if i == count:
            return (2.0 / (blocks[count - 1, 4])) + blocks[count - 1, 2]
        return (2.0 / (blocks[i - 1, 4] + blocks[i, 3])) + blocks[i - 1, 2] + blocks[i, 0]

    def gain(i):
        if i == 0:
            return -blocks[0, 5]
        return blocks[i - 1, 6] - blocks[i, 5] if i < count else blocks[i - 1, 6]

    flows_of(count, pivot, lambda i: blocks[i - 1, 1], lambda i: blocks[i, 1], gain, slots)


def y_merge(low, high):
    inv = 1.0 / (low[2] + high[0])
    e = (low[4] - high[3]) * inv
    a = low[1] * inv
    b = high[1] * inv
    joined = [
        low[0] - low[1] * a,
        low[1] * b,
        high[2] - high[1] * b,
        low[3] - low[1] * e,
        high[4] + high[1] * e,
    ]
    return joined, (e, a, b)


def arrange(own, far, near, shared, place, blocks):
    on_low = lax.rem(lax.axis_index("gx"), 2) == 0
    blocks[place] = own[...]
    blocks[place ^ 3] = near[...]
    blocks[place ^ 2] = jnp.where(on_low, shared[...], far[...])
    blocks[place ^ 1] = jnp.where(on_low, far[...], shared[...])


def y_flows(blocks, slots):
    count = blocks.shape[0]

    def pivot(i):
        if i == 0:
            return blocks[0, 0]
        return blocks[i - 1, 2] + blocks[i, 0] if i < count else blocks[i - 1, 2]

    def gain(i):
        if i == 0:
            return -blocks[0, 3]
        return blocks[i - 1, 4] - blocks[i, 3] if i < count else blocks[i - 1, 4]

    flows_of(count, pivot, lambda i: blocks[i - 1, 1], lambda i: blocks[i, 1], gain, slots)


def load_kernel(st_hbm, kx_hbm, ky_hbm, st, kx, st_t, ky_t, mine, first, second, ky, sems):
    inside = pl.ds(0, BX)
    moves = [
        pltpu.make_async_copy(src, dst, sems.at[n])
        for n, (src, dst) in enumerate(
            ((ky_hbm, ky), (st_hbm, st.at[:, inside, :]), (kx_hbm, kx.at[:, inside, :]))
        )
    ]
    for move in moves:
        move.start()
    moves[0].wait()
    for g in range(GROUPS):
        pair = jnp.concatenate([ky[2 * g], ky[2 * g + 1]], axis=0)
        ky_t[pl.ds(g, BY, stride=GROUPS), :] = pair.T
    moves[1].wait()
    for g in range(GROUPS):
        pair = jnp.concatenate([st[2 * g, inside, :], st[2 * g + 1, inside, :]], axis=0)
        st_t[pl.ds(g, BY, stride=GROUPS), :] = pair.T
    for n, ref in enumerate((st_t, ky_t)):
        mine[n] = y_row(ref, 0)
        mine[2 + n] = y_row(ref, BY - 1)
    even = lax.rem(lax.axis_index("gy"), 2) == 0
    low, high = mine[0:2], mine[2:4]
    first[...] = jnp.where(even, high, low)
    second[...] = jnp.where(even, low, high)
    moves[2].wait()


def sweep(count, row, f, u, ratios, put_first, put_last):
    ahead = jnp.ones_like(row(0))
    back = jnp.ones_like(ahead)
    low, high = row(0), row(count - 1)
    for i in range(count - 1):
        nxt = row(i + 1)
        r = 0.5 * (low + nxt)
        low = nxt
        inv = (1.0 / (r + ahead))
        ratio = r * inv
        ahead = 1.0 + ratio * ahead
        u[i] = inv
        f[i] = ratio
        j = count - 1 - i
        prev = row(j - 1)
        r = 0.5 * (high + prev)
        high = prev
        ratio = r * (1.0 / (r + back))
        back = 1.0 + ratio * back
        ratios[j] = ratio
    start = (1.0 / (back))
    end = (1.0 / (ahead))
    lead, trail = start, end
    put_first(0, start)
    put_last(count - 1, end)
    u[count - 1] = end
    f[count - 1] = jnp.zeros_like(end)
    for i in range(1, count):
        start = start * ratios[i]
        put_first(i, start)
        j = count - 1 - i
        end = end * f[j]
        put_last(j, end)
    return lead, end, trail


def x_matrix_kernel(st_t, kx, ky_t, fx, ux, wf, wl, part, edges, base_t, source, ratios):
    here, k_here = y_row(st_t, 0), y_row(ky_t, 0)
    value = here
    for j in range(BY):
        if j < BY - 1:
            after, k_after = y_row(st_t, j + 1), y_row(ky_t, j + 1)
            flux = 0.5 * (k_here + k_after) * (after - here)
            value = value + flux
        base_t[pl.ds(j * GROUPS, GROUPS), :] = value
        here, k_here, value = after, k_after, after - flux
    for g in range(GROUPS):
        place_group(source, g, base_t[pl.ds(g, BY, stride=GROUPS), :].T)
    sums = [[jnp.zeros((NZ, BY), F32) for _ in range(2)] for _ in range(2)]

    def put(ref, total):
        def store(i, value):
            place_rows(ref, i, value)
            total[i % 2] = total[i % 2] + value * x_row(source, i)

        return store

    values = sweep(BX, lambda i: x_row(kx, i), fx, ux, ratios, put(wf, sums[0]), put(wl, sums[1]))
    values += (x_row(kx, 0), x_row(kx, BX - 1), sums[0][0] + sums[0][1], sums[1][0] + sums[1][1])
    for n, value in enumerate(values):
        part[n] = value
    for n, ref in enumerate((wf, wl)):
        for g in range(GROUPS):
            turned = group(ref, g).T
            edges[2 * n, pl.ds(g, 1), :] = turned[0:1, :]
            edges[2 * n + 1, pl.ds(g, 1), :] = turned[127:128, :]


def y_matrix_kernel(ky_t, after, f, u, yf, yl, my, ratios):
    def put(ref):
        def store(j, value):
            ref[j] = value

        return store

    me = lax.axis_index("gy")
    last = lax.axis_size("gy") - 1
    lead, across, trail = sweep(BY, lambda j: y_row(ky_t, j), f, u, ratios, put(yf), put(yl))
    my[0] = lead
    my[1] = across
    my[2] = trail + jnp.where(me == last, (2.0 / (y_row(ky_t, BY - 1))), 0.0)


def x_ends_kernel(came1, came2, mine, part, edges, send, flux, rows):
    me = lax.axis_index("gy")
    even = lax.rem(me, 2) == 0
    below = jnp.where(me == 0, 0.0, jnp.where(even, came2[...], came1[...]))
    above = jnp.where(me == lax.axis_size("gy") - 1, 0.0, jnp.where(even, came1[...], came2[...]))
    enter = 0.5 * (below[1] + mine[1]) * (mine[0] - below[0])
    leave = 0.5 * (above[1] + mine[3]) * (above[0] - mine[2])
    flux[0] = enter
    flux[1] = leave
    flux[2] = (2.0 / (below[1] + mine[1]))
    lane = lax.broadcasted_iota(jnp.int32, (GROUPS, 128), 1)
    send[0:5] = part[0:5]
    for n in range(2):
        low = -edges[2 * n] * enter
        high = edges[2 * n + 1] * leave
        for h in range(2):
            inside = lane // BX == h
            at_low = jnp.sum(jnp.where(inside, low, 0.0), axis=1, keepdims=True)
            at_high = jnp.sum(jnp.where(inside, high, 0.0), axis=1, keepdims=True)
            value = jnp.where(lane == 0, at_low, jnp.where(lane == 127, at_high, 0.0))
            rows[n, pl.ds(h, GROUPS, stride=2), :] = value
        send[5 + n] = part[5 + n] + rows[n]


def x_local_kernel(base_t, flux, st, fx, ux, d, s, work, work_t):
    work_t[...] = base_t[...]
    work_t[pl.ds(0, GROUPS), :] = y_row(base_t, 0) - flux[0]
    work_t[pl.ds((BY - 1) * GROUPS, GROUPS), :] = y_row(base_t, BY - 1) + flux[1]
    for g in range(GROUPS):
        place_group(s, g, work_t[pl.ds(g, BY, stride=GROUPS), :].T)
    total = x_row(s, 0)
    work[0] = total
    for i in range(1, BX):
        total = x_row(s, i) + fx[i - 1] * total
        work[i] = total
    x = jnp.zeros_like(total)
    for i in range(BX - 1, -1, -1):
        x = ux[i] * work[i] + fx[i] * x
        place_rows(d, i, x - x_row(st, i))


def x_merge_kernel(own, other, after, send, coefs):
    core = lax.rem(lax.axis_index("gx"), 2)
    mine, theirs = [own[n] for n in range(7)], [other[n] for n in range(7)]
    low = [jnp.where(core == 0, a, b) for a, b in zip(mine, theirs)]
    high = [jnp.where(core == 0, b, a) for a, b in zip(mine, theirs)]
    joined, flow = merge(low, high)
    for n in range(7):
        send[n] = joined[n]
    for n in range(3):
        coefs[n] = flow[n]


def relay_kernel(value, after, out):
    out[...] = value[...]


def y_ends_kernel(
    own, far, near, shared, coefs, d, wf, wl, yf, yl, my, flux, v_t, send, blocks, slots, flows
):
    me = lax.axis_index("gx")
    place = lax.div(me, 2)
    on_low = lax.rem(me, 2) == 0
    arrange(own, far, near, shared, place, blocks)
    x_flows(blocks, slots)
    enter, leave = slots[place], slots[place + 1]
    middle = coefs[0] + coefs[1] * enter + coefs[2] * leave
    flows[0] = jnp.where(on_low, enter, middle)
    flows[1] = jnp.where(on_low, middle, leave)
    for g in range(GROUPS):
        parts = []
        for z in range(2 * g, 2 * g + 2):
            rows = pl.ds(z * PITCH, BX)
            parts.append(
                d[rows, :]
                + wf[rows, :] * flows[0, pl.ds(z, 1), :]
                - wl[rows, :] * flows[1, pl.ds(z, 1), :]
            )
        v_t[pl.ds(g, BY, stride=GROUPS), :] = jnp.concatenate(parts, axis=0).T
    firsts = [jnp.zeros((GROUPS, 128), F32) for _ in range(4)]
    lasts = [jnp.zeros((GROUPS, 128), F32) for _ in range(4)]
    for j in range(BY):
        row = y_row(v_t, j)
        firsts[j % 4] = firsts[j % 4] + yf[j] * row
        lasts[j % 4] = lasts[j % 4] + yl[j] * row
    first = (firsts[0] + firsts[1]) + (firsts[2] + firsts[3])
    last = (lasts[0] + lasts[1]) + (lasts[2] + lasts[3])
    send[0] = my[0] + flux[2]
    send[1:3] = my[1:3]
    send[3] = first
    send[4] = last


def y_pack_kernel(own, other, both):
    on_low = lax.rem(lax.axis_index("gx"), 2) == 0
    both[:, 0:GROUPS] = jnp.where(on_low, own[...], other[...])
    both[:, GROUPS : 2 * GROUPS] = jnp.where(on_low, other[...], own[...])


def y_local_kernel(v_t, f, u, after, g_t):
    total = y_row(v_t, 0)
    g_t[0] = total
    for j in range(1, BY):
        total = y_row(v_t, j) + f[j - 1] * total
        g_t[j] = total
    x = jnp.zeros_like(total)
    for j in range(BY - 1, -1, -1):
        x = u[j] * g_t[j] + f[j] * x
        g_t[j] = x


def own_rows():
    start = lax.rem(lax.axis_index("gx"), 2) * GROUPS
    return pl.ds(pl.multiple_of(start, GROUPS), GROUPS)


def other_rows():
    start = (1 - lax.rem(lax.axis_index("gx"), 2)) * GROUPS
    return pl.ds(pl.multiple_of(start, GROUPS), GROUPS)


def pick_kernel(value, out):
    out[...] = value[:, other_rows(), :]


def y_merge_kernel(own, far, near, shared, quad, mine, coefs, blocks):
    arrange(own, far, near, shared, lax.rem(lax.axis_index("gy"), SIDE), blocks)
    joined = [blocks[0, n] for n in range(5)]
    for c in range(1, SIDE):
        joined, flow = y_merge(joined, [blocks[c, n] for n in range(5)])
        for n in range(3):
            coefs[c - 1, n] = flow[n]
    for n in range(5):
        quad[n] = joined[n]
    mine[...] = quad[:, own_rows(), :]


def y_solve_kernel(
    mine, far, near, shared, coefs, g_t, yf, yl, st, out_hbm, blocks, slots, inner, work, out, sems
):
    me = lax.axis_index("gy")
    place, depth = lax.div(me, SIDE), lax.rem(me, SIDE)
    rows = own_rows()
    arrange(mine, far.at[:, rows, :], near, shared, place, blocks)
    y_flows(blocks, slots)
    enter, flow = slots[place], slots[place + 1]
    inner[0] = enter
    inner[SIDE] = flow
    for c in range(SIDE - 1, 0, -1):
        e, a, b = [coefs[c - 1, n, rows, :] for n in range(3)]
        flow = e + a * enter + b * flow
        inner[c] = flow
    enter, leave = inner[depth], inner[depth + 1]
    for j in range(BY):
        work[pl.ds(j * GROUPS, GROUPS), :] = 2.0 * (g_t[j] + yf[j] * enter - yl[j] * leave)
    moves = []
    for g in range(GROUPS):
        rows = pl.ds(g * 128, 128)
        out[rows, :] = group(st, g) + work[pl.ds(g, BY, stride=GROUPS), :].T
        move = pltpu.make_async_copy(out.at[rows], out_hbm.at[rows], sems.at[g])
        move.start()
        moves.append(move)
    for move in moves:
        move.wait()


def call(kernel, outs, args, scratch=(), cost=100_000):
    vm = pl.BlockSpec(memory_space=pltpu.VMEM)
    hbm = pl.BlockSpec(memory_space=pltpu.HBM)
    return pl.pallas_call(
        kernel,
        out_shape=[
            jax.ShapeDtypeStruct(shape, F32) if far else pltpu.VMEM(shape, F32)
            for shape, far in outs
        ],
        in_specs=[hbm if far else vm for _, far in args],
        out_specs=[hbm if far else vm for _, far in outs],
        scratch_shapes=list(scratch),
        compiler_params=pltpu.CompilerParams(vmem_limit_bytes=LIMIT),
        cost_estimate=pl.CostEstimate(flops=cost, bytes_accessed=cost, transcendentals=0),
    )(*[value for value, _ in args])


def near(*values):
    return [(value, False) for value in values]


def on_device(state, kappa_x, kappa_y):
    flat = [
        pltpu.with_memory_space_constraint(a, pltpu.HBM) for a in (state, kappa_x, kappa_y)
    ]
    plane = (ROWS, BY)
    pitched = (NZ * PITCH, BY)
    planes = (NZ, PITCH, BY)
    xs = (BX, NZ, BY)
    ys = (BY, GROUPS, 128)
    x_block = (7, NZ, BY)
    edge = (2, GROUPS, 128)
    nx, ny = lax.axis_size("gx"), lax.axis_size("gy")
    wide = (5, 2 * GROUPS, 128)
    st, kx, st_t, ky_t, mine, first, second = call(
        load_kernel,
        near(planes, planes, plane, plane, (4, GROUPS, 128), edge, edge),
        [(a, True) for a in flat],
        [pltpu.VMEM((NZ, BX, BY), F32), pltpu.SemaphoreType.DMA((3,))],
    )
    st, kx = st.reshape(pitched), kx.reshape(pitched)
    pairs = [
        (i * ny + j, i * ny + j + 2 * (j % 2) - 1 if 0 < j < ny - 1 else (i ^ 1) * ny + j)
        for i in range(nx)
        for j in range(ny)
    ]
    came2 = lax.ppermute(second, ("gx", "gy"), pairs)
    came1 = lax.ppermute(first, "gy", [(i, i ^ 1) for i in range(ny)])
    fx, ux, wf, wl, part, edges, base_t = call(
        x_matrix_kernel,
        near(xs, xs, pitched, pitched, x_block, (4, GROUPS, 128), plane),
        near(st_t, kx, ky_t),
        [pltpu.VMEM(pitched, F32), pltpu.VMEM(xs, F32)],
        cost=5_000_000,
    )
    ends, flux = call(
        x_ends_kernel,
        near(x_block, (3, GROUPS, 128)),
        near(came1, came2, mine, part, edges),
        [pltpu.VMEM((2, NZ, BY), F32)],
    )
    other = lax.ppermute(ends, "gx", [(i, i ^ 1) for i in range(nx)])
    (d,) = call(
        x_local_kernel,
        near(pitched),
        near(base_t, flux, st, fx, ux),
        [pltpu.VMEM(pitched, F32), pltpu.VMEM(xs, F32), pltpu.VMEM(plane, F32)],
        cost=3_000_000,
    )
    chip, coefs = call(x_merge_kernel, near(x_block, (3, NZ, BY)), near(ends, other, d))
    def swap(axes, bits, value):
        return lax.ppermute(
            value,
            ("gx", "gy"),
            [
                (i * ny + j, (i ^ (2 * bits[i % 2])) * ny + j if axes == "x" else i * ny + (j ^ bits[i % 2]))
                for i in range(nx)
                for j in range(ny)
            ],
        )

    def share(value):
        return lax.ppermute(value, "gx", [(i, i ^ 1) for i in range(nx)])

    far = swap("x", (1, 2), chip)
    near_x = swap("x", (3, 3), chip)
    f, u, yf, yl, my = call(
        y_matrix_kernel,
        near(ys, ys, ys, ys, (3, GROUPS, 128)),
        near(ky_t, coefs),
        [pltpu.VMEM(ys, F32)],
        cost=5_000_000,
    )
    (relayed,) = call(relay_kernel, near(x_block), near(far, my))
    v_t, own = call(
        y_ends_kernel,
        near(plane, (5, GROUPS, 128)),
        near(chip, far, near_x, share(relayed), coefs, d, wf, wl, yf, yl, my, flux),
        [
            pltpu.VMEM((SIDE,) + x_block, F32),
            pltpu.VMEM((SIDE + 1, NZ, BY), F32),
            pltpu.VMEM((2, NZ, BY), F32),
        ],
    )
    (both,) = call(y_pack_kernel, near(wide), near(own, share(own)))
    far = swap("y", (1, 2), both)
    near_y = swap("y", (3, 3), both)
    (g_t,) = call(y_local_kernel, near(ys), near(v_t, f, u, both), cost=3_000_000)
    (relayed,) = call(relay_kernel, near(wide), near(far, g_t))
    quad, mine, coefs = call(
        y_merge_kernel,
        near(wide, (5, GROUPS, 128), (SIDE - 1, 3, 2 * GROUPS, 128)),
        near(both, far, near_y, share(relayed)),
        [pltpu.VMEM((SIDE,) + wide, F32)],
    )
    far = swap("y", (4, 8), quad)
    near_y = swap("y", (12, 12), mine)
    (picked,) = call(pick_kernel, near((5, GROUPS, 128)), near(far))
    (out,) = call(
        y_solve_kernel,
        [(plane, True)],
        near(mine, far, near_y, share(picked), coefs, g_t, yf, yl, st),
        [
            pltpu.VMEM((SIDE, 5, GROUPS, 128), F32),
            pltpu.VMEM((SIDE + 1, GROUPS, 128), F32),
            pltpu.VMEM((SIDE + 1, GROUPS, 128), F32),
            pltpu.VMEM(plane, F32),
            pltpu.VMEM(plane, F32),
            pltpu.SemaphoreType.DMA((GROUPS,)),
        ],
    )
    return out.reshape(state.shape)


def solution(mesh):
    spec = P(None, "gx", "gy")
    return jax.shard_map(
        on_device, mesh=mesh, in_specs=(spec, spec, spec), out_specs=spec, check_vma=False
    )
```

```python
import jax
import jax.numpy as jnp
from jax import lax
from jax.experimental import pallas as pl
from jax.experimental.pallas import tpu as pltpu
from jax.sharding import PartitionSpec as P

F32 = jnp.float32
NZ, BX, BY = 16, 64, 128
ROWS = NZ * BX
GROUPS = ROWS // 128
LIMIT = 8 * 1024 * 1024
SIDE = 4
PITCH = 72


def x_row(ref, i):
    return jnp.concatenate(
        [ref[pl.ds(i, 8, stride=PITCH), :], ref[pl.ds(8 * PITCH + i, 8, stride=PITCH), :]], axis=0
    )


def y_row(ref, j):
    return ref[pl.ds(j * GROUPS, GROUPS), :]


def place_rows(ref, i, value):
    ref[pl.ds(i, 8, stride=PITCH), :] = value[:8]
    ref[pl.ds(8 * PITCH + i, 8, stride=PITCH), :] = value[8:]


def group(ref, g):
    return jnp.concatenate([ref[pl.ds(z * PITCH, BX), :] for z in (2 * g, 2 * g + 1)], axis=0)


def place_group(ref, g, value):
    ref[pl.ds(2 * g * PITCH, BX), :] = value[:BX]
    ref[pl.ds((2 * g + 1) * PITCH, BX), :] = value[BX:]


def merge(low, high):
    inv = 1.0 / (low[2] + high[0])
    e = (low[4] - high[3]) * inv
    a = low[1] * inv
    b = high[1] * inv
    joined = [
        low[0] - low[1] * a,
        low[1] * b,
        high[2] - high[1] * b,
        low[3] - low[1] * e,
        high[4] + high[1] * e,
    ]
    return joined, (e, a, b)


def flows_of(count, pivot, lower, upper, gain, slots):
    half = (count + 1) // 2
    up, down = {}, {}
    for n in range(half + 1):
        i = n
        if i < half:
            gain_i, pivot_i = gain(i), pivot(i)
            if i:
                gain_i = gain_i + lower(i) * up[i - 1][0]
                pivot_i = pivot_i - lower(i) * up[i - 1][1]
            inv = (1.0 / (pivot_i))
            up[i] = gain_i * inv, upper(i) * inv
        i = count - n
        if i > half:
            gain_i, pivot_i = gain(i), pivot(i)
            if n:
                gain_i = gain_i + upper(i) * down[i + 1][0]
                pivot_i = pivot_i - upper(i) * down[i + 1][1]
            inv = (1.0 / (pivot_i))
            down[i] = gain_i * inv, lower(i) * inv
    below, above = up[half - 1], down[half + 1]
    low, high = lower(half), upper(half)
    flow = (gain(half) + low * below[0] + high * above[0]) * (1.0 / (
        pivot(half) - low * below[1] - high * above[1]
    ))
    slots[half] = flow
    rising = flow
    for n in range(1, half + 1):
        if half - n >= 0:
            flow = up[half - n][0] + up[half - n][1] * flow
            slots[half - n] = flow
        if half + n <= count:
            rising = down[half + n][0] + down[half + n][1] * rising
            slots[half + n] = rising


def arrange(own, far, near, shared, place, blocks):
    on_low = lax.rem(lax.axis_index("gx"), 2) == 0
    blocks[place] = own[...]
    blocks[place ^ 3] = near[...]
    blocks[place ^ 2] = jnp.where(on_low, shared[...], far[...])
    blocks[place ^ 1] = jnp.where(on_low, far[...], shared[...])


def line_flows(blocks, slots):
    count = blocks.shape[0]

    def pivot(i):
        if i == 0:
            return blocks[0, 0]
        return blocks[i - 1, 2] + blocks[i, 0] if i < count else blocks[i - 1, 2]

    def gain(i):
        if i == 0:
            return -blocks[0, 3]
        return blocks[i - 1, 4] - blocks[i, 3] if i < count else blocks[i - 1, 4]

    flows_of(count, pivot, lambda i: blocks[i - 1, 1], lambda i: blocks[i, 1], gain, slots)


def load_kernel(st_hbm, kx_hbm, ky_hbm, st, kx, st_t, ky_t, mine, first, second, last, ky, sems):
    inside = pl.ds(0, BX)
    moves = [
        pltpu.make_async_copy(src, dst, sems.at[n])
        for n, (src, dst) in enumerate(
            ((ky_hbm, ky), (st_hbm, st.at[:, inside, :]), (kx_hbm, kx.at[:, inside, :]))
        )
    ]
    for move in moves:
        move.start()
    moves[0].wait()
    for g in range(GROUPS):
        pair = jnp.concatenate([ky[2 * g], ky[2 * g + 1]], axis=0)
        ky_t[pl.ds(g, BY, stride=GROUPS), :] = pair.T
    moves[1].wait()
    for g in range(GROUPS):
        pair = jnp.concatenate([st[2 * g, inside, :], st[2 * g + 1, inside, :]], axis=0)
        st_t[pl.ds(g, BY, stride=GROUPS), :] = pair.T
    for n, ref in enumerate((st_t, ky_t)):
        mine[n] = y_row(ref, 0)
        mine[2 + n] = y_row(ref, BY - 1)
    even = lax.rem(lax.axis_index("gy"), 2) == 0
    low, high = mine[0:2], mine[2:4]
    first[...] = jnp.where(even, high, low)
    second[...] = jnp.where(even, low, high)
    moves[2].wait()
    for z in range(NZ):
        last[pl.ds(z, 1), :] = kx[z, pl.ds(BX - 1, 1), :]


def sweep(count, row, f, u, ratios, put_first, put_last):
    ahead = jnp.ones_like(row(0))
    back = jnp.ones_like(ahead)
    low, high = row(0), row(count - 1)
    for i in range(count - 1):
        nxt = row(i + 1)
        r = 0.5 * (low + nxt)
        low = nxt
        inv = (1.0 / (r + ahead))
        ratio = r * inv
        ahead = 1.0 + ratio * ahead
        u[i] = inv
        f[i] = ratio
        j = count - 1 - i
        prev = row(j - 1)
        r = 0.5 * (high + prev)
        high = prev
        ratio = r * (1.0 / (r + back))
        back = 1.0 + ratio * back
        ratios[j] = ratio
    start = (1.0 / (back))
    end = (1.0 / (ahead))
    lead, trail = start, end
    put_first(0, start)
    put_last(count - 1, end)
    u[count - 1] = end
    f[count - 1] = jnp.zeros_like(end)
    for i in range(1, count):
        start = start * ratios[i]
        put_first(i, start)
        j = count - 1 - i
        end = end * f[j]
        put_last(j, end)
    return lead, end, trail


def x_matrix_kernel(st_t, kx, ky_t, fx, ux, wf, wl, part, edges, base_t, source, ratios):
    here, k_here = y_row(st_t, 0), y_row(ky_t, 0)
    value = here
    for j in range(BY):
        if j < BY - 1:
            after, k_after = y_row(st_t, j + 1), y_row(ky_t, j + 1)
            flux = 0.5 * (k_here + k_after) * (after - here)
            value = value + flux
        base_t[pl.ds(j * GROUPS, GROUPS), :] = value
        here, k_here, value = after, k_after, after - flux
    for g in range(GROUPS):
        place_group(source, g, base_t[pl.ds(g, BY, stride=GROUPS), :].T)
    sums = [[jnp.zeros((NZ, BY), F32) for _ in range(2)] for _ in range(2)]

    def put(ref, total):
        def store(i, value):
            place_rows(ref, i, value)
            total[i % 2] = total[i % 2] + value * x_row(source, i)

        return store

    values = sweep(BX, lambda i: x_row(kx, i), fx, ux, ratios, put(wf, sums[0]), put(wl, sums[1]))
    lead, across, trail = values
    last = lax.axis_index("gx") == lax.axis_size("gx") - 1
    trail = trail + jnp.where(last, 2.0 / x_row(kx, BX - 1), 0.0)
    values = (lead, across, trail, sums[0][0] + sums[0][1], sums[1][0] + sums[1][1], x_row(kx, 0))
    for n, value in enumerate(values):
        part[n] = value
    for n, ref in enumerate((wf, wl)):
        for g in range(GROUPS):
            turned = group(ref, g).T
            edges[2 * n, pl.ds(g, 1), :] = turned[0:1, :]
            edges[2 * n + 1, pl.ds(g, 1), :] = turned[127:128, :]


def y_matrix_kernel(ky_t, after, f, u, yf, yl, my, ratios):
    def put(ref):
        def store(j, value):
            ref[j] = value

        return store

    me = lax.axis_index("gy")
    last = lax.axis_size("gy") - 1
    lead, across, trail = sweep(BY, lambda j: y_row(ky_t, j), f, u, ratios, put(yf), put(yl))
    my[0] = lead
    my[1] = across
    my[2] = trail + jnp.where(me == last, (2.0 / (y_row(ky_t, BY - 1))), 0.0)


def x_ends_kernel(came1, came2, below_x, mine, part, edges, send, flux, rows):
    me = lax.axis_index("gy")
    even = lax.rem(me, 2) == 0
    below = jnp.where(me == 0, 0.0, jnp.where(even, came2[...], came1[...]))
    above = jnp.where(me == lax.axis_size("gy") - 1, 0.0, jnp.where(even, came1[...], came2[...]))
    enter = 0.5 * (below[1] + mine[1]) * (mine[0] - below[0])
    leave = 0.5 * (above[1] + mine[3]) * (above[0] - mine[2])
    flux[0] = enter
    flux[1] = leave
    flux[2] = (2.0 / (below[1] + mine[1]))
    lane = lax.broadcasted_iota(jnp.int32, (GROUPS, 128), 1)
    below_x = jnp.where(lax.axis_index("gx") == 0, 0.0, below_x[...])
    send[0] = part[0] + 2.0 / (below_x + part[5])
    send[1:3] = part[1:3]
    for n in range(2):
        low = -edges[2 * n] * enter
        high = edges[2 * n + 1] * leave
        for h in range(2):
            inside = lane // BX == h
            at_low = jnp.sum(jnp.where(inside, low, 0.0), axis=1, keepdims=True)
            at_high = jnp.sum(jnp.where(inside, high, 0.0), axis=1, keepdims=True)
            value = jnp.where(lane == 0, at_low, jnp.where(lane == 127, at_high, 0.0))
            rows[n, pl.ds(h, GROUPS, stride=2), :] = value
        send[3 + n] = part[3 + n] + rows[n]


def x_local_kernel(base_t, flux, st, fx, ux, d, s, work, work_t):
    work_t[...] = base_t[...]
    work_t[pl.ds(0, GROUPS), :] = y_row(base_t, 0) - flux[0]
    work_t[pl.ds((BY - 1) * GROUPS, GROUPS), :] = y_row(base_t, BY - 1) + flux[1]
    for g in range(GROUPS):
        place_group(s, g, work_t[pl.ds(g, BY, stride=GROUPS), :].T)
    total = x_row(s, 0)
    work[0] = total
    for i in range(1, BX):
        total = x_row(s, i) + fx[i - 1] * total
        work[i] = total
    x = jnp.zeros_like(total)
    for i in range(BX - 1, -1, -1):
        x = ux[i] * work[i] + fx[i] * x
        place_rows(d, i, x - x_row(st, i))


def x_merge_kernel(own, other, after, send, coefs):
    core = lax.rem(lax.axis_index("gx"), 2)
    mine, theirs = [own[n] for n in range(5)], [other[n] for n in range(5)]
    low = [jnp.where(core == 0, a, b) for a, b in zip(mine, theirs)]
    high = [jnp.where(core == 0, b, a) for a, b in zip(mine, theirs)]
    joined, flow = merge(low, high)
    for n in range(5):
        send[n] = joined[n]
    for n in range(3):
        coefs[n] = flow[n]


def relay_kernel(value, after, out):
    out[...] = value[...]


def y_ends_kernel(
    own, far, near, shared, coefs, d, wf, wl, yf, yl, my, flux, v_t, send, blocks, slots, flows
):
    me = lax.axis_index("gx")
    place = lax.div(me, 2)
    on_low = lax.rem(me, 2) == 0
    arrange(own, far, near, shared, place, blocks)
    line_flows(blocks, slots)
    enter, leave = slots[place], slots[place + 1]
    middle = coefs[0] + coefs[1] * enter + coefs[2] * leave
    flows[0] = jnp.where(on_low, enter, middle)
    flows[1] = jnp.where(on_low, middle, leave)
    for g in range(GROUPS):
        parts = []
        for z in range(2 * g, 2 * g + 2):
            rows = pl.ds(z * PITCH, BX)
            parts.append(
                d[rows, :]
                + wf[rows, :] * flows[0, pl.ds(z, 1), :]
                - wl[rows, :] * flows[1, pl.ds(z, 1), :]
            )
        v_t[pl.ds(g, BY, stride=GROUPS), :] = jnp.concatenate(parts, axis=0).T
    firsts = [jnp.zeros((GROUPS, 128), F32) for _ in range(4)]
    lasts = [jnp.zeros((GROUPS, 128), F32) for _ in range(4)]
    for j in range(BY):
        row = y_row(v_t, j)
        firsts[j % 4] = firsts[j % 4] + yf[j] * row
        lasts[j % 4] = lasts[j % 4] + yl[j] * row
    first = (firsts[0] + firsts[1]) + (firsts[2] + firsts[3])
    last = (lasts[0] + lasts[1]) + (lasts[2] + lasts[3])
    send[0] = my[0] + flux[2]
    send[1:3] = my[1:3]
    send[3] = first
    send[4] = last


def y_pack_kernel(own, other, both):
    on_low = lax.rem(lax.axis_index("gx"), 2) == 0
    both[:, 0:GROUPS] = jnp.where(on_low, own[...], other[...])
    both[:, GROUPS : 2 * GROUPS] = jnp.where(on_low, other[...], own[...])


def y_local_kernel(v_t, f, u, after, g_t):
    total = y_row(v_t, 0)
    g_t[0] = total
    for j in range(1, BY):
        total = y_row(v_t, j) + f[j - 1] * total
        g_t[j] = total
    x = jnp.zeros_like(total)
    for j in range(BY - 1, -1, -1):
        x = u[j] * g_t[j] + f[j] * x
        g_t[j] = x


def own_rows():
    start = lax.rem(lax.axis_index("gx"), 2) * GROUPS
    return pl.ds(pl.multiple_of(start, GROUPS), GROUPS)


def other_rows():
    start = (1 - lax.rem(lax.axis_index("gx"), 2)) * GROUPS
    return pl.ds(pl.multiple_of(start, GROUPS), GROUPS)


def pick_kernel(value, out):
    out[...] = value[:, other_rows(), :]


def y_merge_kernel(own, far, near, shared, quad, mine, coefs, blocks):
    arrange(own, far, near, shared, lax.rem(lax.axis_index("gy"), SIDE), blocks)
    joined = [blocks[0, n] for n in range(5)]
    for c in range(1, SIDE):
        joined, flow = merge(joined, [blocks[c, n] for n in range(5)])
        for n in range(3):
            coefs[c - 1, n] = flow[n]
    for n in range(5):
        quad[n] = joined[n]
    mine[...] = quad[:, own_rows(), :]


def y_solve_kernel(
    mine, far, near, shared, coefs, g_t, yf, yl, st, out_hbm, blocks, slots, inner, work, out, sem
):
    me = lax.axis_index("gy")
    place, depth = lax.div(me, SIDE), lax.rem(me, SIDE)
    rows = own_rows()
    arrange(mine, far.at[:, rows, :], near, shared, place, blocks)
    line_flows(blocks, slots)
    enter, flow = slots[place], slots[place + 1]
    inner[0] = enter
    inner[SIDE] = flow
    for c in range(SIDE - 1, 0, -1):
        e, a, b = [coefs[c - 1, n, rows, :] for n in range(3)]
        flow = e + a * enter + b * flow
        inner[c] = flow
    enter, leave = inner[depth], inner[depth + 1]
    for j in range(BY):
        work[pl.ds(j * GROUPS, GROUPS), :] = 2.0 * (g_t[j] + yf[j] * enter - yl[j] * leave)
    for g in range(GROUPS):
        rows = pl.ds(g * 128, 128)
        out[rows, :] = group(st, g) + work[pl.ds(g, BY, stride=GROUPS), :].T
        pltpu.make_async_copy(out.at[rows], out_hbm.at[rows], sem).start()
    pltpu.make_async_copy(out, out_hbm, sem).wait()


def call(kernel, outs, args, scratch=(), cost=100_000):
    vm = pl.BlockSpec(memory_space=pltpu.VMEM)
    hbm = pl.BlockSpec(memory_space=pltpu.HBM)
    return pl.pallas_call(
        kernel,
        out_shape=[
            jax.ShapeDtypeStruct(shape, F32) if far else pltpu.VMEM(shape, F32)
            for shape, far in outs
        ],
        in_specs=[hbm if far else vm for _, far in args],
        out_specs=[hbm if far else vm for _, far in outs],
        scratch_shapes=list(scratch),
        compiler_params=pltpu.CompilerParams(vmem_limit_bytes=LIMIT),
        cost_estimate=pl.CostEstimate(flops=cost, bytes_accessed=cost, transcendentals=0),
    )(*[value for value, _ in args])


def near(*values):
    return [(value, False) for value in values]


def on_device(state, kappa_x, kappa_y):
    flat = [
        pltpu.with_memory_space_constraint(a, pltpu.HBM) for a in (state, kappa_x, kappa_y)
    ]
    plane = (ROWS, BY)
    pitched = (NZ * PITCH, BY)
    planes = (NZ, PITCH, BY)
    xs = (BX, NZ, BY)
    ys = (BY, GROUPS, 128)
    x_block = (5, NZ, BY)
    edge = (2, GROUPS, 128)
    nx, ny = lax.axis_size("gx"), lax.axis_size("gy")
    wide = (5, 2 * GROUPS, 128)
    st, kx, st_t, ky_t, mine, first, second, last = call(
        load_kernel,
        near(planes, planes, plane, plane, (4, GROUPS, 128), edge, edge, (NZ, BY)),
        [(a, True) for a in flat],
        [pltpu.VMEM((NZ, BX, BY), F32), pltpu.SemaphoreType.DMA((3,))],
    )
    st, kx = st.reshape(pitched), kx.reshape(pitched)
    pairs = [
        (i * ny + j, i * ny + j + 2 * (j % 2) - 1 if 0 < j < ny - 1 else (i ^ 1) * ny + j)
        for i in range(nx)
        for j in range(ny)
    ]
    came2 = lax.ppermute(second, ("gx", "gy"), pairs)
    came1 = lax.ppermute(first, "gy", [(i, i ^ 1) for i in range(ny)])
    below_x = lax.ppermute(last, "gx", [(i, (i + 1) % nx) for i in range(nx)])
    fx, ux, wf, wl, part, edges, base_t = call(
        x_matrix_kernel,
        near(xs, xs, pitched, pitched, (6, NZ, BY), (4, GROUPS, 128), plane),
        near(st_t, kx, ky_t),
        [pltpu.VMEM(pitched, F32), pltpu.VMEM(xs, F32)],
        cost=5_000_000,
    )
    ends, flux = call(
        x_ends_kernel,
        near(x_block, (3, GROUPS, 128)),
        near(came1, came2, below_x, mine, part, edges),
        [pltpu.VMEM((2, NZ, BY), F32)],
    )
    other = lax.ppermute(ends, "gx", [(i, i ^ 1) for i in range(nx)])
    (d,) = call(
        x_local_kernel,
        near(pitched),
        near(base_t, flux, st, fx, ux),
        [pltpu.VMEM(pitched, F32), pltpu.VMEM(xs, F32), pltpu.VMEM(plane, F32)],
        cost=3_000_000,
    )
    chip, coefs = call(x_merge_kernel, near(x_block, (3, NZ, BY)), near(ends, other, d))
    def swap(axes, bits, value):
        return lax.ppermute(
            value,
            ("gx", "gy"),
            [
                (i * ny + j, (i ^ (2 * bits[i % 2])) * ny + j if axes == "x" else i * ny + (j ^ bits[i % 2]))
                for i in range(nx)
                for j in range(ny)
            ],
        )

    def share(value):
        return lax.ppermute(value, "gx", [(i, i ^ 1) for i in range(nx)])

    far = swap("x", (1, 2), chip)
    near_x = swap("x", (3, 3), chip)
    f, u, yf, yl, my = call(
        y_matrix_kernel,
        near(ys, ys, ys, ys, (3, GROUPS, 128)),
        near(ky_t, coefs),
        [pltpu.VMEM(ys, F32)],
        cost=5_000_000,
    )
    (relayed,) = call(relay_kernel, near(x_block), near(far, my))
    v_t, own = call(
        y_ends_kernel,
        near(plane, (5, GROUPS, 128)),
        near(chip, far, near_x, share(relayed), coefs, d, wf, wl, yf, yl, my, flux),
        [
            pltpu.VMEM((SIDE,) + x_block, F32),
            pltpu.VMEM((SIDE + 1, NZ, BY), F32),
            pltpu.VMEM((2, NZ, BY), F32),
        ],
    )
    (both,) = call(y_pack_kernel, near(wide), near(own, share(own)))
    far = swap("y", (1, 2), both)
    near_y = swap("y", (3, 3), both)
    (g_t,) = call(y_local_kernel, near(ys), near(v_t, f, u, both), cost=3_000_000)
    (relayed,) = call(relay_kernel, near(wide), near(far, g_t))
    quad, mine, coefs = call(
        y_merge_kernel,
        near(wide, (5, GROUPS, 128), (SIDE - 1, 3, 2 * GROUPS, 128)),
        near(both, far, near_y, share(relayed)),
        [pltpu.VMEM((SIDE,) + wide, F32)],
    )
    far = swap("y", (4, 8), quad)
    near_y = swap("y", (12, 12), mine)
    (picked,) = call(pick_kernel, near((5, GROUPS, 128)), near(far))
    (out,) = call(
        y_solve_kernel,
        [(plane, True)],
        near(mine, far, near_y, share(picked), coefs, g_t, yf, yl, st),
        [
            pltpu.VMEM((SIDE, 5, GROUPS, 128), F32),
            pltpu.VMEM((SIDE + 1, GROUPS, 128), F32),
            pltpu.VMEM((SIDE + 1, GROUPS, 128), F32),
            pltpu.VMEM(plane, F32),
            pltpu.VMEM(plane, F32),
            pltpu.SemaphoreType.DMA,
        ],
    )
    return out.reshape(state.shape)


def solution(mesh):
    spec = P(None, "gx", "gy")
    return jax.shard_map(
        on_device, mesh=mesh, in_specs=(spec, spec, spec), out_specs=spec, check_vma=False
    )
```

```python
import jax
import jax.numpy as jnp
from jax import lax
from jax.experimental import pallas as pl
from jax.experimental.pallas import tpu as pltpu
from jax.sharding import PartitionSpec as P

F32 = jnp.float32
NZ, BX, BY = 16, 64, 128
ROWS = NZ * BX
GROUPS = ROWS // 128
LIMIT = 8 * 1024 * 1024
SIDE = 4
PITCH = 72


def x_row(ref, i):
    return jnp.concatenate(
        [ref[pl.ds(i, 8, stride=PITCH), :], ref[pl.ds(8 * PITCH + i, 8, stride=PITCH), :]], axis=0
    )


def y_row(ref, j):
    return ref[pl.ds(j * GROUPS, GROUPS), :]


def place_rows(ref, i, value):
    ref[pl.ds(i, 8, stride=PITCH), :] = value[:8]
    ref[pl.ds(8 * PITCH + i, 8, stride=PITCH), :] = value[8:]


def group(ref, g):
    return jnp.concatenate([ref[pl.ds(z * PITCH, BX), :] for z in (2 * g, 2 * g + 1)], axis=0)


def place_group(ref, g, value):
    ref[pl.ds(2 * g * PITCH, BX), :] = value[:BX]
    ref[pl.ds((2 * g + 1) * PITCH, BX), :] = value[BX:]


def merge(low, high):
    inv = 1.0 / (low[2] + high[0])
    e = (low[4] - high[3]) * inv
    a = low[1] * inv
    b = high[1] * inv
    joined = [
        low[0] - low[1] * a,
        low[1] * b,
        high[2] - high[1] * b,
        low[3] - low[1] * e,
        high[4] + high[1] * e,
    ]
    return joined, (e, a, b)


def flows_of(count, pivot, lower, upper, gain, slots):
    half = (count + 1) // 2
    up, down = {}, {}
    for n in range(half + 1):
        i = n
        if i < half:
            gain_i, pivot_i = gain(i), pivot(i)
            if i:
                gain_i = gain_i + lower(i) * up[i - 1][0]
                pivot_i = pivot_i - lower(i) * up[i - 1][1]
            inv = (1.0 / (pivot_i))
            up[i] = gain_i * inv, upper(i) * inv
        i = count - n
        if i > half:
            gain_i, pivot_i = gain(i), pivot(i)
            if n:
                gain_i = gain_i + upper(i) * down[i + 1][0]
                pivot_i = pivot_i - upper(i) * down[i + 1][1]
            inv = (1.0 / (pivot_i))
            down[i] = gain_i * inv, lower(i) * inv
    below, above = up[half - 1], down[half + 1]
    low, high = lower(half), upper(half)
    flow = (gain(half) + low * below[0] + high * above[0]) * (1.0 / (
        pivot(half) - low * below[1] - high * above[1]
    ))
    slots[half] = flow
    rising = flow
    for n in range(1, half + 1):
        if half - n >= 0:
            flow = up[half - n][0] + up[half - n][1] * flow
            slots[half - n] = flow
        if half + n <= count:
            rising = down[half + n][0] + down[half + n][1] * rising
            slots[half + n] = rising


def arrange(own, far, near, shared, place, blocks):
    on_low = lax.rem(lax.axis_index("gx"), 2) == 0
    blocks[place] = own[...]
    blocks[place ^ 3] = near[...]
    blocks[place ^ 2] = jnp.where(on_low, shared[...], far[...])
    blocks[place ^ 1] = jnp.where(on_low, far[...], shared[...])


def line_flows(blocks, slots):
    count = blocks.shape[0]

    def pivot(i):
        if i == 0:
            return blocks[0, 0]
        return blocks[i - 1, 2] + blocks[i, 0] if i < count else blocks[i - 1, 2]

    def gain(i):
        if i == 0:
            return -blocks[0, 3]
        return blocks[i - 1, 4] - blocks[i, 3] if i < count else blocks[i - 1, 4]

    flows_of(count, pivot, lambda i: blocks[i - 1, 1], lambda i: blocks[i, 1], gain, slots)


def load_kernel(st_hbm, kx_hbm, ky_hbm, st, kx, st_t, ky_t, mine, first, second, last, ky, sems):
    inside = pl.ds(0, BX)
    moves = [
        pltpu.make_async_copy(src, dst, sems.at[n])
        for n, (src, dst) in enumerate(
            ((ky_hbm, ky), (st_hbm, st.at[:, inside, :]), (kx_hbm, kx.at[:, inside, :]))
        )
    ]
    for move in moves:
        move.start()
    moves[0].wait()
    for g in range(GROUPS):
        pair = jnp.concatenate([ky[2 * g], ky[2 * g + 1]], axis=0)
        ky_t[pl.ds(g, BY, stride=GROUPS), :] = pair.T
    moves[1].wait()
    for g in range(GROUPS):
        pair = jnp.concatenate([st[2 * g, inside, :], st[2 * g + 1, inside, :]], axis=0)
        st_t[pl.ds(g, BY, stride=GROUPS), :] = pair.T
    for n, ref in enumerate((st_t, ky_t)):
        mine[n] = y_row(ref, 0)
        mine[2 + n] = y_row(ref, BY - 1)
    even = lax.rem(lax.axis_index("gy"), 2) == 0
    low, high = mine[0:2], mine[2:4]
    first[...] = jnp.where(even, high, low)
    second[...] = jnp.where(even, low, high)
    moves[2].wait()
    for z in range(NZ):
        last[pl.ds(z, 1), :] = kx[z, pl.ds(BX - 1, 1), :]


def sweep(count, row, f, u, ratios, put_first, put_last):
    ahead = jnp.ones_like(row(0))
    back = jnp.ones_like(ahead)
    low, high = row(0), row(count - 1)
    for i in range(count - 1):
        nxt = row(i + 1)
        r = 0.5 * (low + nxt)
        low = nxt
        inv = (1.0 / (r + ahead))
        ratio = r * inv
        ahead = 1.0 + ratio * ahead
        u[i] = inv
        f[i] = ratio
        j = count - 1 - i
        prev = row(j - 1)
        r = 0.5 * (high + prev)
        high = prev
        ratio = r * (1.0 / (r + back))
        back = 1.0 + ratio * back
        ratios[j] = ratio
    start = (1.0 / (back))
    end = (1.0 / (ahead))
    lead, trail = start, end
    put_first(0, start)
    put_last(count - 1, end)
    u[count - 1] = end
    f[count - 1] = jnp.zeros_like(end)
    for i in range(1, count):
        start = start * ratios[i]
        put_first(i, start)
        j = count - 1 - i
        end = end * f[j]
        put_last(j, end)
    return lead, end, trail


def x_matrix_kernel(st_t, kx, ky_t, fx, ux, wf, wl, part, edges, base_t, source, ratios):
    here, k_here = y_row(st_t, 0), y_row(ky_t, 0)
    value = here
    for j in range(BY):
        if j < BY - 1:
            after, k_after = y_row(st_t, j + 1), y_row(ky_t, j + 1)
            flux = 0.5 * (k_here + k_after) * (after - here)
            value = value + flux
        base_t[pl.ds(j * GROUPS, GROUPS), :] = value
        here, k_here, value = after, k_after, after - flux
    for g in range(GROUPS):
        place_group(source, g, base_t[pl.ds(g, BY, stride=GROUPS), :].T)
    sums = [[jnp.zeros((NZ, BY), F32) for _ in range(2)] for _ in range(2)]

    def put(ref, total):
        def store(i, value):
            place_rows(ref, i, value)
            total[i % 2] = total[i % 2] + value * x_row(source, i)

        return store

    values = sweep(BX, lambda i: x_row(kx, i), fx, ux, ratios, put(wf, sums[0]), put(wl, sums[1]))
    lead, across, trail = values
    last = lax.axis_index("gx") == lax.axis_size("gx") - 1
    trail = trail + jnp.where(last, 2.0 / x_row(kx, BX - 1), 0.0)
    values = (lead, across, trail, sums[0][0] + sums[0][1], sums[1][0] + sums[1][1], x_row(kx, 0))
    for n, value in enumerate(values):
        part[n] = value
    for n, ref in enumerate((wf, wl)):
        for g in range(GROUPS):
            turned = group(ref, g).T
            edges[2 * n, pl.ds(g, 1), :] = turned[0:1, :]
            edges[2 * n + 1, pl.ds(g, 1), :] = turned[127:128, :]


def y_matrix_kernel(ky_t, after, f, u, yf, yl, my, ratios):
    def put(ref):
        def store(j, value):
            ref[j] = value

        return store

    me = lax.axis_index("gy")
    last = lax.axis_size("gy") - 1
    lead, across, trail = sweep(BY, lambda j: y_row(ky_t, j), f, u, ratios, put(yf), put(yl))
    my[0] = lead
    my[1] = across
    my[2] = trail + jnp.where(me == last, (2.0 / (y_row(ky_t, BY - 1))), 0.0)


def x_ends_kernel(came2, came1, below_x, mine, part, edges, send, flux, rows):
    me = lax.axis_index("gy")
    even = lax.rem(me, 2) == 0
    below = jnp.where(me == 0, 0.0, jnp.where(even, came2[...], came1[...]))
    above = jnp.where(me == lax.axis_size("gy") - 1, 0.0, jnp.where(even, came1[...], came2[...]))
    enter = 0.5 * (below[1] + mine[1]) * (mine[0] - below[0])
    leave = 0.5 * (above[1] + mine[3]) * (above[0] - mine[2])
    flux[0] = enter
    flux[1] = leave
    flux[2] = (2.0 / (below[1] + mine[1]))
    lane = lax.broadcasted_iota(jnp.int32, (GROUPS, 128), 1)
    below_x = jnp.where(lax.axis_index("gx") == 0, 0.0, below_x[...])
    send[0] = part[0] + 2.0 / (below_x + part[5])
    send[1:3] = part[1:3]
    for n in range(2):
        low = -edges[2 * n] * enter
        high = edges[2 * n + 1] * leave
        for h in range(2):
            inside = lane // BX == h
            at_low = jnp.sum(jnp.where(inside, low, 0.0), axis=1, keepdims=True)
            at_high = jnp.sum(jnp.where(inside, high, 0.0), axis=1, keepdims=True)
            value = jnp.where(lane == 0, at_low, jnp.where(lane == 127, at_high, 0.0))
            rows[n, pl.ds(h, GROUPS, stride=2), :] = value
        send[3 + n] = part[3 + n] + rows[n]


def x_local_kernel(base_t, flux, st, fx, ux, d, s, work, work_t):
    work_t[...] = base_t[...]
    work_t[pl.ds(0, GROUPS), :] = y_row(base_t, 0) - flux[0]
    work_t[pl.ds((BY - 1) * GROUPS, GROUPS), :] = y_row(base_t, BY - 1) + flux[1]
    for g in range(GROUPS):
        place_group(s, g, work_t[pl.ds(g, BY, stride=GROUPS), :].T)
    total = x_row(s, 0)
    work[0] = total
    for i in range(1, BX):
        total = x_row(s, i) + fx[i - 1] * total
        work[i] = total
    x = jnp.zeros_like(total)
    for i in range(BX - 1, -1, -1):
        x = ux[i] * work[i] + fx[i] * x
        place_rows(d, i, x - x_row(st, i))


def x_merge_kernel(own, other, after, send, coefs):
    core = lax.rem(lax.axis_index("gx"), 2)
    mine, theirs = [own[n] for n in range(5)], [other[n] for n in range(5)]
    low = [jnp.where(core == 0, a, b) for a, b in zip(mine, theirs)]
    high = [jnp.where(core == 0, b, a) for a, b in zip(mine, theirs)]
    joined, flow = merge(low, high)
    for n in range(5):
        send[n] = joined[n]
    for n in range(3):
        coefs[n] = flow[n]


def relay_kernel(value, after, out):
    out[...] = value[...]


def y_ends_kernel(
    own, far, near, shared, coefs, d, wf, wl, yf, yl, my, flux, v_t, send, blocks, slots, flows
):
    me = lax.axis_index("gx")
    place = lax.div(me, 2)
    on_low = lax.rem(me, 2) == 0
    arrange(own, far, near, shared, place, blocks)
    line_flows(blocks, slots)
    enter, leave = slots[place], slots[place + 1]
    middle = coefs[0] + coefs[1] * enter + coefs[2] * leave
    flows[0] = jnp.where(on_low, enter, middle)
    flows[1] = jnp.where(on_low, middle, leave)
    for g in range(GROUPS):
        parts = []
        for z in range(2 * g, 2 * g + 2):
            rows = pl.ds(z * PITCH, BX)
            parts.append(
                d[rows, :]
                + wf[rows, :] * flows[0, pl.ds(z, 1), :]
                - wl[rows, :] * flows[1, pl.ds(z, 1), :]
            )
        v_t[pl.ds(g, BY, stride=GROUPS), :] = jnp.concatenate(parts, axis=0).T
    firsts = [jnp.zeros((GROUPS, 128), F32) for _ in range(4)]
    lasts = [jnp.zeros((GROUPS, 128), F32) for _ in range(4)]
    for j in range(BY):
        row = y_row(v_t, j)
        firsts[j % 4] = firsts[j % 4] + yf[j] * row
        lasts[j % 4] = lasts[j % 4] + yl[j] * row
    first = (firsts[0] + firsts[1]) + (firsts[2] + firsts[3])
    last = (lasts[0] + lasts[1]) + (lasts[2] + lasts[3])
    send[0] = my[0] + flux[2]
    send[1:3] = my[1:3]
    send[3] = first
    send[4] = last


def y_pack_kernel(own, other, after, both):
    on_low = lax.rem(lax.axis_index("gx"), 2) == 0
    both[:, 0:GROUPS] = jnp.where(on_low, own[...], other[...])
    both[:, GROUPS : 2 * GROUPS] = jnp.where(on_low, other[...], own[...])


def y_local_kernel(v_t, f, u, g_t):
    total = y_row(v_t, 0)
    g_t[0] = total
    for j in range(1, BY):
        total = y_row(v_t, j) + f[j - 1] * total
        g_t[j] = total
    x = jnp.zeros_like(total)
    for j in range(BY - 1, -1, -1):
        x = u[j] * g_t[j] + f[j] * x
        g_t[j] = x


def own_rows():
    start = lax.rem(lax.axis_index("gx"), 2) * GROUPS
    return pl.ds(pl.multiple_of(start, GROUPS), GROUPS)


def other_rows():
    start = (1 - lax.rem(lax.axis_index("gx"), 2)) * GROUPS
    return pl.ds(pl.multiple_of(start, GROUPS), GROUPS)


def pick_kernel(value, out):
    out[...] = value[:, other_rows(), :]


def y_merge_kernel(own, far, near, shared, quad, mine, coefs, blocks):
    arrange(own, far, near, shared, lax.rem(lax.axis_index("gy"), SIDE), blocks)
    joined = [blocks[0, n] for n in range(5)]
    for c in range(1, SIDE):
        joined, flow = merge(joined, [blocks[c, n] for n in range(5)])
        for n in range(3):
            coefs[c - 1, n] = flow[n]
    for n in range(5):
        quad[n] = joined[n]
    mine[...] = quad[:, own_rows(), :]


def y_solve_kernel(
    mine, far, near, shared, coefs, g_t, yf, yl, st, out_hbm, blocks, slots, inner, work, out, sem
):
    me = lax.axis_index("gy")
    place, depth = lax.div(me, SIDE), lax.rem(me, SIDE)
    rows = own_rows()
    arrange(mine, far.at[:, rows, :], near, shared, place, blocks)
    line_flows(blocks, slots)
    enter, flow = slots[place], slots[place + 1]
    inner[0] = enter
    inner[SIDE] = flow
    for c in range(SIDE - 1, 0, -1):
        e, a, b = [coefs[c - 1, n, rows, :] for n in range(3)]
        flow = e + a * enter + b * flow
        inner[c] = flow
    enter, leave = inner[depth], inner[depth + 1]
    for j in range(BY):
        work[pl.ds(j * GROUPS, GROUPS), :] = 2.0 * (g_t[j] + yf[j] * enter - yl[j] * leave)
    for g in range(GROUPS):
        rows = pl.ds(g * 128, 128)
        out[rows, :] = group(st, g) + work[pl.ds(g, BY, stride=GROUPS), :].T
        pltpu.make_async_copy(out.at[rows], out_hbm.at[rows], sem).start()
    pltpu.make_async_copy(out, out_hbm, sem).wait()


def call(kernel, outs, args, scratch=(), cost=100_000):
    vm = pl.BlockSpec(memory_space=pltpu.VMEM)
    hbm = pl.BlockSpec(memory_space=pltpu.HBM)
    return pl.pallas_call(
        kernel,
        out_shape=[
            jax.ShapeDtypeStruct(shape, F32) if far else pltpu.VMEM(shape, F32)
            for shape, far in outs
        ],
        in_specs=[hbm if far else vm for _, far in args],
        out_specs=[hbm if far else vm for _, far in outs],
        scratch_shapes=list(scratch),
        compiler_params=pltpu.CompilerParams(vmem_limit_bytes=LIMIT),
        cost_estimate=pl.CostEstimate(flops=cost, bytes_accessed=cost, transcendentals=0),
    )(*[value for value, _ in args])


def near(*values):
    return [(value, False) for value in values]


def on_device(state, kappa_x, kappa_y):
    flat = [
        pltpu.with_memory_space_constraint(a, pltpu.HBM) for a in (state, kappa_x, kappa_y)
    ]
    plane = (ROWS, BY)
    pitched = (NZ * PITCH, BY)
    planes = (NZ, PITCH, BY)
    xs = (BX, NZ, BY)
    ys = (BY, GROUPS, 128)
    x_block = (5, NZ, BY)
    edge = (2, GROUPS, 128)
    nx, ny = lax.axis_size("gx"), lax.axis_size("gy")
    wide = (5, 2 * GROUPS, 128)
    st, kx, st_t, ky_t, mine, first, second, last = call(
        load_kernel,
        near(planes, planes, plane, plane, (4, GROUPS, 128), edge, edge, (NZ, BY)),
        [(a, True) for a in flat],
        [pltpu.VMEM((NZ, BX, BY), F32), pltpu.SemaphoreType.DMA((3,))],
    )
    st, kx = st.reshape(pitched), kx.reshape(pitched)
    pairs = [
        (i * ny + j, i * ny + j + 2 * (j % 2) - 1 if 0 < j < ny - 1 else (i ^ 1) * ny + j)
        for i in range(nx)
        for j in range(ny)
    ]
    came2 = lax.ppermute(second, ("gx", "gy"), pairs)
    came1 = lax.ppermute(first, "gy", [(i, i ^ 1) for i in range(ny)])
    below_x = lax.ppermute(last, "gx", [(i, (i + 1) % nx) for i in range(nx)])
    fx, ux, wf, wl, part, edges, base_t = call(
        x_matrix_kernel,
        near(xs, xs, pitched, pitched, (6, NZ, BY), (4, GROUPS, 128), plane),
        near(st_t, kx, ky_t),
        [pltpu.VMEM(pitched, F32), pltpu.VMEM(xs, F32)],
        cost=5_000_000,
    )
    ends, flux = call(
        x_ends_kernel,
        near(x_block, (3, GROUPS, 128)),
        near(came2, came1, below_x, mine, part, edges),
        [pltpu.VMEM((2, NZ, BY), F32)],
    )
    other = lax.ppermute(ends, "gx", [(i, i ^ 1) for i in range(nx)])
    (d,) = call(
        x_local_kernel,
        near(pitched),
        near(base_t, flux, st, fx, ux),
        [pltpu.VMEM(pitched, F32), pltpu.VMEM(xs, F32), pltpu.VMEM(plane, F32)],
        cost=3_000_000,
    )
    chip, coefs = call(x_merge_kernel, near(x_block, (3, NZ, BY)), near(ends, other, d))
    def swap(axes, bits, value):
        return lax.ppermute(
            value,
            ("gx", "gy"),
            [
                (i * ny + j, (i ^ (2 * bits[i % 2])) * ny + j if axes == "x" else i * ny + (j ^ bits[i % 2]))
                for i in range(nx)
                for j in range(ny)
            ],
        )

    def share(value):
        return lax.ppermute(value, "gx", [(i, i ^ 1) for i in range(nx)])

    far = swap("x", (1, 2), chip)
    near_x = swap("x", (3, 3), chip)
    f, u, yf, yl, my = call(
        y_matrix_kernel,
        near(ys, ys, ys, ys, (3, GROUPS, 128)),
        near(ky_t, coefs),
        [pltpu.VMEM(ys, F32)],
        cost=5_000_000,
    )
    (relayed,) = call(relay_kernel, near(x_block), near(far, my))
    v_t, own = call(
        y_ends_kernel,
        near(plane, (5, GROUPS, 128)),
        near(chip, far, near_x, share(relayed), coefs, d, wf, wl, yf, yl, my, flux),
        [
            pltpu.VMEM((SIDE,) + x_block, F32),
            pltpu.VMEM((SIDE + 1, NZ, BY), F32),
            pltpu.VMEM((2, NZ, BY), F32),
        ],
    )
    (g_t,) = call(y_local_kernel, near(ys), near(v_t, f, u), cost=3_000_000)
    (both,) = call(y_pack_kernel, near(wide), near(own, share(own), g_t))
    far = swap("y", (1, 2), both)
    near_y = swap("y", (3, 3), both)
    quad, mine, coefs = call(
        y_merge_kernel,
        near(wide, (5, GROUPS, 128), (SIDE - 1, 3, 2 * GROUPS, 128)),
        near(both, far, near_y, share(far)),
        [pltpu.VMEM((SIDE,) + wide, F32)],
    )
    far = swap("y", (4, 8), quad)
    near_y = swap("y", (12, 12), mine)
    (picked,) = call(pick_kernel, near((5, GROUPS, 128)), near(far))
    (out,) = call(
        y_solve_kernel,
        [(plane, True)],
        near(mine, far, near_y, share(picked), coefs, g_t, yf, yl, st),
        [
            pltpu.VMEM((SIDE, 5, GROUPS, 128), F32),
            pltpu.VMEM((SIDE + 1, GROUPS, 128), F32),
            pltpu.VMEM((SIDE + 1, GROUPS, 128), F32),
            pltpu.VMEM(plane, F32),
            pltpu.VMEM(plane, F32),
            pltpu.SemaphoreType.DMA,
        ],
    )
    return out.reshape(state.shape)


def solution(mesh):
    spec = P(None, "gx", "gy")
    return jax.shard_map(
        on_device, mesh=mesh, in_specs=(spec, spec, spec), out_specs=spec, check_vma=False
    )
```

```python
import jax
import jax.numpy as jnp
from jax import lax
from jax.experimental import pallas as pl
from jax.experimental.pallas import tpu as pltpu
from jax.sharding import PartitionSpec as P

F32 = jnp.float32
NZ, BX, BY = 16, 64, 128
ROWS = NZ * BX
GROUPS = ROWS // 128
LIMIT = 8 * 1024 * 1024
SIDE = 4
PITCH = 72


def x_row(ref, i):
    return jnp.concatenate(
        [ref[pl.ds(i, 8, stride=PITCH), :], ref[pl.ds(8 * PITCH + i, 8, stride=PITCH), :]], axis=0
    )


def y_row(ref, j):
    return ref[pl.ds(j * GROUPS, GROUPS), :]


def place_rows(ref, i, value):
    ref[pl.ds(i, 8, stride=PITCH), :] = value[:8]
    ref[pl.ds(8 * PITCH + i, 8, stride=PITCH), :] = value[8:]


def group(ref, g):
    return jnp.concatenate([ref[pl.ds(z * PITCH, BX), :] for z in (2 * g, 2 * g + 1)], axis=0)


def place_group(ref, g, value):
    ref[pl.ds(2 * g * PITCH, BX), :] = value[:BX]
    ref[pl.ds((2 * g + 1) * PITCH, BX), :] = value[BX:]


def merge(low, high):
    inv = 1.0 / (low[2] + high[0])
    e = (low[4] - high[3]) * inv
    a = low[1] * inv
    b = high[1] * inv
    joined = [
        low[0] - low[1] * a,
        low[1] * b,
        high[2] - high[1] * b,
        low[3] - low[1] * e,
        high[4] + high[1] * e,
    ]
    return joined, (e, a, b)


def flows_of(count, pivot, lower, upper, gain, slots):
    half = (count + 1) // 2
    up, down = {}, {}
    for n in range(half + 1):
        i = n
        if i < half:
            gain_i, pivot_i = gain(i), pivot(i)
            if i:
                gain_i = gain_i + lower(i) * up[i - 1][0]
                pivot_i = pivot_i - lower(i) * up[i - 1][1]
            inv = (1.0 / (pivot_i))
            up[i] = gain_i * inv, upper(i) * inv
        i = count - n
        if i > half:
            gain_i, pivot_i = gain(i), pivot(i)
            if n:
                gain_i = gain_i + upper(i) * down[i + 1][0]
                pivot_i = pivot_i - upper(i) * down[i + 1][1]
            inv = (1.0 / (pivot_i))
            down[i] = gain_i * inv, lower(i) * inv
    below, above = up[half - 1], down[half + 1]
    low, high = lower(half), upper(half)
    flow = (gain(half) + low * below[0] + high * above[0]) * (1.0 / (
        pivot(half) - low * below[1] - high * above[1]
    ))
    slots[half] = flow
    rising = flow
    for n in range(1, half + 1):
        if half - n >= 0:
            flow = up[half - n][0] + up[half - n][1] * flow
            slots[half - n] = flow
        if half + n <= count:
            rising = down[half + n][0] + down[half + n][1] * rising
            slots[half + n] = rising


def arrange(own, far, near, shared, place, blocks):
    on_low = lax.rem(lax.axis_index("gx"), 2) == 0
    blocks[place] = own[...]
    blocks[place ^ 3] = near[...]
    blocks[place ^ 2] = jnp.where(on_low, shared[...], far[...])
    blocks[place ^ 1] = jnp.where(on_low, far[...], shared[...])


def line_flows(blocks, slots):
    count = blocks.shape[0]

    def pivot(i):
        if i == 0:
            return blocks[0, 0]
        return blocks[i - 1, 2] + blocks[i, 0] if i < count else blocks[i - 1, 2]

    def gain(i):
        if i == 0:
            return -blocks[0, 3]
        return blocks[i - 1, 4] - blocks[i, 3] if i < count else blocks[i - 1, 4]

    flows_of(count, pivot, lambda i: blocks[i - 1, 1], lambda i: blocks[i, 1], gain, slots)


def load_kernel(st_hbm, kx_hbm, ky_hbm, st, kx, st_t, ky_t, mine, first, second, last, ky, sems):
    inside = pl.ds(0, BX)
    moves = [
        pltpu.make_async_copy(src, dst, sems.at[n])
        for n, (src, dst) in enumerate(
            ((ky_hbm, ky), (st_hbm, st.at[:, inside, :]), (kx_hbm, kx.at[:, inside, :]))
        )
    ]
    for move in moves:
        move.start()
    moves[0].wait()
    for g in range(GROUPS):
        pair = jnp.concatenate([ky[2 * g], ky[2 * g + 1]], axis=0)
        ky_t[pl.ds(g, BY, stride=GROUPS), :] = pair.T
    moves[1].wait()
    for g in range(GROUPS):
        pair = jnp.concatenate([st[2 * g, inside, :], st[2 * g + 1, inside, :]], axis=0)
        st_t[pl.ds(g, BY, stride=GROUPS), :] = pair.T
    for n, ref in enumerate((st_t, ky_t)):
        mine[n] = y_row(ref, 0)
        mine[2 + n] = y_row(ref, BY - 1)
    even = lax.rem(lax.axis_index("gy"), 2) == 0
    low, high = mine[0:2], mine[2:4]
    first[...] = jnp.where(even, high, low)
    second[...] = jnp.where(even, low, high)
    moves[2].wait()
    for z in range(NZ):
        last[pl.ds(z, 1), :] = kx[z, pl.ds(BX - 1, 1), :]


def sweep(count, row, f, u, ratios, put_first, put_last):
    ahead = jnp.ones_like(row(0))
    back = jnp.ones_like(ahead)
    low, high = row(0), row(count - 1)
    for i in range(count - 1):
        nxt = row(i + 1)
        r = 0.5 * (low + nxt)
        low = nxt
        inv = (1.0 / (r + ahead))
        ratio = r * inv
        ahead = 1.0 + ratio * ahead
        u[i] = inv
        f[i] = ratio
        j = count - 1 - i
        prev = row(j - 1)
        r = 0.5 * (high + prev)
        high = prev
        ratio = r * (1.0 / (r + back))
        back = 1.0 + ratio * back
        ratios[j] = ratio
    start = (1.0 / (back))
    end = (1.0 / (ahead))
    lead, trail = start, end
    put_first(0, start)
    put_last(count - 1, end)
    u[count - 1] = end
    f[count - 1] = jnp.zeros_like(end)
    for i in range(1, count):
        start = start * ratios[i]
        put_first(i, start)
        j = count - 1 - i
        end = end * f[j]
        put_last(j, end)
    return lead, end, trail


def x_matrix_kernel(st_t, kx, ky_t, fx, ux, wf, wl, part, edges, base_t, source, ratios):
    here, k_here = y_row(st_t, 0), y_row(ky_t, 0)
    value = here
    for j in range(BY):
        if j < BY - 1:
            after, k_after = y_row(st_t, j + 1), y_row(ky_t, j + 1)
            flux = 0.5 * (k_here + k_after) * (after - here)
            value = value + flux
        base_t[pl.ds(j * GROUPS, GROUPS), :] = value
        here, k_here, value = after, k_after, after - flux
    for g in range(GROUPS):
        place_group(source, g, base_t[pl.ds(g, BY, stride=GROUPS), :].T)
    sums = [[jnp.zeros((NZ, BY), F32) for _ in range(2)] for _ in range(2)]

    def put(ref, total):
        def store(i, value):
            place_rows(ref, i, value)
            total[i % 2] = total[i % 2] + value * x_row(source, i)

        return store

    values = sweep(BX, lambda i: x_row(kx, i), fx, ux, ratios, put(wf, sums[0]), put(wl, sums[1]))
    lead, across, trail = values
    last = lax.axis_index("gx") == lax.axis_size("gx") - 1
    trail = trail + jnp.where(last, 2.0 / x_row(kx, BX - 1), 0.0)
    values = (lead, across, trail, sums[0][0] + sums[0][1], sums[1][0] + sums[1][1], x_row(kx, 0))
    for n, value in enumerate(values):
        part[n] = value
    for n, ref in enumerate((wf, wl)):
        for g in range(GROUPS):
            turned = group(ref, g).T
            edges[2 * n, pl.ds(g, 1), :] = turned[0:1, :]
            edges[2 * n + 1, pl.ds(g, 1), :] = turned[127:128, :]


def y_matrix_kernel(ky_t, after, f, u, yf, yl, my, ratios):
    def put(ref):
        def store(j, value):
            ref[j] = value

        return store

    me = lax.axis_index("gy")
    last = lax.axis_size("gy") - 1
    lead, across, trail = sweep(BY, lambda j: y_row(ky_t, j), f, u, ratios, put(yf), put(yl))
    my[0] = lead
    my[1] = across
    my[2] = trail + jnp.where(me == last, (2.0 / (y_row(ky_t, BY - 1))), 0.0)


def x_ends_kernel(came2, below_x, came1, mine, part, edges, send, flux, rows):
    me = lax.axis_index("gy")
    even = lax.rem(me, 2) == 0
    below = jnp.where(me == 0, 0.0, jnp.where(even, came2[...], came1[...]))
    above = jnp.where(me == lax.axis_size("gy") - 1, 0.0, jnp.where(even, came1[...], came2[...]))
    enter = 0.5 * (below[1] + mine[1]) * (mine[0] - below[0])
    leave = 0.5 * (above[1] + mine[3]) * (above[0] - mine[2])
    flux[0] = enter
    flux[1] = leave
    flux[2] = (2.0 / (below[1] + mine[1]))
    lane = lax.broadcasted_iota(jnp.int32, (GROUPS, 128), 1)
    below_x = jnp.where(lax.axis_index("gx") == 0, 0.0, below_x[...])
    send[0] = part[0] + 2.0 / (below_x + part[5])
    send[1:3] = part[1:3]
    for n in range(2):
        low = -edges[2 * n] * enter
        high = edges[2 * n + 1] * leave
        for h in range(2):
            inside = lane // BX == h
            at_low = jnp.sum(jnp.where(inside, low, 0.0), axis=1, keepdims=True)
            at_high = jnp.sum(jnp.where(inside, high, 0.0), axis=1, keepdims=True)
            value = jnp.where(lane == 0, at_low, jnp.where(lane == 127, at_high, 0.0))
            rows[n, pl.ds(h, GROUPS, stride=2), :] = value
        send[3 + n] = part[3 + n] + rows[n]


def x_local_kernel(base_t, flux, st, fx, ux, d, s, work, work_t):
    work_t[...] = base_t[...]
    work_t[pl.ds(0, GROUPS), :] = y_row(base_t, 0) - flux[0]
    work_t[pl.ds((BY - 1) * GROUPS, GROUPS), :] = y_row(base_t, BY - 1) + flux[1]
    for g in range(GROUPS):
        place_group(s, g, work_t[pl.ds(g, BY, stride=GROUPS), :].T)
    total = x_row(s, 0)
    work[0] = total
    for i in range(1, BX):
        total = x_row(s, i) + fx[i - 1] * total
        work[i] = total
    x = jnp.zeros_like(total)
    for i in range(BX - 1, -1, -1):
        x = ux[i] * work[i] + fx[i] * x
        place_rows(d, i, x - x_row(st, i))


def x_merge_kernel(own, other, after, send, coefs):
    core = lax.rem(lax.axis_index("gx"), 2)
    mine, theirs = [own[n] for n in range(5)], [other[n] for n in range(5)]
    low = [jnp.where(core == 0, a, b) for a, b in zip(mine, theirs)]
    high = [jnp.where(core == 0, b, a) for a, b in zip(mine, theirs)]
    joined, flow = merge(low, high)
    for n in range(5):
        send[n] = joined[n]
    for n in range(3):
        coefs[n] = flow[n]


def relay_kernel(value, after, out):
    out[...] = value[...]


def y_ends_kernel(
    own, far, near, shared, coefs, d, wf, wl, yf, yl, my, flux, v_t, send, blocks, slots, flows
):
    me = lax.axis_index("gx")
    place = lax.div(me, 2)
    on_low = lax.rem(me, 2) == 0
    arrange(own, far, near, shared, place, blocks)
    line_flows(blocks, slots)
    enter, leave = slots[place], slots[place + 1]
    middle = coefs[0] + coefs[1] * enter + coefs[2] * leave
    flows[0] = jnp.where(on_low, enter, middle)
    flows[1] = jnp.where(on_low, middle, leave)
    for g in range(GROUPS):
        parts = []
        for z in range(2 * g, 2 * g + 2):
            rows = pl.ds(z * PITCH, BX)
            parts.append(
                d[rows, :]
                + wf[rows, :] * flows[0, pl.ds(z, 1), :]
                - wl[rows, :] * flows[1, pl.ds(z, 1), :]
            )
        v_t[pl.ds(g, BY, stride=GROUPS), :] = jnp.concatenate(parts, axis=0).T
    firsts = [jnp.zeros((GROUPS, 128), F32) for _ in range(4)]
    lasts = [jnp.zeros((GROUPS, 128), F32) for _ in range(4)]
    for j in range(BY):
        row = y_row(v_t, j)
        firsts[j % 4] = firsts[j % 4] + yf[j] * row
        lasts[j % 4] = lasts[j % 4] + yl[j] * row
    first = (firsts[0] + firsts[1]) + (firsts[2] + firsts[3])
    last = (lasts[0] + lasts[1]) + (lasts[2] + lasts[3])
    send[0] = my[0] + flux[2]
    send[1:3] = my[1:3]
    send[3] = first
    send[4] = last


def y_pack_kernel(own, other, after, both):
    on_low = lax.rem(lax.axis_index("gx"), 2) == 0
    both[:, 0:GROUPS] = jnp.where(on_low, own[...], other[...])
    both[:, GROUPS : 2 * GROUPS] = jnp.where(on_low, other[...], own[...])


def y_local_kernel(v_t, f, u, g_t):
    total = y_row(v_t, 0)
    g_t[0] = total
    for j in range(1, BY):
        total = y_row(v_t, j) + f[j - 1] * total
        g_t[j] = total
    x = jnp.zeros_like(total)
    for j in range(BY - 1, -1, -1):
        x = u[j] * g_t[j] + f[j] * x
        g_t[j] = x


def own_rows():
    start = lax.rem(lax.axis_index("gx"), 2) * GROUPS
    return pl.ds(pl.multiple_of(start, GROUPS), GROUPS)


def other_rows():
    start = (1 - lax.rem(lax.axis_index("gx"), 2)) * GROUPS
    return pl.ds(pl.multiple_of(start, GROUPS), GROUPS)


def pick_kernel(value, out):
    out[...] = value[:, other_rows(), :]


def y_merge_kernel(own, far, near, shared, quad, mine, coefs, blocks):
    arrange(own, far, near, shared, lax.rem(lax.axis_index("gy"), SIDE), blocks)
    joined = [blocks[0, n] for n in range(5)]
    for c in range(1, SIDE):
        joined, flow = merge(joined, [blocks[c, n] for n in range(5)])
        for n in range(3):
            coefs[c - 1, n] = flow[n]
    for n in range(5):
        quad[n] = joined[n]
    mine[...] = quad[:, own_rows(), :]


def y_solve_kernel(
    mine, far, near, shared, coefs, g_t, yf, yl, st, out_hbm, blocks, slots, inner, work, out, sem
):
    me = lax.axis_index("gy")
    place, depth = lax.div(me, SIDE), lax.rem(me, SIDE)
    rows = own_rows()
    arrange(mine, far.at[:, rows, :], near, shared, place, blocks)
    line_flows(blocks, slots)
    enter, flow = slots[place], slots[place + 1]
    inner[0] = enter
    inner[SIDE] = flow
    for c in range(SIDE - 1, 0, -1):
        e, a, b = [coefs[c - 1, n, rows, :] for n in range(3)]
        flow = e + a * enter + b * flow
        inner[c] = flow
    enter, leave = inner[depth], inner[depth + 1]
    for j in range(BY):
        work[pl.ds(j * GROUPS, GROUPS), :] = 2.0 * (g_t[j] + yf[j] * enter - yl[j] * leave)
    for g in range(GROUPS):
        rows = pl.ds(g * 128, 128)
        out[rows, :] = group(st, g) + work[pl.ds(g, BY, stride=GROUPS), :].T
        pltpu.make_async_copy(out.at[rows], out_hbm.at[rows], sem).start()
    pltpu.make_async_copy(out, out_hbm, sem).wait()


def call(kernel, outs, args, scratch=(), cost=100_000):
    vm = pl.BlockSpec(memory_space=pltpu.VMEM)
    hbm = pl.BlockSpec(memory_space=pltpu.HBM)
    return pl.pallas_call(
        kernel,
        out_shape=[
            jax.ShapeDtypeStruct(shape, F32) if far else pltpu.VMEM(shape, F32)
            for shape, far in outs
        ],
        in_specs=[hbm if far else vm for _, far in args],
        out_specs=[hbm if far else vm for _, far in outs],
        scratch_shapes=list(scratch),
        compiler_params=pltpu.CompilerParams(vmem_limit_bytes=LIMIT),
        cost_estimate=pl.CostEstimate(flops=cost, bytes_accessed=cost, transcendentals=0),
    )(*[value for value, _ in args])


def near(*values):
    return [(value, False) for value in values]


def on_device(state, kappa_x, kappa_y):
    flat = [
        pltpu.with_memory_space_constraint(a, pltpu.HBM) for a in (state, kappa_x, kappa_y)
    ]
    plane = (ROWS, BY)
    pitched = (NZ * PITCH, BY)
    planes = (NZ, PITCH, BY)
    xs = (BX, NZ, BY)
    ys = (BY, GROUPS, 128)
    x_block = (5, NZ, BY)
    edge = (2, GROUPS, 128)
    nx, ny = lax.axis_size("gx"), lax.axis_size("gy")
    wide = (5, 2 * GROUPS, 128)
    st, kx, st_t, ky_t, mine, first, second, last = call(
        load_kernel,
        near(planes, planes, plane, plane, (4, GROUPS, 128), edge, edge, (NZ, BY)),
        [(a, True) for a in flat],
        [pltpu.VMEM((NZ, BX, BY), F32), pltpu.SemaphoreType.DMA((3,))],
    )
    st, kx = st.reshape(pitched), kx.reshape(pitched)
    pairs = [
        (i * ny + j, i * ny + j + 2 * (j % 2) - 1 if 0 < j < ny - 1 else (i ^ 1) * ny + j)
        for i in range(nx)
        for j in range(ny)
    ]
    came2 = lax.ppermute(second, ("gx", "gy"), pairs)
    came1 = lax.ppermute(first, "gy", [(i, i ^ 1) for i in range(ny)])
    below_x = lax.ppermute(last, "gx", [(i, (i + 1) % nx) for i in range(nx)])
    fx, ux, wf, wl, part, edges, base_t = call(
        x_matrix_kernel,
        near(xs, xs, pitched, pitched, (6, NZ, BY), (4, GROUPS, 128), plane),
        near(st_t, kx, ky_t),
        [pltpu.VMEM(pitched, F32), pltpu.VMEM(xs, F32)],
        cost=5_000_000,
    )
    ends, flux = call(
        x_ends_kernel,
        near(x_block, (3, GROUPS, 128)),
        near(came2, below_x, came1, mine, part, edges),
        [pltpu.VMEM((2, NZ, BY), F32)],
    )
    other = lax.ppermute(ends, "gx", [(i, i ^ 1) for i in range(nx)])
    (d,) = call(
        x_local_kernel,
        near(pitched),
        near(base_t, flux, st, fx, ux),
        [pltpu.VMEM(pitched, F32), pltpu.VMEM(xs, F32), pltpu.VMEM(plane, F32)],
        cost=3_000_000,
    )
    chip, coefs = call(x_merge_kernel, near(x_block, (3, NZ, BY)), near(ends, other, d))
    def swap(axes, bits, value):
        return lax.ppermute(
            value,
            ("gx", "gy"),
            [
                (i * ny + j, (i ^ (2 * bits[i % 2])) * ny + j if axes == "x" else i * ny + (j ^ bits[i % 2]))
                for i in range(nx)
                for j in range(ny)
            ],
        )

    def share(value):
        return lax.ppermute(value, "gx", [(i, i ^ 1) for i in range(nx)])

    far = swap("x", (1, 2), chip)
    near_x = swap("x", (3, 3), chip)
    f, u, yf, yl, my = call(
        y_matrix_kernel,
        near(ys, ys, ys, ys, (3, GROUPS, 128)),
        near(ky_t, coefs),
        [pltpu.VMEM(ys, F32)],
        cost=5_000_000,
    )
    (relayed,) = call(relay_kernel, near(x_block), near(far, my))
    v_t, own = call(
        y_ends_kernel,
        near(plane, (5, GROUPS, 128)),
        near(chip, far, near_x, share(relayed), coefs, d, wf, wl, yf, yl, my, flux),
        [
            pltpu.VMEM((SIDE,) + x_block, F32),
            pltpu.VMEM((SIDE + 1, NZ, BY), F32),
            pltpu.VMEM((2, NZ, BY), F32),
        ],
    )
    (g_t,) = call(y_local_kernel, near(ys), near(v_t, f, u), cost=3_000_000)
    (both,) = call(y_pack_kernel, near(wide), near(own, share(own), g_t))
    far = swap("y", (1, 2), both)
    near_y = swap("y", (3, 3), both)
    quad, mine, coefs = call(
        y_merge_kernel,
        near(wide, (5, GROUPS, 128), (SIDE - 1, 3, 2 * GROUPS, 128)),
        near(both, far, near_y, share(far)),
        [pltpu.VMEM((SIDE,) + wide, F32)],
    )
    far = swap("y", (4, 8), quad)
    near_y = swap("y", (12, 12), mine)
    (picked,) = call(pick_kernel, near((5, GROUPS, 128)), near(far))
    (out,) = call(
        y_solve_kernel,
        [(plane, True)],
        near(mine, far, near_y, share(picked), coefs, g_t, yf, yl, st),
        [
            pltpu.VMEM((SIDE, 5, GROUPS, 128), F32),
            pltpu.VMEM((SIDE + 1, GROUPS, 128), F32),
            pltpu.VMEM((SIDE + 1, GROUPS, 128), F32),
            pltpu.VMEM(plane, F32),
            pltpu.VMEM(plane, F32),
            pltpu.SemaphoreType.DMA,
        ],
    )
    return out.reshape(state.shape)


def solution(mesh):
    spec = P(None, "gx", "gy")
    return jax.shard_map(
        on_device, mesh=mesh, in_specs=(spec, spec, spec), out_specs=spec, check_vma=False
    )
```

```python
import jax
import jax.numpy as jnp
from jax import lax
from jax.experimental import pallas as pl
from jax.experimental.pallas import tpu as pltpu
from jax.sharding import PartitionSpec as P

F32 = jnp.float32
NZ, BX, BY = 16, 64, 128
ROWS = NZ * BX
GROUPS = ROWS // 128
LIMIT = 8 * 1024 * 1024
SIDE = 4
PITCH = 72


def x_row(ref, i):
    return jnp.concatenate(
        [ref[pl.ds(i, 8, stride=PITCH), :], ref[pl.ds(8 * PITCH + i, 8, stride=PITCH), :]], axis=0
    )


def y_row(ref, j):
    return ref[pl.ds(j * GROUPS, GROUPS), :]


def place_rows(ref, i, value):
    ref[pl.ds(i, 8, stride=PITCH), :] = value[:8]
    ref[pl.ds(8 * PITCH + i, 8, stride=PITCH), :] = value[8:]


def group(ref, g):
    return jnp.concatenate([ref[pl.ds(z * PITCH, BX), :] for z in (2 * g, 2 * g + 1)], axis=0)


def place_group(ref, g, value):
    ref[pl.ds(2 * g * PITCH, BX), :] = value[:BX]
    ref[pl.ds((2 * g + 1) * PITCH, BX), :] = value[BX:]


def merge(low, high):
    inv = (1.0 / ((2.0 / (low[4] + high[3])) + low[2] + high[0]))
    e = (low[6] - high[5]) * inv
    a = low[1] * inv
    b = high[1] * inv
    joined = [
        low[0] - low[1] * a,
        low[1] * b,
        high[2] - high[1] * b,
        low[3],
        high[4],
        low[5] - low[1] * e,
        high[6] + high[1] * e,
    ]
    return joined, (e, a, b)


def flows_of(count, pivot, lower, upper, gain, slots):
    half = (count + 1) // 2
    up, down = {}, {}
    for n in range(half + 1):
        i = n
        if i < half:
            gain_i, pivot_i = gain(i), pivot(i)
            if i:
                gain_i = gain_i + lower(i) * up[i - 1][0]
                pivot_i = pivot_i - lower(i) * up[i - 1][1]
            inv = (1.0 / (pivot_i))
            up[i] = gain_i * inv, upper(i) * inv
        i = count - n
        if i > half:
            gain_i, pivot_i = gain(i), pivot(i)
            if n:
                gain_i = gain_i + upper(i) * down[i + 1][0]
                pivot_i = pivot_i - upper(i) * down[i + 1][1]
            inv = (1.0 / (pivot_i))
            down[i] = gain_i * inv, lower(i) * inv
    below, above = up[half - 1], down[half + 1]
    low, high = lower(half), upper(half)
    flow = (gain(half) + low * below[0] + high * above[0]) * (1.0 / (
        pivot(half) - low * below[1] - high * above[1]
    ))
    slots[half] = flow
    rising = flow
    for n in range(1, half + 1):
        if half - n >= 0:
            flow = up[half - n][0] + up[half - n][1] * flow
            slots[half - n] = flow
        if half + n <= count:
            rising = down[half + n][0] + down[half + n][1] * rising
            slots[half + n] = rising


def x_flows(blocks, slots):
    count = blocks.shape[0]

    def pivot(i):
        if i == 0:
            return (2.0 / (blocks[0, 3])) + blocks[0, 0]
        if i == count:
            return (2.0 / (blocks[count - 1, 4])) + blocks[count - 1, 2]
        return (2.0 / (blocks[i - 1, 4] + blocks[i, 3])) + blocks[i - 1, 2] + blocks[i, 0]

    def gain(i):
        if i == 0:
            return -blocks[0, 5]
        return blocks[i - 1, 6] - blocks[i, 5] if i < count else blocks[i - 1, 6]

    flows_of(count, pivot, lambda i: blocks[i - 1, 1], lambda i: blocks[i, 1], gain, slots)


def y_merge(low, high):
    inv = 1.0 / (low[2] + high[0])
    e = (low[4] - high[3]) * inv
    a = low[1] * inv
    b = high[1] * inv
    joined = [
        low[0] - low[1] * a,
        low[1] * b,
        high[2] - high[1] * b,
        low[3] - low[1] * e,
        high[4] + high[1] * e,
    ]
    return joined, (e, a, b)


def arrange(own, far, near, shared, place, blocks):
    on_low = lax.rem(lax.axis_index("gx"), 2) == 0
    blocks[place] = own[...]
    blocks[place ^ 3] = near[...]
    blocks[place ^ 2] = jnp.where(on_low, shared[...], far[...])
    blocks[place ^ 1] = jnp.where(on_low, far[...], shared[...])


def y_flows(blocks, slots):
    count = blocks.shape[0]

    def pivot(i):
        if i == 0:
            return blocks[0, 0]
        return blocks[i - 1, 2] + blocks[i, 0] if i < count else blocks[i - 1, 2]

    def gain(i):
        if i == 0:
            return -blocks[0, 3]
        return blocks[i - 1, 4] - blocks[i, 3] if i < count else blocks[i - 1, 4]

    flows_of(count, pivot, lambda i: blocks[i - 1, 1], lambda i: blocks[i, 1], gain, slots)


def load_kernel(st_hbm, kx_hbm, ky_hbm, st, kx, st_t, ky_t, mine, first, second, ky, sems):
    inside = pl.ds(0, BX)
    moves = [
        pltpu.make_async_copy(src, dst, sems.at[n])
        for n, (src, dst) in enumerate(
            ((ky_hbm, ky), (st_hbm, st.at[:, inside, :]), (kx_hbm, kx.at[:, inside, :]))
        )
    ]
    for move in moves:
        move.start()
    moves[0].wait()
    for g in range(GROUPS):
        pair = jnp.concatenate([ky[2 * g], ky[2 * g + 1]], axis=0)
        ky_t[pl.ds(g, BY, stride=GROUPS), :] = pair.T
    moves[1].wait()
    for g in range(GROUPS):
        pair = jnp.concatenate([st[2 * g, inside, :], st[2 * g + 1, inside, :]], axis=0)
        st_t[pl.ds(g, BY, stride=GROUPS), :] = pair.T
    for n, ref in enumerate((st_t, ky_t)):
        mine[n] = y_row(ref, 0)
        mine[2 + n] = y_row(ref, BY - 1)
    even = lax.rem(lax.axis_index("gy"), 2) == 0
    low, high = mine[0:2], mine[2:4]
    first[...] = jnp.where(even, high, low)
    second[...] = jnp.where(even, low, high)
    moves[2].wait()


def sweep(count, row, f, u, ratios, put_first, put_last):
    ahead = jnp.ones_like(row(0))
    back = jnp.ones_like(ahead)
    low, high = row(0), row(count - 1)
    for i in range(count - 1):
        nxt = row(i + 1)
        r = 0.5 * (low + nxt)
        low = nxt
        inv = (1.0 / (r + ahead))
        ratio = r * inv
        ahead = 1.0 + ratio * ahead
        u[i] = inv
        f[i] = ratio
        j = count - 1 - i
        prev = row(j - 1)
        r = 0.5 * (high + prev)
        high = prev
        ratio = r * (1.0 / (r + back))
        back = 1.0 + ratio * back
        ratios[j] = ratio
    start = (1.0 / (back))
    end = (1.0 / (ahead))
    lead, trail = start, end
    put_first(0, start)
    put_last(count - 1, end)
    u[count - 1] = end
    f[count - 1] = jnp.zeros_like(end)
    for i in range(1, count):
        start = start * ratios[i]
        put_first(i, start)
        j = count - 1 - i
        end = end * f[j]
        put_last(j, end)
    return lead, end, trail


def x_matrix_kernel(st_t, kx, ky_t, fx, ux, wf, wl, part, edges, base_t, source, ratios):
    here, k_here = y_row(st_t, 0), y_row(ky_t, 0)
    value = here
    for j in range(BY):
        if j < BY - 1:
            after, k_after = y_row(st_t, j + 1), y_row(ky_t, j + 1)
            flux = 0.5 * (k_here + k_after) * (after - here)
            value = value + flux
        base_t[pl.ds(j * GROUPS, GROUPS), :] = value
        here, k_here, value = after, k_after, after - flux
    for g in range(GROUPS):
        place_group(source, g, base_t[pl.ds(g, BY, stride=GROUPS), :].T)
    sums = [[jnp.zeros((NZ, BY), F32) for _ in range(2)] for _ in range(2)]

    def put(ref, total):
        def store(i, value):
            place_rows(ref, i, value)
            total[i % 2] = total[i % 2] + value * x_row(source, i)

        return store

    values = sweep(BX, lambda i: x_row(kx, i), fx, ux, ratios, put(wf, sums[0]), put(wl, sums[1]))
    values += (x_row(kx, 0), x_row(kx, BX - 1), sums[0][0] + sums[0][1], sums[1][0] + sums[1][1])
    for n, value in enumerate(values):
        part[n] = value
    for n, ref in enumerate((wf, wl)):
        for g in range(GROUPS):
            turned = group(ref, g).T
            edges[2 * n, pl.ds(g, 1), :] = turned[0:1, :]
            edges[2 * n + 1, pl.ds(g, 1), :] = turned[127:128, :]


def y_matrix_kernel(ky_t, after, f, u, yf, yl, my, ratios):
    def put(ref):
        def store(j, value):
            ref[j] = value

        return store

    me = lax.axis_index("gy")
    last = lax.axis_size("gy") - 1
    lead, across, trail = sweep(BY, lambda j: y_row(ky_t, j), f, u, ratios, put(yf), put(yl))
    my[0] = lead
    my[1] = across
    my[2] = trail + jnp.where(me == last, (2.0 / (y_row(ky_t, BY - 1))), 0.0)


def x_ends_kernel(came2, came1, mine, part, edges, send, flux, rows):
    me = lax.axis_index("gy")
    even = lax.rem(me, 2) == 0
    below = jnp.where(me == 0, 0.0, jnp.where(even, came2[...], came1[...]))
    above = jnp.where(me == lax.axis_size("gy") - 1, 0.0, jnp.where(even, came1[...], came2[...]))
    enter = 0.5 * (below[1] + mine[1]) * (mine[0] - below[0])
    leave = 0.5 * (above[1] + mine[3]) * (above[0] - mine[2])
    flux[0] = enter
    flux[1] = leave
    flux[2] = (2.0 / (below[1] + mine[1]))
    lane = lax.broadcasted_iota(jnp.int32, (GROUPS, 128), 1)
    send[0:5] = part[0:5]
    for n in range(2):
        low = -edges[2 * n] * enter
        high = edges[2 * n + 1] * leave
        for h in range(2):
            inside = lane // BX == h
            at_low = jnp.sum(jnp.where(inside, low, 0.0), axis=1, keepdims=True)
            at_high = jnp.sum(jnp.where(inside, high, 0.0), axis=1, keepdims=True)
            value = jnp.where(lane == 0, at_low, jnp.where(lane == 127, at_high, 0.0))
            rows[n, pl.ds(h, GROUPS, stride=2), :] = value
        send[5 + n] = part[5 + n] + rows[n]


def x_local_kernel(base_t, flux, st, fx, ux, d, s, work, work_t):
    work_t[...] = base_t[...]
    work_t[pl.ds(0, GROUPS), :] = y_row(base_t, 0) - flux[0]
    work_t[pl.ds((BY - 1) * GROUPS, GROUPS), :] = y_row(base_t, BY - 1) + flux[1]
    for g in range(GROUPS):
        place_group(s, g, work_t[pl.ds(g, BY, stride=GROUPS), :].T)
    total = x_row(s, 0)
    work[0] = total
    for i in range(1, BX):
        total = x_row(s, i) + fx[i - 1] * total
        work[i] = total
    x = jnp.zeros_like(total)
    for i in range(BX - 1, -1, -1):
        x = ux[i] * work[i] + fx[i] * x
        place_rows(d, i, x - x_row(st, i))


def x_merge_kernel(own, other, after, send, coefs):
    core = lax.rem(lax.axis_index("gx"), 2)
    mine, theirs = [own[n] for n in range(7)], [other[n] for n in range(7)]
    low = [jnp.where(core == 0, a, b) for a, b in zip(mine, theirs)]
    high = [jnp.where(core == 0, b, a) for a, b in zip(mine, theirs)]
    joined, flow = merge(low, high)
    for n in range(7):
        send[n] = joined[n]
    for n in range(3):
        coefs[n] = flow[n]


def relay_kernel(value, after, out):
    out[...] = value[...]


def y_ends_kernel(
    own, far, near, shared, coefs, d, wf, wl, yf, yl, my, flux, v_t, send, blocks, slots, flows
):
    me = lax.axis_index("gx")
    place = lax.div(me, 2)
    on_low = lax.rem(me, 2) == 0
    arrange(own, far, near, shared, place, blocks)
    x_flows(blocks, slots)
    enter, leave = slots[place], slots[place + 1]
    middle = coefs[0] + coefs[1] * enter + coefs[2] * leave
    flows[0] = jnp.where(on_low, enter, middle)
    flows[1] = jnp.where(on_low, middle, leave)
    for g in range(GROUPS):
        parts = []
        for z in range(2 * g, 2 * g + 2):
            rows = pl.ds(z * PITCH, BX)
            parts.append(
                d[rows, :]
                + wf[rows, :] * flows[0, pl.ds(z, 1), :]
                - wl[rows, :] * flows[1, pl.ds(z, 1), :]
            )
        v_t[pl.ds(g, BY, stride=GROUPS), :] = jnp.concatenate(parts, axis=0).T
    firsts = [jnp.zeros((GROUPS, 128), F32) for _ in range(4)]
    lasts = [jnp.zeros((GROUPS, 128), F32) for _ in range(4)]
    for j in range(BY):
        row = y_row(v_t, j)
        firsts[j % 4] = firsts[j % 4] + yf[j] * row
        lasts[j % 4] = lasts[j % 4] + yl[j] * row
    first = (firsts[0] + firsts[1]) + (firsts[2] + firsts[3])
    last = (lasts[0] + lasts[1]) + (lasts[2] + lasts[3])
    send[0] = my[0] + flux[2]
    send[1:3] = my[1:3]
    send[3] = first
    send[4] = last


def y_pack_kernel(own, other, after, both):
    on_low = lax.rem(lax.axis_index("gx"), 2) == 0
    both[:, 0:GROUPS] = jnp.where(on_low, own[...], other[...])
    both[:, GROUPS : 2 * GROUPS] = jnp.where(on_low, other[...], own[...])


def y_local_kernel(v_t, f, u, g_t):
    total = y_row(v_t, 0)
    g_t[0] = total
    for j in range(1, BY):
        total = y_row(v_t, j) + f[j - 1] * total
        g_t[j] = total
    x = jnp.zeros_like(total)
    for j in range(BY - 1, -1, -1):
        x = u[j] * g_t[j] + f[j] * x
        g_t[j] = x


def own_rows():
    start = lax.rem(lax.axis_index("gx"), 2) * GROUPS
    return pl.ds(pl.multiple_of(start, GROUPS), GROUPS)


def other_rows():
    start = (1 - lax.rem(lax.axis_index("gx"), 2)) * GROUPS
    return pl.ds(pl.multiple_of(start, GROUPS), GROUPS)


def pick_kernel(value, out):
    out[...] = value[:, other_rows(), :]


def y_merge_kernel(own, far, near, shared, quad, mine, coefs, blocks):
    arrange(own, far, near, shared, lax.rem(lax.axis_index("gy"), SIDE), blocks)
    joined = [blocks[0, n] for n in range(5)]
    for c in range(1, SIDE):
        joined, flow = y_merge(joined, [blocks[c, n] for n in range(5)])
        for n in range(3):
            coefs[c - 1, n] = flow[n]
    for n in range(5):
        quad[n] = joined[n]
    mine[...] = quad[:, own_rows(), :]


def y_solve_kernel(
    mine, far, near, shared, coefs, g_t, yf, yl, st, out_hbm, blocks, slots, inner, work, out, sem
):
    me = lax.axis_index("gy")
    place, depth = lax.div(me, SIDE), lax.rem(me, SIDE)
    rows = own_rows()
    arrange(mine, far.at[:, rows, :], near, shared, place, blocks)
    y_flows(blocks, slots)
    enter, flow = slots[place], slots[place + 1]
    inner[0] = enter
    inner[SIDE] = flow
    for c in range(SIDE - 1, 0, -1):
        e, a, b = [coefs[c - 1, n, rows, :] for n in range(3)]
        flow = e + a * enter + b * flow
        inner[c] = flow
    enter, leave = inner[depth], inner[depth + 1]
    for j in range(BY):
        work[pl.ds(j * GROUPS, GROUPS), :] = 2.0 * (g_t[j] + yf[j] * enter - yl[j] * leave)
    for g in range(GROUPS):
        rows = pl.ds(g * 128, 128)
        out[rows, :] = group(st, g) + work[pl.ds(g, BY, stride=GROUPS), :].T
        pltpu.make_async_copy(out.at[rows], out_hbm.at[rows], sem).start()
    pltpu.make_async_copy(out, out_hbm, sem).wait()


def call(kernel, outs, args, scratch=(), cost=100_000):
    vm = pl.BlockSpec(memory_space=pltpu.VMEM)
    hbm = pl.BlockSpec(memory_space=pltpu.HBM)
    return pl.pallas_call(
        kernel,
        out_shape=[
            jax.ShapeDtypeStruct(shape, F32) if far else pltpu.VMEM(shape, F32)
            for shape, far in outs
        ],
        in_specs=[hbm if far else vm for _, far in args],
        out_specs=[hbm if far else vm for _, far in outs],
        scratch_shapes=list(scratch),
        compiler_params=pltpu.CompilerParams(vmem_limit_bytes=LIMIT),
        cost_estimate=pl.CostEstimate(flops=cost, bytes_accessed=cost, transcendentals=0),
    )(*[value for value, _ in args])


def near(*values):
    return [(value, False) for value in values]


def on_device(state, kappa_x, kappa_y):
    flat = [
        pltpu.with_memory_space_constraint(a, pltpu.HBM) for a in (state, kappa_x, kappa_y)
    ]
    plane = (ROWS, BY)
    pitched = (NZ * PITCH, BY)
    planes = (NZ, PITCH, BY)
    xs = (BX, NZ, BY)
    ys = (BY, GROUPS, 128)
    x_block = (7, NZ, BY)
    edge = (2, GROUPS, 128)
    nx, ny = lax.axis_size("gx"), lax.axis_size("gy")
    wide = (5, 2 * GROUPS, 128)
    st, kx, st_t, ky_t, mine, first, second = call(
        load_kernel,
        near(planes, planes, plane, plane, (4, GROUPS, 128), edge, edge),
        [(a, True) for a in flat],
        [pltpu.VMEM((NZ, BX, BY), F32), pltpu.SemaphoreType.DMA((3,))],
    )
    st, kx = st.reshape(pitched), kx.reshape(pitched)
    pairs = [
        (i * ny + j, i * ny + j + 2 * (j % 2) - 1 if 0 < j < ny - 1 else (i ^ 1) * ny + j)
        for i in range(nx)
        for j in range(ny)
    ]
    came2 = lax.ppermute(second, ("gx", "gy"), pairs)
    came1 = lax.ppermute(first, "gy", [(i, i ^ 1) for i in range(ny)])
    fx, ux, wf, wl, part, edges, base_t = call(
        x_matrix_kernel,
        near(xs, xs, pitched, pitched, x_block, (4, GROUPS, 128), plane),
        near(st_t, kx, ky_t),
        [pltpu.VMEM(pitched, F32), pltpu.VMEM(xs, F32)],
        cost=5_000_000,
    )
    ends, flux = call(
        x_ends_kernel,
        near(x_block, (3, GROUPS, 128)),
        near(came2, came1, mine, part, edges),
        [pltpu.VMEM((2, NZ, BY), F32)],
    )
    other = lax.ppermute(ends, "gx", [(i, i ^ 1) for i in range(nx)])
    (d,) = call(
        x_local_kernel,
        near(pitched),
        near(base_t, flux, st, fx, ux),
        [pltpu.VMEM(pitched, F32), pltpu.VMEM(xs, F32), pltpu.VMEM(plane, F32)],
        cost=3_000_000,
    )
    chip, coefs = call(x_merge_kernel, near(x_block, (3, NZ, BY)), near(ends, other, d))
    def swap(axes, bits, value):
        return lax.ppermute(
            value,
            ("gx", "gy"),
            [
                (i * ny + j, (i ^ (2 * bits[i % 2])) * ny + j if axes == "x" else i * ny + (j ^ bits[i % 2]))
                for i in range(nx)
                for j in range(ny)
            ],
        )

    def share(value):
        return lax.ppermute(value, "gx", [(i, i ^ 1) for i in range(nx)])

    far = swap("x", (1, 2), chip)
    near_x = swap("x", (3, 3), chip)
    f, u, yf, yl, my = call(
        y_matrix_kernel,
        near(ys, ys, ys, ys, (3, GROUPS, 128)),
        near(ky_t, coefs),
        [pltpu.VMEM(ys, F32)],
        cost=5_000_000,
    )
    (relayed,) = call(relay_kernel, near(x_block), near(far, my))
    v_t, own = call(
        y_ends_kernel,
        near(plane, (5, GROUPS, 128)),
        near(chip, far, near_x, share(relayed), coefs, d, wf, wl, yf, yl, my, flux),
        [
            pltpu.VMEM((SIDE,) + x_block, F32),
            pltpu.VMEM((SIDE + 1, NZ, BY), F32),
            pltpu.VMEM((2, NZ, BY), F32),
        ],
    )
    (g_t,) = call(y_local_kernel, near(ys), near(v_t, f, u), cost=3_000_000)
    (both,) = call(y_pack_kernel, near(wide), near(own, share(own), g_t))
    far = swap("y", (1, 2), both)
    near_y = swap("y", (3, 3), both)
    quad, mine, coefs = call(
        y_merge_kernel,
        near(wide, (5, GROUPS, 128), (SIDE - 1, 3, 2 * GROUPS, 128)),
        near(both, far, near_y, share(far)),
        [pltpu.VMEM((SIDE,) + wide, F32)],
    )
    far = swap("y", (4, 8), quad)
    near_y = swap("y", (12, 12), mine)
    (picked,) = call(pick_kernel, near((5, GROUPS, 128)), near(far))
    (out,) = call(
        y_solve_kernel,
        [(plane, True)],
        near(mine, far, near_y, share(picked), coefs, g_t, yf, yl, st),
        [
            pltpu.VMEM((SIDE, 5, GROUPS, 128), F32),
            pltpu.VMEM((SIDE + 1, GROUPS, 128), F32),
            pltpu.VMEM((SIDE + 1, GROUPS, 128), F32),
            pltpu.VMEM(plane, F32),
            pltpu.VMEM(plane, F32),
            pltpu.SemaphoreType.DMA,
        ],
    )
    return out.reshape(state.shape)


def solution(mesh):
    spec = P(None, "gx", "gy")
    return jax.shard_map(
        on_device, mesh=mesh, in_specs=(spec, spec, spec), out_specs=spec, check_vma=False
    )
```
